32 devices in a mesh: fsdp: 8 (over y, x, core), seq: 4 (over z).
Axes of the slice: x: 2, y: 2, z: 4, core: 2. Of those that a mesh axis runs over, the one named last changes fastest.
Arguments:
- pixels: bfloat16 [24, 1024, 768], P('fsdp', 'seq'), may hold values from -6 to 6
- restore: int32 [24, 1024], P('fsdp'), may hold values from 0 to 1023, each once within a row
- enc_w: float32 [768, 10496], P('fsdp'), may hold values from -0.21875 to 0.21875
- enc_m: float32 [768, 10496], P('fsdp'), may hold values from -0.00318944 to 0.00318944
- enc_v: float32 [768, 10496], P('fsdp'), may hold values from 2.1192763e-07 to 8.477105e-07
- dec_w: float32 [512, 6144], P('fsdp'), may hold values from -0.25 to 0.25
- dec_m: float32 [512, 6144], P('fsdp'), may hold values from -0.00318944 to 0.00318944
- dec_v: float32 [512, 6144], P('fsdp'), may hold values from 2.1192763e-07 to 8.477105e-07
- head_w: float32 [512, 768], replicated, may hold values from -0.25 to 0.25
- head_m: float32 [512, 768], replicated, may hold values from -0.000115088995 to 0.000115088995
- head_v: float32 [512, 768], replicated, may hold values from 2.7594743e-10 to 1.1037897e-09
- gain_w: float32 [3840], replicated, may hold values from 0.5 to 1.5
- gain_m: float32 [3840], replicated, may hold values from -0.00318944 to 0.00318944
- gain_v: float32 [3840], replicated, may hold values from 2.1192763e-07 to 8.477105e-07
- bias_w: float32 [17408], replicated, may hold values from -1.5 to 1.5
- bias_m: float32 [17408], replicated, may hold values from -0.00318944 to 0.00318944
- bias_v: float32 [17408], replicated, may hold values from 2.1192763e-07 to 8.477105e-07
Outputs:
- loss: float32 [], replicated
- enc_m_new: float32 [768, 10496], P('fsdp')
- enc_v_new: float32 [768, 10496], P('fsdp')
- enc_w_new: float32 [768, 10496], P('fsdp')
- dec_m_new: float32 [512, 6144], P('fsdp')
- dec_v_new: float32 [512, 6144], P('fsdp')
- dec_w_new: float32 [512, 6144], P('fsdp')
- head_m_new: float32 [512, 768], replicated
- head_v_new: float32 [512, 768], replicated
- head_w_new: float32 [512, 768], replicated
- gain_m_new: float32 [3840], replicated
- gain_v_new: float32 [3840], replicated
- gain_w_new: float32 [3840], replicated
- bias_m_new: float32 [17408], replicated
- bias_v_new: float32 [17408], replicated
- bias_w_new: float32 [17408], replicated
The draws below stay inside these ranges and needn't reach their ends.
Inputs may be any that keep to these rules, and one draw needn't show every extreme that they name: `restore`: each image's row is a permutation of 0 to 1023; a patch is visible when its entry is under 256.
All inputs are finite; a program needn't handle non-finite values.
Results may differ from the reference program's by a relative error of at most 0.00075.
The reference program's roundings to bfloat16 on the way count: a program that leaves them out, or rounds other values in their place, can miss the bound.
Values may be sent and summed in bfloat16 or wider, within the bound.
A program may use at most 256 MiB of HBM per device.

```python
import math
from functools import partial
import jax
import jax.numpy as jnp
from jax import lax

D_E = 768
H_E = 12
FF_E = 3072
D_D = 512
H_D = 16
FF_D = 2048
PIX = 768
PATCHES = 1024
KEEP = 256
STEP = 5
IMAGES = 24
ENC_PAD = 260
DEC_PAD = 1028
MASKED = 18432
ENC_COLS = 10496
DEC_COLS = 6144
NGAIN = 3840
NBIAS = 17408


def level_of(own_key, extent, shards, least, high):
    def one(axis_at, blocks):
        steps = jax.random.uniform(jax.random.fold_in(jax.random.fold_in(own_key, 6), axis_at), (blocks,), jnp.float32, least / len(shards), high / len(shards))
        return jnp.repeat(jnp.exp(steps), extent[axis_at] // blocks).reshape((-1,) + (1,) * (len(extent) - axis_at - 1))

    loudness = one(*shards[0])
    for cut in shards[1:]:
        loudness = loudness * one(*cut)
    return loudness


def bell_draw(key, dims, scale, bound, cuts=(), kind=jnp.bfloat16):
    loudness = level_of(key, dims, cuts, -0.22, 0.18) if cuts else 1.0
    array = jax.random.normal(key, dims, jnp.float32) * scale * loudness
    return jnp.minimum(jnp.maximum(array, -bound), bound).astype(kind)


def setup_inputs(seed: int = 0) -> dict:
    key_of = jax.random.split(jax.random.key(seed), 18)
    pixels = bell_draw(key_of[0], (IMAGES, PATCHES, PIX), 1.0, 6.0, ((0, 8), (1, 4)))
    restore = jax.vmap(lambda own: jax.random.permutation(own, PATCHES))(jax.random.split(key_of[1], IMAGES)).reshape((IMAGES, PATCHES)).astype(jnp.int32)
    enc_w = bell_draw(key_of[2], (D_E, ENC_COLS), D_E ** -0.5, 0.21875, ((0, 8),), jnp.float32)
    enc_m = bell_draw(key_of[3], (D_E, ENC_COLS), (3 * (PIX * MASKED) ** -0.5), 0.00318944, ((0, 8),), jnp.float32)
    enc_v = jnp.clip(jnp.exp(math.log(8.477105097881577e-07) - 1.3862944 * jax.random.uniform(key_of[4], (D_E, ENC_COLS), jnp.float32) ** level_of(key_of[4], (D_E, ENC_COLS), ((0, 8),), -0.2, 0.2)), 2.119276274470394e-07, 8.477105097881577e-07)
    dec_w = bell_draw(key_of[5], (D_D, DEC_COLS), D_D ** -0.5, 0.25, ((0, 8),), jnp.float32)
    dec_m = bell_draw(key_of[6], (D_D, DEC_COLS), (3 * (PIX * MASKED) ** -0.5), 0.00318944, ((0, 8),), jnp.float32)
    dec_v = jnp.clip(jnp.exp(math.log(8.477105097881577e-07) - 1.3862944 * jax.random.uniform(key_of[7], (D_D, DEC_COLS), jnp.float32) ** level_of(key_of[7], (D_D, DEC_COLS), ((0, 8),), -0.2, 0.2)), 2.119276274470394e-07, 8.477105097881577e-07)
    head_w = bell_draw(key_of[8], (D_D, PIX), D_D ** -0.5, 0.25, (), jnp.float32)
    head_m = bell_draw(key_of[9], (D_D, PIX), (3 * PIX ** -1 * MASKED ** -0.5), 0.000115088995, (), jnp.float32)
    head_v = jnp.clip(jnp.exp(jax.random.uniform(key_of[10], (D_D, PIX), jnp.float32, math.log(2.759474315716659e-10), math.log(1.1037897262866636e-09))), 2.759474315716659e-10, 1.1037897262866636e-09)
    gain_w = jnp.clip(1.0 + 0.1 * jax.random.normal(key_of[11], (NGAIN,), jnp.float32), 0.5, 1.5)
    gain_m = bell_draw(key_of[12], (NGAIN,), (3 * (PIX * MASKED) ** -0.5), 0.00318944, (), jnp.float32)
    gain_v = jnp.clip(jnp.exp(jax.random.uniform(key_of[13], (NGAIN,), jnp.float32, math.log(2.119276274470394e-07), math.log(8.477105097881577e-07))), 2.119276274470394e-07, 8.477105097881577e-07)
    bias_w = bell_draw(key_of[14], (NBIAS,), 0.3, 1.5, (), jnp.float32)
    bias_m = bell_draw(key_of[15], (NBIAS,), (3 * (PIX * MASKED) ** -0.5), 0.00318944, (), jnp.float32)
    bias_v = jnp.clip(jnp.exp(jax.random.uniform(key_of[16], (NBIAS,), jnp.float32, math.log(2.119276274470394e-07), math.log(8.477105097881577e-07))), 2.119276274470394e-07, 8.477105097881577e-07)
    return dict(pixels=pixels, restore=restore, enc_w=enc_w, enc_m=enc_m, enc_v=enc_v, dec_w=dec_w, dec_m=dec_m, dec_v=dec_v, head_w=head_w, head_m=head_m, head_v=head_v, gain_w=gain_w, gain_m=gain_m, gain_v=gain_v, bias_w=bias_w, bias_m=bias_m, bias_v=bias_v)


HIGH = lax.Precision.HIGHEST
NORM_EPS = 1e-06
PIXEL_EPS = 1e-06
BETA_ONE = 0.5
BETA_TWO = 0.75
MATRIX_RATE = 0.03
SMALL_RATE = 0.1
MATRIX_DECAY = 0.05
ADAM_EPS = 1e-08

@jax.custom_vjp
def low(v):
    return lax.optimization_barrier(v.astype(jnp.bfloat16)).astype(jnp.float32)

@jax.custom_vjp
def low_back(v):
    return v

def low_keep(v):
    return (low(v), None)

def low_pass(kept, grad):
    return (grad,)

def back_keep(v):
    return (v, None)

def back_low(kept, grad):
    return (low(grad),)
low.defvjp(low_keep, low_pass)
low_back.defvjp(back_keep, back_low)

def bias_widths():
    return [D_E, D_E, D_E, D_E, D_E, D_E, D_E, FF_E, D_E, D_E, D_D, D_D, D_D, D_D, D_D, D_D, D_D, FF_D, D_D, D_D, PIX]

def split_vector(vector, widths):
    pieces = []
    offset = 0
    for span_width in widths:
        pieces.append(vector[offset:offset + span_width])
        offset += span_width
    return pieces

def matmul(left, right):
    return jnp.dot(left, right, precision=HIGH, preferred_element_type=jnp.float32)

def layer_norm(inputs, gain_vec, shift_vec):
    centre = inputs - lax.optimization_barrier(jnp.mean(inputs, axis=-1, keepdims=True))
    scaled = centre * lax.rsqrt(lax.optimization_barrier(jnp.mean(centre * centre, axis=-1, keepdims=True)) + NORM_EPS)
    return scaled * gain_vec + shift_vec

def positions(index_arr, width_dim):
    halves = width_dim // 2
    frequency = 10000.0 ** (-jnp.arange(halves, dtype=jnp.float32) / halves)
    angles = (index_arr.astype(jnp.float32) + 1.0)[..., None] * frequency
    return jnp.concatenate([jnp.sin(angles), jnp.cos(angles)], axis=-1)

def head_attend(live_count, scale_val, parts):
    query_h, key_h, value_h = parts
    scores = low_back(matmul(query_h, key_h.T) * scale_val)
    valid_keys = jnp.arange(key_h.shape[0]) < live_count
    scores = jnp.where(valid_keys[None, :], scores, -1e+30)
    prob_rows = jax.nn.softmax(scores, axis=-1)
    return matmul(low(prob_rows), value_h)

def attention(queries, key_rows, value_rows, head_count, live_count):
    seq_len, width_dim = queries.shape
    head_dim = width_dim // head_count

    def split_heads(tensor):
        return tensor.reshape(seq_len, head_count, head_dim).transpose(1, 0, 2)
    head_fn = jax.checkpoint(partial(head_attend, live_count, head_dim ** (-0.5)))
    out_heads = lax.map(head_fn, (split_heads(queries), split_heads(key_rows), split_heads(value_rows)))
    return out_heads.transpose(1, 0, 2).reshape(seq_len, width_dim)

def block(inputs, mats, gain_one, gain_two, vecs, head_count, live_count):
    w_qkv, w_out, w_up, w_down = mats
    shift_one, bias_q, bias_v, bias_out, shift_two, bias_up, bias_down = vecs
    width_dim = inputs.shape[1]
    normed = layer_norm(inputs, gain_one, shift_one)
    mixed_qkv = matmul(low(normed), w_qkv)
    queries = low(low_back(mixed_qkv[:, :width_dim] + bias_q))
    key_rows = low(low_back(mixed_qkv[:, width_dim:2 * width_dim]))
    value_rows = low(low_back(mixed_qkv[:, 2 * width_dim:] + bias_v))
    attended = low(low_back(attention(queries, key_rows, value_rows, head_count, live_count)))
    middle = inputs + low_back(matmul(attended, w_out)) + bias_out
    hidden = low_back(matmul(low(layer_norm(middle, gain_two, shift_two)), w_up) + bias_up)
    active = low(jax.nn.gelu(hidden, approximate=False))
    return middle + low_back(matmul(active, w_down.T)) + bias_down

def image_loss(params, pixel_rows, restore_row):
    enc_w, dec_w, head_w, gain_w, bias_w = params
    enc_w, dec_w, head_w = (low(enc_w), low(dec_w), low(head_w))
    pieces = split_vector(bias_w, bias_widths())
    gain_parts = split_vector(gain_w, [D_E, D_E, D_E, D_D, D_D, D_D])
    rank_ids = jnp.arange(KEEP, dtype=jnp.int32)
    patch_ids = jnp.arange(PATCHES, dtype=jnp.int32)
    keep_ids = lax.optimization_barrier(jnp.sum(jnp.where(restore_row[None, :] == rank_ids[:, None], patch_ids[None, :], 0), axis=1)).astype(jnp.int32)
    kept_pixels = jnp.take(pixel_rows, keep_ids, axis=0)
    embedded = low_back(matmul(kept_pixels, enc_w[:, :D_E])) + pieces[0] + positions(keep_ids, D_E)
    start_rows = jnp.concatenate([pieces[1][None, :], embedded, jnp.zeros((ENC_PAD - KEEP - 1, D_E), jnp.float32)], axis=0)
    enc_mats = (enc_w[:, D_E:4 * D_E], enc_w[:, 4 * D_E:5 * D_E], enc_w[:, 5 * D_E:5 * D_E + FF_E], enc_w[:, 5 * D_E + FF_E:5 * D_E + 2 * FF_E])
    encoded = block(start_rows, enc_mats, gain_parts[0], gain_parts[1], pieces[2:9], H_E, KEEP + 1)
    final_rows = layer_norm(encoded, gain_parts[2], pieces[9])
    shrunk = low(low_back(matmul(low(final_rows), enc_w[:, 5 * D_E + 2 * FF_E:]) + pieces[10]))
    is_kept = restore_row < KEEP
    source = jnp.where(is_kept, restore_row + 1, 0)
    gathered = jnp.take(shrunk, source, axis=0)
    patch_rows = jnp.where(is_kept[:, None], gathered, pieces[11][None, :]) + positions(patch_ids, D_D)
    dec_rows = jnp.concatenate([shrunk[:1], patch_rows, jnp.zeros((DEC_PAD - PATCHES - 1, D_D), jnp.float32)], axis=0)
    dec_mats = (dec_w[:, :3 * D_D], dec_w[:, 3 * D_D:4 * D_D], dec_w[:, 4 * D_D:4 * D_D + FF_D], dec_w[:, 4 * D_D + FF_D:])
    decoded = block(dec_rows, dec_mats, gain_parts[3], gain_parts[4], pieces[12:19], H_D, PATCHES + 1)
    final_dec = layer_norm(decoded, gain_parts[5], pieces[19])
    predicted = low_back(matmul(low(final_dec), head_w)) + pieces[20]
    centre = pixel_rows - lax.optimization_barrier(jnp.mean(pixel_rows, axis=-1, keepdims=True))
    targets = centre * lax.rsqrt(lax.optimization_barrier(jnp.sum(centre * centre, axis=-1, keepdims=True)) / (PIX - 1) + PIXEL_EPS)
    errors = lax.optimization_barrier(jnp.mean((predicted[1:PATCHES + 1] - targets) ** 2, axis=-1))
    return jnp.sum(jnp.where(is_kept, 0.0, errors)) / MASKED

def adamw(weight, moment_one, moment_two, gradient, step_rate, decay_rate):
    moment_one = BETA_ONE * moment_one + (1 - BETA_ONE) * gradient
    moment_two = BETA_TWO * moment_two + (1 - BETA_TWO) * gradient * gradient
    fixed_one = moment_one / (1 - BETA_ONE ** STEP)
    fixed_two = moment_two / (1 - BETA_TWO ** STEP)
    weight = weight - step_rate * (fixed_one / (jnp.sqrt(fixed_two) + ADAM_EPS) + decay_rate * weight)
    return (moment_one, moment_two, weight)

def reference(pixels, restore, enc_w, enc_m, enc_v, dec_w, dec_m, dec_v, head_w, head_m, head_v, gain_w, gain_m, gain_v, bias_w, bias_m, bias_v):
    params = (enc_w, dec_w, head_w, gain_w, bias_w)

    def add_image(running, image_item):
        pixel_rows, restore_row = image_item

        def one_loss(weights):
            return image_loss(weights, pixel_rows.astype(jnp.float32), restore_row)
        loss_sum, pull_back = jax.vjp(one_loss, params)
        grads = pull_back(jnp.ones_like(loss_sum))[0]
        return ((running[0] + loss_sum, jax.tree.map(jnp.add, running[1], grads)), None)
    start_state = (jnp.zeros((), jnp.float32), jax.tree.map(jnp.zeros_like, params))
    (loss_total, grads), _ = lax.scan(add_image, start_state, (pixels, restore))
    enc_new = adamw(enc_w, enc_m, enc_v, grads[0], MATRIX_RATE, MATRIX_DECAY)
    dec_new = adamw(dec_w, dec_m, dec_v, grads[1], MATRIX_RATE, MATRIX_DECAY)
    head_new = adamw(head_w, head_m, head_v, grads[2], MATRIX_RATE, MATRIX_DECAY)
    gain_new = adamw(gain_w, gain_m, gain_v, grads[3], SMALL_RATE, 0.0)
    bias_new = adamw(bias_w, bias_m, bias_v, grads[4], SMALL_RATE, 0.0)
    return (loss_total, enc_new[0], enc_new[1], enc_new[2], dec_new[0], dec_new[1], dec_new[2], head_new[0], head_new[1], head_new[2], gain_new[0], gain_new[1], gain_new[2], bias_new[0], bias_new[1], bias_new[2])
```

```python
from functools import partial

import jax
import jax.numpy as jnp
from jax import lax
from jax.experimental import pallas as pl
from jax.experimental.pallas import tpu as pltpu
from jax.sharding import PartitionSpec as P

D_E = 768
H_E = 12
FF_E = 3072
D_D = 512
H_D = 16
FF_D = 2048
PIX = 768
PATCHES = 1024
KEEP = 256
STEP = 5

NORM_EPS = 1e-06
PIXEL_EPS = 1e-06
BETA_ONE = 0.5
BETA_TWO = 0.75
MATRIX_RATE = 0.03
SMALL_RATE = 0.1
MATRIX_DECAY = 0.05
ADAM_EPS = 1e-08

TAIL = 16
E_ROWS = KEEP + TAIL
D_ROWS = PATCHES + TAIL
LOG2E = 1.4426950408889634
MASKED_SCORE = -1e30


def bias_widths():
    return [D_E] * 7 + [FF_E] + [D_E] * 2 + [D_D] * 7 + [FF_D] + [D_D] * 2 + [PIX]


def split_vector(vector, widths):
    pieces = []
    offset = 0
    for span_width in widths:
        pieces.append(vector[offset : offset + span_width])
        offset += span_width
    return pieces


def positions(index_arr, width_dim):
    halves = width_dim // 2
    frequency = 10000.0 ** (-jnp.arange(halves, dtype=jnp.float32) / halves)
    angles = (index_arr.astype(jnp.float32) + 1.0)[..., None] * frequency
    return jnp.concatenate([jnp.sin(angles), jnp.cos(angles)], axis=-1)


def norm_forward(inputs, gain_vec, shift_vec):
    centre = inputs - jnp.mean(inputs, axis=-1, keepdims=True)
    inverse = lax.rsqrt(jnp.mean(centre * centre, axis=-1, keepdims=True) + NORM_EPS)
    scaled = centre * inverse
    return (scaled * gain_vec + shift_vec, scaled, inverse)


def norm_backward(upstream, scaled, inverse, gain_vec):
    weighted = upstream * gain_vec
    inner_part = (
        weighted
        - jnp.mean(weighted, axis=-1, keepdims=True)
        - scaled * jnp.mean(weighted * scaled, axis=-1, keepdims=True)
    )
    return (
        inverse * inner_part,
        jnp.sum(upstream * scaled, axis=(0, 1)),
        jnp.sum(upstream, axis=(0, 1)),
    )


def low(tensor):
    return tensor.astype(jnp.bfloat16)


def project(row_block, weight):
    return jnp.einsum("isd,de->ise", row_block, weight, preferred_element_type=jnp.float32)


def project_back(row_block, weight):
    return jnp.einsum("ise,de->isd", row_block, weight, preferred_element_type=jnp.float32)


def weight_grad(row_block, upstream):
    return jnp.einsum("isd,ise->de", row_block, upstream, preferred_element_type=jnp.float32)


def row_sum(tensor):
    return jnp.sum(tensor.astype(jnp.float32), axis=(0, 1))


def enc_mats_of(full_rows):
    return (
        full_rows[:, D_E : 4 * D_E],
        full_rows[:, 4 * D_E : 5 * D_E],
        full_rows[:, 5 * D_E : 5 * D_E + FF_E],
        full_rows[:, 5 * D_E + FF_E : 5 * D_E + 2 * FF_E],
    )


def dot_f32(left, right, contract):
    return lax.dot_general(
        left, right, (contract, ((), ())), preferred_element_type=jnp.float32
    )


NN = ((1,), (0,))
TN = ((0,), (0,))


def pieces_of(value):
    first = low(value).astype(jnp.float32)
    rest = value - first
    second = low(rest).astype(jnp.float32)
    return first, second, rest - second


def own_span(shape, axis, head, head_dim):
    place = lax.broadcasted_iota(jnp.int32, shape, axis)
    return (place >= head * head_dim) & (place < (head + 1) * head_dim)


def live_tail(rows, scores, other):
    place = lax.broadcasted_iota(jnp.int32, (rows, scores.shape[1]), 0)
    return jnp.where(place < 1, scores, other)


def attend_forward_kernel(heads, head_dim, q_ref, k_ref, v_ref, o_ref, lse_ref):
    main = k_ref.shape[1] - TAIL
    scale = head_dim ** (-0.5) * LOG2E
    q_t = q_ref[0].astype(jnp.float32).T * scale
    q_high = low(q_t)
    q_rest = low(q_t - q_high.astype(jnp.float32))
    k_main = k_ref[0, :main]
    k_tail = k_ref[0, main:]
    k_main = jnp.concatenate([k_main, k_main], axis=1)
    k_tail = jnp.concatenate([k_tail, k_tail], axis=1)
    v_main = low(v_ref[0, :main].astype(jnp.float32).T)
    v_tail = v_ref[0, main:]
    ones = jnp.ones((TAIL, main), jnp.bfloat16)

    def scores_of(head):
        own = own_span(q_t.shape, 0, head, head_dim)
        none = jnp.zeros_like(q_high)
        q_h = jnp.concatenate([jnp.where(own, q_high, none), jnp.where(own, q_rest, none)], axis=0)
        return dot_f32(k_main, q_h, NN), live_tail(TAIL, dot_f32(k_tail, q_h, NN), MASKED_SCORE)

    outs = []
    following = scores_of(0)
    for head in range(heads):
        span = slice(head * head_dim, (head + 1) * head_dim)
        s_main, s_tail = following
        if head + 1 < heads:
            following = scores_of(head + 1)
        top = jnp.maximum(
            jnp.max(s_main, axis=0, keepdims=True), jnp.max(s_tail, axis=0, keepdims=True)
        )
        p_main = low(jnp.exp2(s_main - top))
        p_tail = low(jnp.exp2(s_tail - top))
        o_t = dot_f32(jnp.concatenate([v_main[span], ones], axis=0), p_main, NN)
        total = o_t[head_dim : head_dim + 1] + jnp.sum(
            p_tail.astype(jnp.float32), axis=0, keepdims=True
        )
        o_t = o_t[:head_dim] + dot_f32(v_tail, p_tail, TN)[span]
        outs.append(o_t * (1.0 / total))
        lse_ref[0, 0, head : head + 1, :] = top + jnp.log2(total)
    o_ref[0] = low(jnp.concatenate(outs, axis=0).T)


def attend_backward_kernel(
    heads, head_dim, q_ref, k_ref, v_ref, lse_ref, do_ref, o_ref, dq_ref, dk_ref, dv_ref
):
    main = k_ref.shape[1] - TAIL
    rows = q_ref.shape[1]
    unit = head_dim ** (-0.5)
    q = q_ref[0]
    do = do_ref[0]
    q_t = q.astype(jnp.float32).T * (unit * LOG2E)
    q_high = low(q_t).astype(jnp.float32)
    q_rest = q_t - q_high
    do_t = do.astype(jnp.float32).T
    inner_t = do_t * o_ref[0].astype(jnp.float32).T
    place = lax.broadcasted_iota(jnp.int32, q_t.shape, 0)

    def with_row(block, offset, value):
        for at, part in enumerate(pieces_of(value)):
            block = jnp.where(place == offset + at, part, block)
        return block

    score_sides, value_sides = [], []
    for head in range(heads):
        own = own_span(q_t.shape, 0, head, head_dim)
        span = slice(head * head_dim, (head + 1) * head_dim)
        other = ((head + 1) % heads) * head_dim
        lse = lse_ref[0, 0, head : head + 1, :]
        inner = jnp.sum(inner_t[span], axis=0, keepdims=True)
        rest = with_row(jnp.where(own, q_rest, 0.0), other, -lse)
        score_sides.append(low(jnp.concatenate([jnp.where(own, q_high, 0.0), rest], axis=0)))
        last = with_row(jnp.zeros_like(do_t), 0, -inner)
        value_sides.append(low(jnp.concatenate([jnp.where(own, do_t, 0.0), last], axis=0)))
    zero = jnp.zeros_like(q)
    q_sides = [jnp.where(own_span(q.shape, 1, h, head_dim), q, zero) for h in range(heads)]
    do_sides = [jnp.where(own_span(q.shape, 1, h, head_dim), do, zero) for h in range(heads)]
    stacked = rows % 128 == 0
    if stacked:
        q_sides = jnp.concatenate(q_sides, axis=0)
        do_sides = jnp.concatenate(do_sides, axis=0)

    def sum_heads(parts, sides):
        if stacked:
            return dot_f32(jnp.concatenate(parts, axis=1), sides, NN)
        terms = [dot_f32(part, side, NN) for part, side in zip(parts, sides)]
        return sum(terms[1:], terms[0])

    k_main = k_ref[0, :main]
    k_tail = k_ref[0, main:]
    k_main_t = low(k_main.astype(jnp.float32).T)

    def with_ones(block):
        return jnp.concatenate([block, jnp.ones_like(block)], axis=1)

    def beside_own(block, head):
        own = jnp.where(own_span(block.shape, 1, head, head_dim), block, jnp.ones_like(block))
        return jnp.concatenate([block, own], axis=1)

    v_main = with_ones(v_ref[0, :main])
    v_tail = with_ones(v_ref[0, main:])
    dq_parts, p_mains, s_mains, p_tails, s_tails = [], [], [], [], []
    for head in range(heads):
        span = slice(head * head_dim, (head + 1) * head_dim)
        p = jnp.exp2(dot_f32(beside_own(k_main, head), score_sides[head], NN))
        s = low(p * dot_f32(v_main, value_sides[head], NN))
        p_mains.append(low(p))
        s_mains.append(s)
        p = jnp.exp2(dot_f32(beside_own(k_tail, head), score_sides[head], NN))
        p = live_tail(TAIL, p, 0.0)
        s_tail = low(p * dot_f32(v_tail, value_sides[head], NN))
        p_tails.append(low(p))
        s_tails.append(s_tail)
        dq_parts.append(dot_f32(k_main_t[span], s, NN) + dot_f32(k_tail, s_tail, TN)[span])
    dk_ref[0, :main] = low(sum_heads(s_mains, q_sides) * unit)
    dk_ref[0, main:] = low(sum_heads(s_tails, q_sides) * unit)
    dv_ref[0, :main] = low(sum_heads(p_mains, do_sides))
    dv_ref[0, main:] = low(sum_heads(p_tails, do_sides))
    dq_ref[0] = low(jnp.concatenate(dq_parts, axis=0).T * unit)


VMEM_LIMIT = 32 * 1024 * 1024


def attend_specs(q_rows, k_rows, heads):
    return (
        pl.BlockSpec((1, q_rows, 128), lambda i, g: (i, 0, g)),
        pl.BlockSpec((1, k_rows, 128), lambda i, g: (i, 0, g)),
        pl.BlockSpec((1, 1, heads, q_rows), lambda i, g: (i, g, 0, 0)),
    )


def attend_forward(queries, key_rows, value_rows, head_count):
    images, q_rows, width = queries.shape
    k_rows = key_rows.shape[1]
    head_dim = width // head_count
    heads = 128 // head_dim
    groups = width // 128
    q_spec, k_spec, l_spec = attend_specs(q_rows, k_rows, heads)
    return pl.pallas_call(
        partial(attend_forward_kernel, heads, head_dim),
        grid=(images, groups),
        in_specs=[q_spec, k_spec, k_spec],
        out_specs=[q_spec, l_spec],
        out_shape=[
            jax.ShapeDtypeStruct((images, q_rows, width), jnp.bfloat16),
            jax.ShapeDtypeStruct((images, groups, heads, q_rows), jnp.float32),
        ],
        compiler_params=pltpu.CompilerParams(vmem_limit_bytes=VMEM_LIMIT),
        cost_estimate=pl.CostEstimate(
            flops=16 * images * q_rows * k_rows * width,
            bytes_accessed=4 * images * (q_rows + k_rows) * width,
            transcendentals=images * head_count * q_rows * k_rows,
        ),
    )(queries, key_rows, value_rows)


def attend_backward(queries, key_rows, value_rows, logsum, upstream, attended, head_count):
    images, q_rows, width = queries.shape
    k_rows = key_rows.shape[1]
    head_dim = width // head_count
    heads = 128 // head_dim
    groups = width // 128
    q_spec, k_spec, l_spec = attend_specs(q_rows, k_rows, heads)
    return pl.pallas_call(
        partial(attend_backward_kernel, heads, head_dim),
        grid=(images, groups),
        in_specs=[q_spec, k_spec, k_spec, l_spec, q_spec, q_spec],
        out_specs=[q_spec, k_spec, k_spec],
        out_shape=[
            jax.ShapeDtypeStruct((images, q_rows, width), jnp.bfloat16),
            jax.ShapeDtypeStruct((images, k_rows, width), jnp.bfloat16),
            jax.ShapeDtypeStruct((images, k_rows, width), jnp.bfloat16),
        ],
        compiler_params=pltpu.CompilerParams(vmem_limit_bytes=VMEM_LIMIT),
        cost_estimate=pl.CostEstimate(
            flops=40 * images * q_rows * k_rows * width,
            bytes_accessed=8 * images * (q_rows + k_rows) * width,
            transcendentals=images * head_count * q_rows * k_rows,
        ),
    )(queries, key_rows, value_rows, logsum, upstream, attended)


MESH = pl.DeviceIdType.MESH


def line_sum_kernel(
    chunks, x_ref, o_ref, from_left, from_right, to_left, to_right, send_sem, recv_sem
):
    count = lax.axis_size("seq")
    place = lax.axis_index("seq")
    has_left = place > 0
    has_right = place < count - 1
    rows = x_ref.shape[0] // chunks
    barrier = pltpu.get_barrier_semaphore()

    def greet(to):
        pl.semaphore_signal(barrier, inc=1, device_id={"seq": to}, device_id_type=MESH)

    pl.when(has_left)(lambda: greet(place - 1))
    pl.when(has_right)(lambda: greet(place + 1))
    peers = jnp.where(has_left, 1, 0) + jnp.where(has_right, 1, 0)
    pl.semaphore_wait(barrier, peers)

    def copy(way, at):
        span = pl.ds(at * rows, rows)
        source, target = ((to_right, from_left), (to_left, from_right))[way]
        return pltpu.make_async_remote_copy(
            src_ref=source.at[span],
            dst_ref=target.at[span],
            send_sem=send_sem.at[way, at],
            recv_sem=recv_sem.at[way, at],
            device_id={"seq": place + 1 if way == 0 else place - 1},
            device_id_type=MESH,
        )

    def end_copy(way, at):
        span = pl.ds(at * rows, rows)
        return pltpu.make_async_remote_copy(
            src_ref=x_ref.at[span],
            dst_ref=(from_left, from_right)[way].at[span],
            send_sem=send_sem.at[way, at],
            recv_sem=recv_sem.at[way, at],
            device_id={"seq": place + 1 if way == 0 else place - 1},
            device_id_type=MESH,
        )

    for way, is_end in ((0, jnp.logical_not(has_left)), (1, jnp.logical_not(has_right))):

        @pl.when(is_end)
        def _():
            for at in range(chunks):
                if at >= 2:
                    end_copy(way, at - 2).wait_send()
                end_copy(way, at).start()
            for at in range(chunks - 2, chunks):
                end_copy(way, at).wait_send()

    for at in range(chunks):
        span = pl.ds(at * rows, rows)

        @pl.when(has_left)
        def _():
            copy(0, at).wait_recv()

            @pl.when(has_right)
            def _():
                to_right[span] = x_ref[span] + from_left[span]
                copy(0, at).start()

        @pl.when(has_right)
        def _():
            copy(1, at).wait_recv()

            @pl.when(has_left)
            def _():
                to_left[span] = x_ref[span] + from_right[span]
                copy(1, at).start()

        @pl.when(has_left & has_right)
        def _():
            o_ref[span] = (x_ref[span] + from_left[span]) + from_right[span]

        @pl.when(jnp.logical_not(has_left))
        def _():
            o_ref[span] = x_ref[span] + from_right[span]

        @pl.when(jnp.logical_not(has_right))
        def _():
            o_ref[span] = x_ref[span] + from_left[span]

    @pl.when(has_left & has_right)
    def _():
        for at in range(chunks):
            copy(0, at).wait_send()
            copy(1, at).wait_send()


def line_sum(block, chunks, collective_id):
    shape = jax.ShapeDtypeStruct(block.shape, block.dtype)
    buffer = pltpu.VMEM(block.shape, block.dtype)
    return pl.pallas_call(
        partial(line_sum_kernel, chunks),
        out_shape=shape,
        in_specs=[pl.BlockSpec(memory_space=pltpu.VMEM)],
        out_specs=pl.BlockSpec(memory_space=pltpu.VMEM),
        scratch_shapes=[buffer] * 4
        + [pltpu.SemaphoreType.DMA((2, chunks)), pltpu.SemaphoreType.DMA((2, chunks))],
        compiler_params=pltpu.CompilerParams(
            collective_id=collective_id, has_side_effects=True, vmem_limit_bytes=VMEM_LIMIT
        ),
        cost_estimate=pl.CostEstimate(
            flops=0, bytes_accessed=100 * block.size, transcendentals=0
        ),
    )(block)


SMALL_BLOCK = (8, 384)
PLANE = 8


def exchange_kernel(
    chunks,
    g_ref,
    small_ref,
    out_ref,
    small_out,
    pair_in,
    plane_send,
    plane_recv,
    small_in,
    small_line,
    pair_sems,
    plane_sems,
    line_sems,
    small_plane_sems,
    small_line_sems,
    small_out_sems,
):
    own = lax.axis_index("fsdp")
    place = lax.axis_index("seq")
    line = lax.axis_size("seq")
    core = lax.rem(own, 2)
    chip = lax.div(own, 2)
    partner = own + 1 - 2 * core
    block = g_ref.shape[0] // PLANE
    rows = block // chunks

    def plane_peer(step):
        return lax.rem(own + step, PLANE)

    def line_peer(step):
        return lax.rem(place + step, line)

    barrier = pltpu.get_barrier_semaphore()
    for step in range(1, PLANE):
        pl.semaphore_signal(
            barrier, inc=1, device_id={"fsdp": plane_peer(step)}, device_id_type=MESH
        )
    for step in range(1, line):
        pl.semaphore_signal(
            barrier, inc=1, device_id={"seq": line_peer(step)}, device_id_type=MESH
        )
    pl.semaphore_wait(barrier, PLANE - 1 + line - 1)

    def send(source, target, sems, at, device):
        return pltpu.make_async_remote_copy(
            src_ref=source,
            dst_ref=target,
            send_sem=sems.at[(0,) + at],
            recv_sem=sems.at[(1,) + at],
            device_id=device,
            device_id_type=MESH,
        )

    def owned_rows(owner, at):
        return pl.ds(pl.multiple_of(owner * block + at * rows, 16), rows)

    def pair_copy(other, at):
        target = lax.rem(chip + other, 4)
        return send(
            g_ref.at[owned_rows(2 * target + 1 - core, at)],
            pair_in.at[other, pl.ds(at * rows, rows)],
            pair_sems,
            (other, at),
            {"fsdp": partner},
        )

    def plane_copy(other, at):
        target = lax.rem(chip + other, 4)
        span = pl.ds(at * rows, rows)
        return send(
            plane_send.at[other - 1, span],
            plane_recv.at[other - 1, span],
            plane_sems,
            (other - 1, at),
            {"fsdp": 2 * target + core},
        )

    def line_copy(step, at):
        span = pl.ds(at * rows, rows)
        return send(
            out_ref.at[place, span],
            out_ref.at[place, span],
            line_sems,
            (step - 1, at),
            {"seq": line_peer(step)},
        )

    def small_plane_copy(step):
        return send(
            small_ref.at[plane_peer(step)],
            small_in.at[step - 1],
            small_plane_sems,
            (step - 1,),
            {"fsdp": plane_peer(step)},
        )

    def small_line_copy(step):
        return send(
            small_line.at[place],
            small_line.at[place],
            small_line_sems,
            (step - 1,),
            {"seq": line_peer(step)},
        )

    def small_out_copy(step):
        return send(
            small_out.at[own],
            small_out.at[own],
            small_out_sems,
            (step - 1,),
            {"fsdp": plane_peer(step)},
        )

    for at in range(chunks):
        for other in (1, 2, 3, 0):
            pair_copy(other, at).start()
        if at == 0:
            for step in range(1, PLANE):
                small_plane_copy(step).start()
    for at in range(chunks):
        for other in (1, 2, 3, 0):
            pair_copy(other, at).wait_recv()
            if other:
                span = pl.ds(at * rows, rows)
                target = lax.rem(chip + other, 4)
                both = g_ref[owned_rows(2 * target + core, at)] + pair_in[other, span]
                plane_send[other - 1, span] = low(both)
                plane_copy(other, at).start()
    for step in range(1, PLANE):
        small_plane_copy(step).wait_recv()
    total = small_ref[own]
    for step in range(1, PLANE):
        total = total + small_in[step - 1]
    small_line[place] = total
    for step in range(1, line):
        small_line_copy(step).start()
    for at in range(chunks):
        span = pl.ds(at * rows, rows)
        total = g_ref[owned_rows(own, at)] + pair_in[0, span]
        for other in (1, 2, 3):
            plane_copy(other, at).wait_recv()
            total = total + plane_recv[other - 1, span].astype(jnp.float32)
        out_ref[place, span] = low(total)
        for step in range(1, line):
            line_copy(step, at).start()
    for step in range(1, line):
        small_line_copy(step).wait_recv()
    total = small_line[0]
    for at in range(1, small_line.shape[0]):
        total = total + small_line[at]
    small_out[own] = total
    for step in range(1, PLANE):
        small_out_copy(step).start()
    for step in range(1, PLANE):
        small_out_copy(step).wait()
        small_plane_copy(step).wait_send()
    for step in range(1, line):
        small_line_copy(step).wait_send()
        for at in range(chunks):
            line_copy(step, at).wait()
    for at in range(chunks):
        for other in range(4):
            pair_copy(other, at).wait_send()
            if other:
                plane_copy(other, at).wait_send()


def exchange(grads, small, line, collective_id, chunks=3):
    plane = lax.axis_size("fsdp")
    total, width = grads.shape
    if plane != PLANE or total % (PLANE * 16 * chunks):
        own = lax.psum_scatter(grads, "fsdp", scatter_dimension=0, tiled=True)
        return lax.all_gather(low(own), "seq", axis=0, tiled=False), lax.psum(
            small, ("fsdp", "seq")
        )
    block = total // PLANE
    padded = PLANE * SMALL_BLOCK[0] * SMALL_BLOCK[1]
    blocks = jnp.pad(small, (0, padded - small.shape[0])).reshape((PLANE,) + SMALL_BLOCK)
    dma = pltpu.SemaphoreType.DMA
    gathered, summed = pl.pallas_call(
        partial(exchange_kernel, chunks),
        out_shape=[
            jax.ShapeDtypeStruct((line, block, width), jnp.bfloat16),
            jax.ShapeDtypeStruct(blocks.shape, jnp.float32),
        ],
        in_specs=[pl.BlockSpec(memory_space=pltpu.VMEM)] * 2,
        out_specs=[pl.BlockSpec(memory_space=pltpu.VMEM)] * 2,
        scratch_shapes=[
            pltpu.VMEM((4, block, width), jnp.float32),
            pltpu.VMEM((3, block, width), jnp.bfloat16),
            pltpu.VMEM((3, block, width), jnp.bfloat16),
            pltpu.VMEM((PLANE - 1,) + SMALL_BLOCK, jnp.float32),
            pltpu.VMEM((line,) + SMALL_BLOCK, jnp.float32),
            dma((2, 4, chunks)),
            dma((2, 3, chunks)),
            dma((2, line - 1, chunks)),
            dma((2, PLANE - 1)),
            dma((2, line - 1)),
            dma((2, PLANE - 1)),
        ],
        compiler_params=pltpu.CompilerParams(
            collective_id=collective_id, has_side_effects=True, vmem_limit_bytes=VMEM_LIMIT
        ),
        cost_estimate=pl.CostEstimate(
            flops=0, bytes_accessed=200 * 1024 * 1024, transcendentals=0
        ),
    )(grads, blocks)
    return gathered, summed.reshape(-1)


def gelu_parts(hidden):
    cdf = 0.5 * (1.0 + lax.erf(hidden * (2.0**-0.5)))
    density = jnp.exp(-0.5 * hidden * hidden) * (0.3989422804014327)
    return hidden * cdf, cdf + hidden * density


def adamw(weight, moment_one, moment_two, gradient, step_rate, decay_rate):
    moment_one = BETA_ONE * moment_one + (1 - BETA_ONE) * gradient
    moment_two = BETA_TWO * moment_two + (1 - BETA_TWO) * gradient * gradient
    fixed_one = moment_one / (1 - BETA_ONE**STEP)
    fixed_two = moment_two / (1 - BETA_TWO**STEP)
    weight = weight - step_rate * (
        fixed_one / (jnp.sqrt(fixed_two) + ADAM_EPS) + decay_rate * weight
    )
    return (moment_one, moment_two, weight)


def shards(
    pixels,
    restore,
    enc_w,
    enc_m,
    enc_v,
    dec_w,
    dec_m,
    dec_v,
    head_w,
    head_m,
    head_v,
    gain_w,
    gain_m,
    gain_v,
    bias_w,
    bias_m,
    bias_v,
):
    seq_count = lax.axis_size("seq")
    place = lax.axis_index("seq")
    images, own_count, _ = pixels.shape
    masked_total = images * lax.axis_size("fsdp") * (PATCHES - KEEP)

    enc_low = low(enc_w)
    enc_first = lax.all_gather(enc_low[:, : 5 * D_E], "fsdp", axis=0, tiled=True)
    enc_second = lax.all_gather(enc_low[:, 5 * D_E :], "fsdp", axis=0, tiled=True)
    dec_full = lax.all_gather(low(dec_w), "fsdp", axis=0, tiled=True)
    head_low = low(head_w)
    w_patch = enc_first[:, :D_E]
    e_qkv = enc_first[:, D_E : 4 * D_E]
    e_out = enc_first[:, 4 * D_E :]
    e_up = enc_second[:, :FF_E]
    e_down = enc_second[:, FF_E : 2 * FF_E]
    w_embed = enc_second[:, 2 * FF_E :]
    d_query = dec_full[:, :D_D]
    d_key = dec_full[:, D_D : 2 * D_D]
    d_value = dec_full[:, 2 * D_D : 3 * D_D]
    d_out = dec_full[:, 3 * D_D : 4 * D_D]
    d_up = dec_full[:, 4 * D_D : 4 * D_D + FF_D]
    d_down = dec_full[:, 4 * D_D + FF_D :]

    pieces = split_vector(bias_w, bias_widths())
    gains = split_vector(gain_w, [D_E, D_E, D_E, D_D, D_D, D_D])
    (b_patch, cls_token, e_shift1, e_bq, e_bv, e_bo, e_shift2, e_bu, e_bd, e_shift3) = pieces[:10]
    (b_embed, mask_token, d_shift1, d_bq, d_bv, d_bo, d_shift2, d_bu, d_bd, d_shift3) = pieces[
        10:20
    ]
    b_head = pieces[20]

    ranks = jnp.arange(KEEP, dtype=jnp.int32)
    turned = lax.dynamic_slice_in_dim(
        jnp.concatenate([restore, restore], axis=1), place * own_count, PATCHES, axis=1
    )
    own_restore = turned[:, :own_count]
    own_pick = low(own_restore[:, None, :] == ranks[None, :, None])
    own_kept = jnp.einsum("irp,ipd->ird", own_pick, pixels, preferred_element_type=jnp.float32)
    kept = line_sum(low(own_kept).reshape(images * KEEP, PIX), 8, 0).reshape(images, KEEP, PIX)
    patch_ids = jnp.arange(PATCHES, dtype=jnp.int32)
    keep_ids = jnp.sum(
        jnp.where(restore[:, None, :] == ranks[None, :, None], patch_ids, 0), axis=2
    )

    embedded = project(kept, w_patch) + (b_patch + positions(keep_ids, D_E))
    e_tail = jnp.where(jnp.arange(TAIL)[:, None] == 0, cls_token[None, :], 0.0)
    x0 = jnp.concatenate(
        [embedded, jnp.broadcast_to(e_tail[None], (images, TAIL, D_E))], axis=1
    )
    e_n1, e_sc1, e_inv1 = norm_forward(x0, gains[0], e_shift1)
    e_n1 = low(e_n1)
    e_qkv_bias = jnp.concatenate([e_bq, jnp.zeros_like(e_bq), e_bv])
    e_mixed = low(project(e_n1, e_qkv) + e_qkv_bias)
    e_q = e_mixed[:, :, :D_E]
    e_k = e_mixed[:, :, D_E : 2 * D_E]
    e_v = e_mixed[:, :, 2 * D_E :]
    e_o, e_lse = attend_forward(e_q, e_k, e_v, H_E)
    e_mid = x0 + project(e_o, e_out) + e_bo
    e_n2, e_sc2, e_inv2 = norm_forward(e_mid, gains[1], e_shift2)
    e_n2 = low(e_n2)
    e_hidden = project(e_n2, e_up) + e_bu
    e_gelu, e_slope = gelu_parts(e_hidden)
    e_act = low(e_gelu)
    encoded = e_mid + project_back(e_act, e_down) + e_bd
    e_n3, e_sc3, e_inv3 = norm_forward(encoded, gains[2], e_shift3)
    e_n3 = low(e_n3)
    shrunk = low(project(e_n3, w_embed) + b_embed)

    pick = low(turned[:, :, None] == ranks[None, None, :])
    is_masked = turned >= KEEP
    turned_ids = lax.rem(patch_ids + place * own_count, PATCHES)
    spread = jnp.einsum(
        "ipr,ird->ipd", pick, shrunk[:, :KEEP], preferred_element_type=jnp.float32
    )
    patch_rows = (
        jnp.where(is_masked[..., None], mask_token, spread) + positions(turned_ids, D_D)[None]
    )
    d_tail = jnp.where(
        jnp.arange(TAIL)[None, :, None] == 0,
        shrunk[:, KEEP : KEEP + 1].astype(jnp.float32),
        0.0,
    )
    y0 = jnp.concatenate([patch_rows, d_tail], axis=1)
    d_n1, d_sc1, d_inv1 = norm_forward(y0, gains[3], d_shift1)
    d_n1 = low(d_n1)

    y0_own = y0[:, :own_count]
    n1_own = d_n1[:, :own_count]
    d_q = low(project(n1_own, d_query) + d_bq)
    d_k = low(project(d_n1, d_key))
    d_v = low(project(d_n1, d_value) + d_bv)
    d_o, d_lse = attend_forward(d_q, d_k, d_v, H_D)
    d_mid = y0_own + project(d_o, d_out) + d_bo
    d_n2, d_sc2, d_inv2 = norm_forward(d_mid, gains[4], d_shift2)
    d_n2 = low(d_n2)
    d_hidden = project(d_n2, d_up) + d_bu
    d_gelu, d_slope = gelu_parts(d_hidden)
    d_act = low(d_gelu)
    decoded = d_mid + project_back(d_act, d_down) + d_bd
    d_n3, d_sc3, d_inv3 = norm_forward(decoded, gains[5], d_shift3)
    d_n3 = low(d_n3)
    predicted = project(d_n3, head_low) + b_head
    targets = pixels.astype(jnp.float32)
    centre = targets - jnp.mean(targets, axis=-1, keepdims=True)
    targets = centre * lax.rsqrt(
        jnp.sum(centre * centre, axis=-1, keepdims=True) / (PIX - 1) + PIXEL_EPS
    )
    errors = predicted - targets
    own_masked = (own_restore >= KEEP)[..., None]
    loss_part = (
        jnp.sum(jnp.where(own_masked, jnp.mean(errors * errors, axis=-1, keepdims=True), 0.0))
        / masked_total
    )

    pred_grad = jnp.where(own_masked, errors * (2.0 / (PIX * masked_total)), 0.0)
    pred_low = low(pred_grad)
    g_head = weight_grad(d_n3, pred_low)
    g_b_head = row_sum(pred_grad)
    d_up3, g_d_gain3, g_d_shift3 = norm_backward(
        project_back(pred_low, head_low), d_sc3, d_inv3, gains[5]
    )
    d_up3_low = low(d_up3)
    g_d_down = weight_grad(d_up3_low, d_act)
    g_d_bd = row_sum(d_up3)
    d_dhidden = low(project(d_up3_low, d_down) * d_slope)
    g_d_up = weight_grad(d_n2, d_dhidden)
    g_d_bu = row_sum(d_dhidden)
    through, g_d_gain2, g_d_shift2 = norm_backward(
        project_back(d_dhidden, d_up), d_sc2, d_inv2, gains[4]
    )
    d_dmid = d_up3 + through
    d_dmid_low = low(d_dmid)
    g_d_out = weight_grad(d_o, d_dmid_low)
    g_d_bo = row_sum(d_dmid)
    d_do = low(project_back(d_dmid_low, d_out))
    late_grads, d_do = lax.optimization_barrier(
        (jnp.concatenate([g_d_out, g_d_up, g_d_down, g_head], axis=1), d_do)
    )
    dec_late = lax.psum_scatter(late_grads, "fsdp", scatter_dimension=0, tiled=True)
    d_dq, d_dk, d_dv = attend_backward(d_q, d_k, d_v, d_lse, d_do, d_o, H_D)
    g_d_qkv = jnp.concatenate(
        [weight_grad(n1_own, d_dq), weight_grad(d_n1, d_dk), weight_grad(d_n1, d_dv)], axis=1
    )
    g_d_bq = row_sum(d_dq)
    g_d_bv = row_sum(d_dv)
    dn1 = project_back(d_dk, d_key) + project_back(d_dv, d_value)
    others = ((0, 0), (0, D_ROWS - own_count), (0, 0))
    dn1 = dn1 + jnp.pad(project_back(d_dq, d_query), others)
    dy0, g_d_gain1, g_d_shift1 = norm_backward(dn1, d_sc1, d_inv1, gains[3])
    dy0 = dy0 + jnp.pad(d_dmid, others)
    dy0_patch = dy0[:, :PATCHES]
    g_mask = jnp.sum(jnp.where(is_masked[..., None], dy0_patch, 0.0), axis=(0, 1))
    dy0_high = low(dy0_patch)
    dy0_rest = low(dy0_patch - dy0_high.astype(jnp.float32))
    de_patch = jnp.einsum(
        "ipr,ipd->ird", pick, dy0_high, preferred_element_type=jnp.float32
    ) + jnp.einsum("ipr,ipd->ird", pick, dy0_rest, preferred_element_type=jnp.float32)
    de_part = jnp.concatenate(
        [de_patch.reshape(images * KEEP, D_D), dy0[:, PATCHES], jnp.zeros((TAIL - images, D_D))],
        axis=0,
    )
    g_d_qkv, de_part = lax.optimization_barrier((g_d_qkv, low(de_part)))
    dec_early = lax.psum_scatter(g_d_qkv, "fsdp", scatter_dimension=0, tiled=True)
    de_sum = line_sum(de_part, 7, 1)
    dec_late, de_sum = lax.optimization_barrier((dec_late, de_sum))
    de = jnp.concatenate(
        [
            de_sum[: images * KEEP].reshape(images, KEEP, D_D),
            jnp.pad(de_sum[images * KEEP :][:images, None], ((0, 0), (0, TAIL - 1), (0, 0))),
        ],
        axis=1,
    )

    def own_columns(tensor):
        size = tensor.shape[2] // seq_count
        return lax.dynamic_slice_in_dim(tensor, place * size, size, axis=2)

    g_embed = weight_grad(e_n3, own_columns(de))
    g_b_embed = row_sum(de)
    e_up3, g_e_gain3, g_e_shift3 = norm_backward(
        project_back(de, w_embed), e_sc3, e_inv3, gains[2]
    )
    e_up3_low = low(e_up3)
    g_e_down = weight_grad(e_up3_low, own_columns(e_act))
    g_e_bd = row_sum(e_up3)
    e_dhidden = low(project(e_up3_low, e_down) * e_slope)
    g_e_up = weight_grad(e_n2, own_columns(e_dhidden))
    g_e_bu = row_sum(e_dhidden)
    through, g_e_gain2, g_e_shift2 = norm_backward(
        project_back(e_dhidden, e_up), e_sc2, e_inv2, gains[1]
    )
    e_dmid = e_up3 + through
    e_dmid_low = low(e_dmid)
    g_e_out = weight_grad(e_o, own_columns(e_dmid_low))
    g_e_bo = row_sum(e_dmid)
    e_do = low(project_back(e_dmid_low, e_out))
    dec_early, e_do = lax.optimization_barrier((dec_early, e_do))
    dec_grad_all = lax.psum(jnp.concatenate([dec_early, dec_late], axis=1), "seq")
    e_dq, e_dk, e_dv = attend_backward(e_q, e_k, e_v, e_lse, e_do, e_o, H_E)
    g_e_qkv = [weight_grad(e_n1, own_columns(part)) for part in (e_dq, e_dk, e_dv)]
    g_e_bq = row_sum(e_dq)
    g_e_bv = row_sum(e_dv)
    e_dmixed = jnp.concatenate([e_dq, e_dk, e_dv], axis=2)
    through, g_e_gain1, g_e_shift1 = norm_backward(
        project_back(e_dmixed, e_qkv), e_sc1, e_inv1, gains[0]
    )
    dx0 = e_dmid + through
    dx0_patch = dx0[:, :KEEP]
    g_patch = weight_grad(kept, own_columns(low(dx0_patch)))
    g_b_patch = row_sum(dx0_patch)
    g_cls = jnp.sum(dx0[:, KEEP], axis=0)
    enc_grads = jnp.concatenate([g_patch] + g_e_qkv + [g_e_out, g_e_up, g_e_down], axis=1)
    embed_own = lax.psum_scatter(g_embed, "fsdp", scatter_dimension=0, tiled=True)
    embed_all = lax.all_gather(embed_own, "seq", axis=0, tiled=False)

    once = jnp.where(place == 0, 1.0, 0.0)
    enc_bias = [g_b_patch, g_cls, g_e_shift1, g_e_bq, g_e_bv, g_e_bo, g_e_shift2, g_e_bu]
    enc_bias = jnp.concatenate(enc_bias + [g_e_bd, g_e_shift3, g_b_embed]) * once
    dec_bias = [g_mask, g_d_shift1, g_d_bq, g_d_bv, g_d_bo, g_d_shift2, g_d_bu, g_d_bd]
    dec_bias = jnp.concatenate(dec_bias + [g_d_shift3, g_b_head])
    enc_gain = jnp.concatenate([g_e_gain1, g_e_gain2, g_e_gain3]) * once
    dec_gain = jnp.concatenate([g_d_gain1, g_d_gain2, g_d_gain3])
    small = jnp.concatenate([enc_gain, dec_gain, enc_bias, dec_bias, loss_part[None]])
    dec_grad_all, enc_grads = lax.optimization_barrier((dec_grad_all, enc_grads))
    enc_all, small = exchange(enc_grads, small, seq_count, 2)
    dec_grad = dec_grad_all[:, : 4 * D_D + 2 * FF_D]
    head_grad = lax.all_gather(
        dec_grad_all[:, 4 * D_D + 2 * FF_D :], "fsdp", axis=0, tiled=True
    )

    def by_column(gathered, offset, size):
        return [gathered[at, :, offset : offset + size] for at in range(seq_count)]

    quarter_e = D_E // seq_count
    quarter_f = FF_E // seq_count
    spans = []
    for at in range(5):
        spans += by_column(enc_all, at * quarter_e, quarter_e)
    spans += by_column(enc_all, 5 * quarter_e, quarter_f)
    spans += by_column(enc_all, 5 * quarter_e + quarter_f, quarter_f)
    spans = [part.astype(jnp.float32) for part in spans]
    enc_grad = jnp.concatenate(spans + [embed_all[at] for at in range(seq_count)], axis=1)
    n_gain = gain_w.shape[0]
    n_bias = bias_w.shape[0]
    gain_grad = small[:n_gain]
    bias_grad = small[n_gain : n_gain + n_bias]
    loss_total = small[n_gain + n_bias]

    enc_new = adamw(enc_w, enc_m, enc_v, enc_grad, MATRIX_RATE, MATRIX_DECAY)
    dec_new = adamw(dec_w, dec_m, dec_v, dec_grad, MATRIX_RATE, MATRIX_DECAY)
    head_new = adamw(head_w, head_m, head_v, head_grad, MATRIX_RATE, MATRIX_DECAY)
    gain_new = adamw(gain_w, gain_m, gain_v, gain_grad, SMALL_RATE, 0.0)
    bias_new = adamw(bias_w, bias_m, bias_v, bias_grad, SMALL_RATE, 0.0)
    return (loss_total,) + enc_new + dec_new + head_new + gain_new + bias_new


def solution(mesh):
    rows = P("fsdp", None)
    in_specs = (P("fsdp", "seq", None), rows) + (rows,) * 6 + (P(),) * 9
    out_specs = (P(),) + (rows,) * 6 + (P(),) * 9
    return jax.shard_map(shards, mesh=mesh, in_specs=in_specs, out_specs=out_specs, check_vma=False)
```

```python
from functools import partial

import jax
import jax.numpy as jnp
from jax import lax
from jax.experimental import pallas as pl
from jax.experimental.pallas import tpu as pltpu
from jax.sharding import PartitionSpec as P

D_E = 768
H_E = 12
FF_E = 3072
D_D = 512
H_D = 16
FF_D = 2048
PIX = 768
PATCHES = 1024
KEEP = 256
STEP = 5

NORM_EPS = 1e-06
PIXEL_EPS = 1e-06
BETA_ONE = 0.5
BETA_TWO = 0.75
MATRIX_RATE = 0.03
SMALL_RATE = 0.1
MATRIX_DECAY = 0.05
ADAM_EPS = 1e-08

TAIL = 16
E_ROWS = KEEP + TAIL
D_ROWS = PATCHES + TAIL
LOG2E = 1.4426950408889634
MASKED_SCORE = -1e30


def bias_widths():
    return [D_E] * 7 + [FF_E] + [D_E] * 2 + [D_D] * 7 + [FF_D] + [D_D] * 2 + [PIX]


def split_vector(vector, widths):
    pieces = []
    offset = 0
    for span_width in widths:
        pieces.append(vector[offset : offset + span_width])
        offset += span_width
    return pieces


def positions(index_arr, width_dim):
    halves = width_dim // 2
    frequency = 10000.0 ** (-jnp.arange(halves, dtype=jnp.float32) / halves)
    angles = (index_arr.astype(jnp.float32) + 1.0)[..., None] * frequency
    return jnp.concatenate([jnp.sin(angles), jnp.cos(angles)], axis=-1)


def norm_forward(inputs, gain_vec, shift_vec):
    centre = inputs - jnp.mean(inputs, axis=-1, keepdims=True)
    inverse = lax.rsqrt(jnp.mean(centre * centre, axis=-1, keepdims=True) + NORM_EPS)
    scaled = centre * inverse
    return (scaled * gain_vec + shift_vec, scaled, inverse)


def norm_backward(upstream, scaled, inverse, gain_vec):
    weighted = upstream * gain_vec
    inner_part = (
        weighted
        - jnp.mean(weighted, axis=-1, keepdims=True)
        - scaled * jnp.mean(weighted * scaled, axis=-1, keepdims=True)
    )
    return (
        inverse * inner_part,
        jnp.sum(upstream * scaled, axis=(0, 1)),
        jnp.sum(upstream, axis=(0, 1)),
    )


def low(tensor):
    return tensor.astype(jnp.bfloat16)


def project(row_block, weight):
    return jnp.einsum("isd,de->ise", row_block, weight, preferred_element_type=jnp.float32)


def project_back(row_block, weight):
    return jnp.einsum("ise,de->isd", row_block, weight, preferred_element_type=jnp.float32)


def weight_grad(row_block, upstream):
    return jnp.einsum("isd,ise->de", row_block, upstream, preferred_element_type=jnp.float32)


def row_sum(tensor):
    return jnp.sum(tensor.astype(jnp.float32), axis=(0, 1))


def enc_mats_of(full_rows):
    return (
        full_rows[:, D_E : 4 * D_E],
        full_rows[:, 4 * D_E : 5 * D_E],
        full_rows[:, 5 * D_E : 5 * D_E + FF_E],
        full_rows[:, 5 * D_E + FF_E : 5 * D_E + 2 * FF_E],
    )


def dot_f32(left, right, contract):
    return lax.dot_general(
        left, right, (contract, ((), ())), preferred_element_type=jnp.float32
    )


NN = ((1,), (0,))
TN = ((0,), (0,))


def pieces_of(value):
    first = low(value).astype(jnp.float32)
    rest = value - first
    second = low(rest).astype(jnp.float32)
    return first, second, rest - second


def own_span(shape, axis, head, head_dim):
    place = lax.broadcasted_iota(jnp.int32, shape, axis)
    return (place >= head * head_dim) & (place < (head + 1) * head_dim)


def live_tail(rows, scores, other):
    place = lax.broadcasted_iota(jnp.int32, (rows, scores.shape[1]), 0)
    return jnp.where(place < 1, scores, other)


def attend_forward_kernel(heads, head_dim, q_ref, k_ref, v_ref, o_ref, lse_ref):
    main = k_ref.shape[1] - TAIL
    scale = head_dim ** (-0.5) * LOG2E
    q_t = q_ref[0].astype(jnp.float32).T * scale
    q_high = low(q_t)
    q_rest = low(q_t - q_high.astype(jnp.float32))
    k_main = k_ref[0, :main]
    k_tail = k_ref[0, main:]
    k_main = jnp.concatenate([k_main, k_main], axis=1)
    k_tail = jnp.concatenate([k_tail, k_tail], axis=1)
    v_main = low(v_ref[0, :main].astype(jnp.float32).T)
    v_tail = v_ref[0, main:]
    ones = jnp.ones((TAIL, main), jnp.bfloat16)

    def scores_of(head):
        own = own_span(q_t.shape, 0, head, head_dim)
        none = jnp.zeros_like(q_high)
        q_h = jnp.concatenate([jnp.where(own, q_high, none), jnp.where(own, q_rest, none)], axis=0)
        return dot_f32(k_main, q_h, NN), live_tail(TAIL, dot_f32(k_tail, q_h, NN), MASKED_SCORE)

    outs = []
    following = scores_of(0)
    for head in range(heads):
        span = slice(head * head_dim, (head + 1) * head_dim)
        s_main, s_tail = following
        if head + 1 < heads:
            following = scores_of(head + 1)
        top = jnp.maximum(
            jnp.max(s_main, axis=0, keepdims=True), jnp.max(s_tail, axis=0, keepdims=True)
        )
        p_main = low(jnp.exp2(s_main - top))
        p_tail = low(jnp.exp2(s_tail - top))
        o_t = dot_f32(jnp.concatenate([v_main[span], ones], axis=0), p_main, NN)
        total = o_t[head_dim : head_dim + 1] + jnp.sum(
            p_tail.astype(jnp.float32), axis=0, keepdims=True
        )
        o_t = o_t[:head_dim] + dot_f32(v_tail, p_tail, TN)[span]
        outs.append(o_t * (1.0 / total))
        lse_ref[0, 0, head : head + 1, :] = top + jnp.log2(total)
    o_ref[0] = low(jnp.concatenate(outs, axis=0).T)


def attend_backward_kernel(
    heads, head_dim, q_ref, k_ref, v_ref, lse_ref, do_ref, o_ref, dq_ref, dk_ref, dv_ref
):
    main = k_ref.shape[1] - TAIL
    rows = q_ref.shape[1]
    unit = head_dim ** (-0.5)
    q = q_ref[0]
    do = do_ref[0]
    q_t = q.astype(jnp.float32).T * (unit * LOG2E)
    q_high = low(q_t).astype(jnp.float32)
    q_rest = q_t - q_high
    do_t = do.astype(jnp.float32).T
    inner_t = do_t * o_ref[0].astype(jnp.float32).T
    place = lax.broadcasted_iota(jnp.int32, q_t.shape, 0)

    def with_row(block, offset, value):
        for at, part in enumerate(pieces_of(value)):
            block = jnp.where(place == offset + at, part, block)
        return block

    score_sides, value_sides = [], []
    for head in range(heads):
        own = own_span(q_t.shape, 0, head, head_dim)
        span = slice(head * head_dim, (head + 1) * head_dim)
        other = ((head + 1) % heads) * head_dim
        lse = lse_ref[0, 0, head : head + 1, :]
        inner = jnp.sum(inner_t[span], axis=0, keepdims=True)
        rest = with_row(jnp.where(own, q_rest, 0.0), other, -lse)
        score_sides.append(low(jnp.concatenate([jnp.where(own, q_high, 0.0), rest], axis=0)))
        last = with_row(jnp.zeros_like(do_t), 0, -inner)
        value_sides.append(low(jnp.concatenate([jnp.where(own, do_t, 0.0), last], axis=0)))
    zero = jnp.zeros_like(q)
    q_sides = [jnp.where(own_span(q.shape, 1, h, head_dim), q, zero) for h in range(heads)]
    do_sides = [jnp.where(own_span(q.shape, 1, h, head_dim), do, zero) for h in range(heads)]
    stacked = rows % 128 == 0
    if stacked:
        q_sides = jnp.concatenate(q_sides, axis=0)
        do_sides = jnp.concatenate(do_sides, axis=0)

    def sum_heads(parts, sides):
        if stacked:
            return dot_f32(jnp.concatenate(parts, axis=1), sides, NN)
        terms = [dot_f32(part, side, NN) for part, side in zip(parts, sides)]
        return sum(terms[1:], terms[0])

    k_main = k_ref[0, :main]
    k_tail = k_ref[0, main:]
    k_main_t = low(k_main.astype(jnp.float32).T)

    def with_ones(block):
        return jnp.concatenate([block, jnp.ones_like(block)], axis=1)

    def beside_own(block, head):
        own = jnp.where(own_span(block.shape, 1, head, head_dim), block, jnp.ones_like(block))
        return jnp.concatenate([block, own], axis=1)

    v_main = with_ones(v_ref[0, :main])
    v_tail = with_ones(v_ref[0, main:])
    dq_parts, p_mains, s_mains, p_tails, s_tails = [], [], [], [], []
    for head in range(heads):
        span = slice(head * head_dim, (head + 1) * head_dim)
        p = jnp.exp2(dot_f32(beside_own(k_main, head), score_sides[head], NN))
        s = low(p * dot_f32(v_main, value_sides[head], NN))
        p_mains.append(low(p))
        s_mains.append(s)
        p = jnp.exp2(dot_f32(beside_own(k_tail, head), score_sides[head], NN))
        p = live_tail(TAIL, p, 0.0)
        s_tail = low(p * dot_f32(v_tail, value_sides[head], NN))
        p_tails.append(low(p))
        s_tails.append(s_tail)
        dq_parts.append(dot_f32(k_main_t[span], s, NN) + dot_f32(k_tail, s_tail, TN)[span])
    dk_ref[0, :main] = low(sum_heads(s_mains, q_sides) * unit)
    dk_ref[0, main:] = low(sum_heads(s_tails, q_sides) * unit)
    dv_ref[0, :main] = low(sum_heads(p_mains, do_sides))
    dv_ref[0, main:] = low(sum_heads(p_tails, do_sides))
    dq_ref[0] = low(jnp.concatenate(dq_parts, axis=0).T * unit)


VMEM_LIMIT = 32 * 1024 * 1024


def attend_specs(q_rows, k_rows, heads):
    return (
        pl.BlockSpec((1, q_rows, 128), lambda i, g: (i, 0, g)),
        pl.BlockSpec((1, k_rows, 128), lambda i, g: (i, 0, g)),
        pl.BlockSpec((1, 1, heads, q_rows), lambda i, g: (i, g, 0, 0)),
    )


def attend_forward(queries, key_rows, value_rows, head_count):
    images, q_rows, width = queries.shape
    k_rows = key_rows.shape[1]
    head_dim = width // head_count
    heads = 128 // head_dim
    groups = width // 128
    q_spec, k_spec, l_spec = attend_specs(q_rows, k_rows, heads)
    return pl.pallas_call(
        partial(attend_forward_kernel, heads, head_dim),
        grid=(images, groups),
        in_specs=[q_spec, k_spec, k_spec],
        out_specs=[q_spec, l_spec],
        out_shape=[
            jax.ShapeDtypeStruct((images, q_rows, width), jnp.bfloat16),
            jax.ShapeDtypeStruct((images, groups, heads, q_rows), jnp.float32),
        ],
        compiler_params=pltpu.CompilerParams(vmem_limit_bytes=VMEM_LIMIT),
        cost_estimate=pl.CostEstimate(
            flops=16 * images * q_rows * k_rows * width,
            bytes_accessed=4 * images * (q_rows + k_rows) * width,
            transcendentals=images * head_count * q_rows * k_rows,
        ),
    )(queries, key_rows, value_rows)


def attend_backward(queries, key_rows, value_rows, logsum, upstream, attended, head_count):
    images, q_rows, width = queries.shape
    k_rows = key_rows.shape[1]
    head_dim = width // head_count
    heads = 128 // head_dim
    groups = width // 128
    q_spec, k_spec, l_spec = attend_specs(q_rows, k_rows, heads)
    return pl.pallas_call(
        partial(attend_backward_kernel, heads, head_dim),
        grid=(images, groups),
        in_specs=[q_spec, k_spec, k_spec, l_spec, q_spec, q_spec],
        out_specs=[q_spec, k_spec, k_spec],
        out_shape=[
            jax.ShapeDtypeStruct((images, q_rows, width), jnp.bfloat16),
            jax.ShapeDtypeStruct((images, k_rows, width), jnp.bfloat16),
            jax.ShapeDtypeStruct((images, k_rows, width), jnp.bfloat16),
        ],
        compiler_params=pltpu.CompilerParams(vmem_limit_bytes=VMEM_LIMIT),
        cost_estimate=pl.CostEstimate(
            flops=40 * images * q_rows * k_rows * width,
            bytes_accessed=8 * images * (q_rows + k_rows) * width,
            transcendentals=images * head_count * q_rows * k_rows,
        ),
    )(queries, key_rows, value_rows, logsum, upstream, attended)


MESH = pl.DeviceIdType.MESH


def line_sum_kernel(
    chunks, lines, x_ref, o_ref, from_left, from_right, to_left, to_right, send_sem, recv_sem
):
    count = lax.axis_size("seq")
    place = lax.axis_index("seq")
    has_left = place > 0
    has_right = place < count - 1
    rows = x_ref.shape[0] // chunks
    barrier = pltpu.get_barrier_semaphore()

    def greet(to):
        pl.semaphore_signal(barrier, inc=1, device_id={"seq": to}, device_id_type=MESH)

    pl.when(has_left)(lambda: greet(place - 1))
    pl.when(has_right)(lambda: greet(place + 1))
    peers = jnp.where(has_left, 1, 0) + jnp.where(has_right, 1, 0)
    pl.semaphore_wait(barrier, peers)

    def copy(way, at):
        span = pl.ds(pl.multiple_of(at * rows, 16), rows)
        source, target = ((to_right, from_left), (to_left, from_right))[way]
        return pltpu.make_async_remote_copy(
            src_ref=source.at[span],
            dst_ref=target.at[span],
            send_sem=send_sem.at[way, at],
            recv_sem=recv_sem.at[way, at],
            device_id={"seq": place + 1 if way == 0 else place - 1},
            device_id_type=MESH,
        )

    def end_copy(way, at):
        span = pl.ds(at * rows, rows)
        return pltpu.make_async_remote_copy(
            src_ref=x_ref.at[span],
            dst_ref=(from_left, from_right)[way].at[span],
            send_sem=send_sem.at[way, at],
            recv_sem=recv_sem.at[way, at],
            device_id={"seq": place + 1 if way == 0 else place - 1},
            device_id_type=MESH,
        )

    for way, is_end in ((0, jnp.logical_not(has_left)), (1, jnp.logical_not(has_right))):

        @pl.when(is_end)
        def _():
            for at in range(chunks):
                if at >= 2:
                    end_copy(way, at - 2).wait_send()
                end_copy(way, at).start()
            for at in range(chunks - 2, chunks):
                end_copy(way, at).wait_send()

    def span_of(at):
        return pl.ds(pl.multiple_of(at * rows, 16), rows)

    for step in range(chunks + lines - 1):
        from_first = step - place
        from_last = step - (count - 1 - place)

        @pl.when(has_left & (from_first >= 0) & (from_first < chunks))
        def _():
            copy(0, from_first).wait_recv()

            @pl.when(has_right)
            def _():
                span = span_of(from_first)
                to_right[span] = x_ref[span] + from_left[span]
                copy(0, from_first).start()

        @pl.when(has_right & (from_last >= 0) & (from_last < chunks))
        def _():
            copy(1, from_last).wait_recv()

            @pl.when(has_left)
            def _():
                span = span_of(from_last)
                to_left[span] = x_ref[span] + from_right[span]
                copy(1, from_last).start()

    @pl.when(jnp.logical_not(has_left))
    def _():
        o_ref[...] = x_ref[...] + from_right[...]

    @pl.when(jnp.logical_not(has_right))
    def _():
        o_ref[...] = x_ref[...] + from_left[...]

    @pl.when(has_left & has_right)
    def _():
        o_ref[...] = (x_ref[...] + from_left[...]) + from_right[...]
        for at in range(chunks):
            copy(0, at).wait_send()
            copy(1, at).wait_send()


def line_sum(block, chunks, collective_id):
    shape = jax.ShapeDtypeStruct(block.shape, block.dtype)
    buffer = pltpu.VMEM(block.shape, block.dtype)
    return pl.pallas_call(
        partial(line_sum_kernel, chunks, lax.axis_size("seq")),
        out_shape=shape,
        in_specs=[pl.BlockSpec(memory_space=pltpu.VMEM)],
        out_specs=pl.BlockSpec(memory_space=pltpu.VMEM),
        scratch_shapes=[buffer] * 4
        + [pltpu.SemaphoreType.DMA((2, chunks)), pltpu.SemaphoreType.DMA((2, chunks))],
        compiler_params=pltpu.CompilerParams(
            collective_id=collective_id, has_side_effects=True, vmem_limit_bytes=VMEM_LIMIT
        ),
        cost_estimate=pl.CostEstimate(
            flops=0, bytes_accessed=100 * block.size, transcendentals=0
        ),
    )(block)


SMALL_BLOCK = (8, 384)
PLANE = 8


def exchange_kernel(
    chunks,
    g_ref,
    small_ref,
    out_ref,
    small_out,
    pair_in,
    plane_send,
    plane_recv,
    small_in,
    small_line,
    pair_sems,
    plane_sems,
    line_sems,
    small_plane_sems,
    small_line_sems,
    small_out_sems,
):
    own = lax.axis_index("fsdp")
    place = lax.axis_index("seq")
    line = lax.axis_size("seq")
    core = lax.rem(own, 2)
    chip = lax.div(own, 2)
    partner = own + 1 - 2 * core
    block = g_ref.shape[0] // PLANE
    rows = block // chunks

    def plane_peer(step):
        return lax.rem(own + step, PLANE)

    def line_peer(step):
        return lax.rem(place + step, line)

    barrier = pltpu.get_barrier_semaphore()
    for step in range(1, PLANE):
        pl.semaphore_signal(
            barrier, inc=1, device_id={"fsdp": plane_peer(step)}, device_id_type=MESH
        )
    for step in range(1, line):
        pl.semaphore_signal(
            barrier, inc=1, device_id={"seq": line_peer(step)}, device_id_type=MESH
        )
    pl.semaphore_wait(barrier, PLANE - 1 + line - 1)

    def send(source, target, sems, at, device):
        return pltpu.make_async_remote_copy(
            src_ref=source,
            dst_ref=target,
            send_sem=sems.at[(0,) + at],
            recv_sem=sems.at[(1,) + at],
            device_id=device,
            device_id_type=MESH,
        )

    def owned_rows(owner, at):
        return pl.ds(pl.multiple_of(owner * block + at * rows, 16), rows)

    def pair_copy(other, at):
        target = lax.rem(chip + other, 4)
        return send(
            g_ref.at[owned_rows(2 * target + 1 - core, at)],
            pair_in.at[other, pl.ds(at * rows, rows)],
            pair_sems,
            (other, at),
            {"fsdp": partner},
        )

    def plane_copy(other, at):
        target = lax.rem(chip + other, 4)
        span = pl.ds(at * rows, rows)
        return send(
            plane_send.at[other - 1, span],
            plane_recv.at[other - 1, span],
            plane_sems,
            (other - 1, at),
            {"fsdp": 2 * target + core},
        )

    def line_copy(step, at):
        span = pl.ds(at * rows, rows)
        return send(
            out_ref.at[place, span],
            out_ref.at[place, span],
            line_sems,
            (step - 1, at),
            {"seq": line_peer(step)},
        )

    def small_plane_copy(step):
        return send(
            small_ref.at[plane_peer(step)],
            small_in.at[step - 1],
            small_plane_sems,
            (step - 1,),
            {"fsdp": plane_peer(step)},
        )

    def small_line_copy(step):
        return send(
            small_line.at[place],
            small_line.at[place],
            small_line_sems,
            (step - 1,),
            {"seq": line_peer(step)},
        )

    def small_out_copy(step):
        return send(
            small_out.at[own],
            small_out.at[own],
            small_out_sems,
            (step - 1,),
            {"fsdp": plane_peer(step)},
        )

    for at in range(chunks):
        for other in (1, 2, 3, 0):
            pair_copy(other, at).start()
        if at == 0:
            for step in range(1, PLANE):
                small_plane_copy(step).start()
    for at in range(chunks):
        for other in (1, 2, 3, 0):
            pair_copy(other, at).wait_recv()
            if other:
                span = pl.ds(at * rows, rows)
                target = lax.rem(chip + other, 4)
                both = g_ref[owned_rows(2 * target + core, at)] + pair_in[other, span]
                plane_send[other - 1, span] = low(both)
                plane_copy(other, at).start()
    for step in range(1, PLANE):
        small_plane_copy(step).wait_recv()
    total = small_ref[own]
    for step in range(1, PLANE):
        total = total + small_in[step - 1]
    small_line[place] = total
    for step in range(1, line):
        small_line_copy(step).start()
    for at in range(chunks):
        span = pl.ds(at * rows, rows)
        total = g_ref[owned_rows(own, at)] + pair_in[0, span]
        for other in (1, 2, 3):
            plane_copy(other, at).wait_recv()
            total = total + plane_recv[other - 1, span].astype(jnp.float32)
        out_ref[place, span] = low(total)
        for step in range(1, line):
            line_copy(step, at).start()
    for step in range(1, line):
        small_line_copy(step).wait_recv()
    total = small_line[0]
    for at in range(1, small_line.shape[0]):
        total = total + small_line[at]
    small_out[own] = total
    for step in range(1, PLANE):
        small_out_copy(step).start()
    for step in range(1, PLANE):
        small_out_copy(step).wait()
        small_plane_copy(step).wait_send()
    for step in range(1, line):
        small_line_copy(step).wait_send()
        for at in range(chunks):
            line_copy(step, at).wait()
    for at in range(chunks):
        for other in range(4):
            pair_copy(other, at).wait_send()
            if other:
                plane_copy(other, at).wait_send()


def exchange(grads, small, line, collective_id, chunks=3):
    plane = lax.axis_size("fsdp")
    total, width = grads.shape
    if plane != PLANE or total % (PLANE * 16 * chunks):
        own = lax.psum_scatter(grads, "fsdp", scatter_dimension=0, tiled=True)
        return lax.all_gather(low(own), "seq", axis=0, tiled=False), lax.psum(
            small, ("fsdp", "seq")
        )
    block = total // PLANE
    padded = PLANE * SMALL_BLOCK[0] * SMALL_BLOCK[1]
    blocks = jnp.pad(small, (0, padded - small.shape[0])).reshape((PLANE,) + SMALL_BLOCK)
    dma = pltpu.SemaphoreType.DMA
    gathered, summed = pl.pallas_call(
        partial(exchange_kernel, chunks),
        out_shape=[
            jax.ShapeDtypeStruct((line, block, width), jnp.bfloat16),
            jax.ShapeDtypeStruct(blocks.shape, jnp.float32),
        ],
        in_specs=[pl.BlockSpec(memory_space=pltpu.VMEM)] * 2,
        out_specs=[pl.BlockSpec(memory_space=pltpu.VMEM)] * 2,
        scratch_shapes=[
            pltpu.VMEM((4, block, width), jnp.float32),
            pltpu.VMEM((3, block, width), jnp.bfloat16),
            pltpu.VMEM((3, block, width), jnp.bfloat16),
            pltpu.VMEM((PLANE - 1,) + SMALL_BLOCK, jnp.float32),
            pltpu.VMEM((line,) + SMALL_BLOCK, jnp.float32),
            dma((2, 4, chunks)),
            dma((2, 3, chunks)),
            dma((2, line - 1, chunks)),
            dma((2, PLANE - 1)),
            dma((2, line - 1)),
            dma((2, PLANE - 1)),
        ],
        compiler_params=pltpu.CompilerParams(
            collective_id=collective_id, has_side_effects=True, vmem_limit_bytes=VMEM_LIMIT
        ),
        cost_estimate=pl.CostEstimate(
            flops=0, bytes_accessed=200 * 1024 * 1024, transcendentals=0
        ),
    )(grads, blocks)
    return gathered, summed.reshape(-1)


def gelu_parts(hidden):
    cdf = 0.5 * (1.0 + lax.erf(hidden * (2.0**-0.5)))
    density = jnp.exp(-0.5 * hidden * hidden) * (0.3989422804014327)
    return hidden * cdf, cdf + hidden * density


NT = ((1,), (1,))


def norm_rows(rows):
    centre = rows - jnp.mean(rows, axis=-1, keepdims=True)
    inverse = lax.rsqrt(jnp.mean(centre * centre, axis=-1, keepdims=True) + NORM_EPS)
    return centre * inverse, inverse


def norm_rows_back(upstream, scaled, inverse, gain):
    weighted = upstream * gain
    inner = (
        weighted
        - jnp.mean(weighted, axis=-1, keepdims=True)
        - scaled * jnp.mean(weighted * scaled, axis=-1, keepdims=True)
    )
    return inverse * inner, column_sum(upstream * scaled), column_sum(upstream)


def column_sum(rows):
    return jnp.sum(rows, axis=0, keepdims=True)


def clear_first(refs):
    @pl.when(pl.program_id(0) == 0)
    def _():
        for ref in refs:
            ref[...] = jnp.zeros_like(ref)


def dec_middle_kernel(
    grad_scale,
    o_ref,
    y_ref,
    pixel_ref,
    masked_ref,
    out_w,
    up_w,
    down_w,
    head_w,
    vec_ref,
    bu_ref,
    bh_ref,
    do_ref,
    dmid_ref,
    grad_ref,
    vec_grad,
    bu_grad,
    bh_grad,
    slope_ref,
    act_ref,
):
    clear_first((grad_ref, vec_grad, bu_grad, bh_grad))
    bo, gain2, shift2, bd, gain3, shift3 = (vec_ref[i : i + 1, :] for i in range(6))
    attended = o_ref[0]
    middle = y_ref[0] + dot_f32(attended, out_w[...], NN) + bo
    scaled2, inverse2 = norm_rows(middle)
    second = low(scaled2 * gain2 + shift2)
    size = 512
    decoded = middle + bd
    for at in range(0, FF_D, size):
        span = slice(at, at + size)
        value, slope = gelu_parts(dot_f32(second, up_w[:, span], NN) + bu_ref[:, span])
        slope_ref[:, span] = slope
        act_ref[:, span] = low(value)
        decoded = decoded + dot_f32(act_ref[:, span], down_w[:, span], NT)
    scaled3, inverse3 = norm_rows(decoded)
    third = low(scaled3 * gain3 + shift3)
    predicted = dot_f32(third, head_w[...], NN) + bh_ref[...]
    pixel = pixel_ref[0].astype(jnp.float32)
    centre = pixel - jnp.mean(pixel, axis=-1, keepdims=True)
    target = centre * lax.rsqrt(
        jnp.sum(centre * centre, axis=-1, keepdims=True) / (PIX - 1) + PIXEL_EPS
    )
    masked = masked_ref[0][:, :1]
    error = (predicted - target) * masked
    pred_grad = error * grad_scale
    pred_low = low(pred_grad)
    bh_grad[0:1, :] += column_sum(pred_grad)
    bh_grad[1:2, :] += column_sum(error * error)
    o_span, u_span = D_D, D_D + FF_D
    h_span = D_D + 2 * FF_D
    grad_ref[:, h_span:] += dot_f32(third, pred_low, TN)
    up3, g_gain3, g_shift3 = norm_rows_back(
        dot_f32(pred_low, head_w[...], NT), scaled3, inverse3, gain3
    )
    up3_low = low(up3)
    back = jnp.zeros_like(up3)
    for at in range(0, FF_D, size):
        span = slice(at, at + size)
        hidden_grad = low(dot_f32(up3_low, down_w[:, span], NN) * slope_ref[:, span])
        grad_ref[:, u_span + at : u_span + at + size] += dot_f32(up3_low, act_ref[:, span], TN)
        grad_ref[:, o_span + at : o_span + at + size] += dot_f32(second, hidden_grad, TN)
        bu_grad[0:1, span] += column_sum(hidden_grad.astype(jnp.float32))
        back = back + dot_f32(hidden_grad, up_w[:, span], NT)
    through, g_gain2, g_shift2 = norm_rows_back(back, scaled2, inverse2, gain2)
    middle_grad = up3 + through
    middle_low = low(middle_grad)
    dmid_ref[0] = middle_grad
    grad_ref[:, :o_span] += dot_f32(attended, middle_low, TN)
    do_ref[0] = low(dot_f32(middle_low, out_w[...], NT))
    sums = (column_sum(middle_grad), g_gain2, g_shift2, column_sum(up3), g_gain3, g_shift3)
    for at, part in enumerate(sums):
        vec_grad[at : at + 1, :] += part


def whole(shape):
    return pl.BlockSpec(shape, lambda i: (0,) * len(shape), pipeline_mode=pl.Buffered(1))


def columns(rows, width, at):
    return pl.BlockSpec((rows, width), lambda i: (0, at), pipeline_mode=pl.Buffered(1))


def per_image(rows, width):
    return pl.BlockSpec((1, rows, width), lambda i: (i, 0, 0))


def dec_middle(attended, y_own, pixels, masked, dec_full, head_low, vectors, bu, bh, grad_scale):
    images, rows, _ = attended.shape
    f32 = jnp.float32
    return pl.pallas_call(
        partial(dec_middle_kernel, grad_scale),
        grid=(images,),
        in_specs=[
            per_image(rows, D_D),
            per_image(rows, D_D),
            per_image(rows, PIX),
            per_image(rows, 128),
            columns(D_D, D_D, 3),
            columns(D_D, FF_D, 1),
            columns(D_D, FF_D, 2),
            whole((D_D, PIX)),
            whole((8, D_D)),
            whole((1, FF_D)),
            whole((1, PIX)),
        ],
        out_specs=[
            per_image(rows, D_D),
            per_image(rows, D_D),
            whole((D_D, D_D + 2 * FF_D + PIX)),
            whole((8, D_D)),
            whole((8, FF_D)),
            whole((8, PIX)),
        ],
        out_shape=[
            jax.ShapeDtypeStruct((images, rows, D_D), jnp.bfloat16),
            jax.ShapeDtypeStruct((images, rows, D_D), f32),
            jax.ShapeDtypeStruct((D_D, D_D + 2 * FF_D + PIX), f32),
            jax.ShapeDtypeStruct((8, D_D), f32),
            jax.ShapeDtypeStruct((8, FF_D), f32),
            jax.ShapeDtypeStruct((8, PIX), f32),
        ],
        scratch_shapes=[pltpu.VMEM((rows, FF_D), f32), pltpu.VMEM((rows, FF_D), jnp.bfloat16)],
        compiler_params=pltpu.CompilerParams(vmem_limit_bytes=44 * 1024 * 1024),
        cost_estimate=pl.CostEstimate(
            flops=12 * images * rows * D_D * (D_D + 2 * FF_D + PIX),
            bytes_accessed=30 * 1024 * 1024,
            transcendentals=2 * images * rows * FF_D,
        ),
    )(
        attended, y_own, pixels, masked, dec_full, dec_full, dec_full, head_low, vectors, bu, bh
    )


def dec_entry_back_kernel(
    y_ref,
    dq_ref,
    dk_ref,
    dv_ref,
    dmid_ref,
    rank_ref,
    q_w,
    k_w,
    v_w,
    vec_ref,
    de_ref,
    grad_ref,
    vec_grad,
    cls_ref,
):
    image = pl.program_id(0)
    clear_first((grad_ref, vec_grad, cls_ref))
    gain, shift = vec_ref[0:1, :], vec_ref[1:2, :]
    scaled, inverse = norm_rows(y_ref[0])
    normed = low(scaled * gain + shift)
    dq, dk, dv = dq_ref[0], dk_ref[0], dv_ref[0]
    own = dq.shape[0]
    grad_ref[:, :D_D] += dot_f32(normed[:own], dq, TN)
    grad_ref[:, D_D : 2 * D_D] += dot_f32(normed, dk, TN)
    grad_ref[:, 2 * D_D :] += dot_f32(normed, dv, TN)
    up = dot_f32(dk, k_w[...], NT) + dot_f32(dv, v_w[...], NT)
    up = jnp.concatenate([up[:own] + dot_f32(dq, q_w[...], NT), up[own:]], axis=0)
    back, g_gain, g_shift = norm_rows_back(up, scaled, inverse, gain)
    back = jnp.concatenate([back[:own] + dmid_ref[0], back[own:]], axis=0)
    patches = back[:PATCHES]
    high = low(patches)
    rest = low(patches - high.astype(jnp.float32))
    ranks = rank_ref[0]
    at = lax.broadcasted_iota(jnp.int32, (KEEP, PATCHES), 0)
    pick = low(jnp.where(at == ranks, 1.0, 0.0))
    hidden = low(jnp.where(jnp.broadcast_to(ranks, (16, PATCHES)) >= KEEP, 1.0, 0.0))
    de_ref[pl.ds(pl.multiple_of(image * KEEP, KEEP), KEEP)] = low(dot_f32(pick, high, NN))
    g_mask = dot_f32(hidden, high, NN) + dot_f32(hidden, rest, NN)
    cls_ref[pl.ds(image, 1), :] = back[PATCHES : PATCHES + 1]
    sums = (
        g_mask[0:1],
        g_shift,
        column_sum(dq.astype(jnp.float32)),
        column_sum(dv.astype(jnp.float32)),
        g_gain,
    )
    for at, part in enumerate(sums):
        vec_grad[at : at + 1, :] += part

    @pl.when(image == pl.num_programs(0) - 1)
    def _():
        de_ref[de_ref.shape[0] - TAIL :] = low(cls_ref[...])


def dec_entry_back(y0, dq, dk, dv, dmid, ranks, dec_full, vectors):
    images, rows, _ = y0.shape
    own = dq.shape[1]
    f32 = jnp.float32
    return pl.pallas_call(
        dec_entry_back_kernel,
        grid=(images,),
        in_specs=[
            per_image(rows, D_D),
            per_image(own, D_D),
            per_image(rows, D_D),
            per_image(rows, D_D),
            per_image(own, D_D),
            per_image(1, PATCHES),
            columns(D_D, D_D, 0),
            columns(D_D, D_D, 1),
            columns(D_D, D_D, 2),
            whole((8, D_D)),
        ],
        out_specs=[whole((images * KEEP + TAIL, D_D)), whole((D_D, 3 * D_D)), whole((8, D_D))],
        out_shape=[
            jax.ShapeDtypeStruct((images * KEEP + TAIL, D_D), jnp.bfloat16),
            jax.ShapeDtypeStruct((D_D, 3 * D_D), f32),
            jax.ShapeDtypeStruct((8, D_D), f32),
        ],
        scratch_shapes=[pltpu.VMEM((TAIL, D_D), f32)],
        compiler_params=pltpu.CompilerParams(vmem_limit_bytes=44 * 1024 * 1024),
        cost_estimate=pl.CostEstimate(
            flops=12 * images * rows * D_D * D_D * 2,
            bytes_accessed=24 * 1024 * 1024,
            transcendentals=0,
        ),
    )(y0, dq, dk, dv, dmid, ranks, dec_full, dec_full, dec_full, vectors)


def stack_rows(parts):
    rows = jnp.stack(parts)
    return jnp.pad(rows, ((0, 8 - len(parts)), (0, 0)))


def adamw(weight, moment_one, moment_two, gradient, step_rate, decay_rate):
    moment_one = BETA_ONE * moment_one + (1 - BETA_ONE) * gradient
    moment_two = BETA_TWO * moment_two + (1 - BETA_TWO) * gradient * gradient
    fixed_one = moment_one / (1 - BETA_ONE**STEP)
    fixed_two = moment_two / (1 - BETA_TWO**STEP)
    weight = weight - step_rate * (
        fixed_one / (jnp.sqrt(fixed_two) + ADAM_EPS) + decay_rate * weight
    )
    return (moment_one, moment_two, weight)


def shards(
    pixels,
    restore,
    enc_w,
    enc_m,
    enc_v,
    dec_w,
    dec_m,
    dec_v,
    head_w,
    head_m,
    head_v,
    gain_w,
    gain_m,
    gain_v,
    bias_w,
    bias_m,
    bias_v,
):
    seq_count = lax.axis_size("seq")
    place = lax.axis_index("seq")
    images, own_count, _ = pixels.shape
    masked_total = images * lax.axis_size("fsdp") * (PATCHES - KEEP)

    enc_low = low(enc_w)
    enc_first = lax.all_gather(enc_low[:, : 5 * D_E], "fsdp", axis=0, tiled=True)
    enc_second = lax.all_gather(enc_low[:, 5 * D_E :], "fsdp", axis=0, tiled=True)
    dec_full = lax.all_gather(low(dec_w), "fsdp", axis=0, tiled=True)
    head_low = low(head_w)
    w_patch = enc_first[:, :D_E]
    e_qkv = enc_first[:, D_E : 4 * D_E]
    e_out = enc_first[:, 4 * D_E :]
    e_up = enc_second[:, :FF_E]
    e_down = enc_second[:, FF_E : 2 * FF_E]
    w_embed = enc_second[:, 2 * FF_E :]
    d_query = dec_full[:, :D_D]
    d_key = dec_full[:, D_D : 2 * D_D]
    d_value = dec_full[:, 2 * D_D : 3 * D_D]

    pieces = split_vector(bias_w, bias_widths())
    gains = split_vector(gain_w, [D_E, D_E, D_E, D_D, D_D, D_D])
    (b_patch, cls_token, e_shift1, e_bq, e_bv, e_bo, e_shift2, e_bu, e_bd, e_shift3) = pieces[:10]
    (b_embed, mask_token, d_shift1, d_bq, d_bv, d_bo, d_shift2, d_bu, d_bd, d_shift3) = pieces[
        10:20
    ]
    b_head = pieces[20]

    ranks = jnp.arange(KEEP, dtype=jnp.int32)
    turned = lax.dynamic_slice_in_dim(
        jnp.concatenate([restore, restore], axis=1), place * own_count, PATCHES, axis=1
    )
    own_restore = turned[:, :own_count]
    own_pick = low(own_restore[:, None, :] == ranks[None, :, None])
    own_kept = jnp.einsum("irp,ipd->ird", own_pick, pixels, preferred_element_type=jnp.float32)
    kept = line_sum(low(own_kept).reshape(images * KEEP, PIX), 8, 0).reshape(images, KEEP, PIX)
    patch_ids = jnp.arange(PATCHES, dtype=jnp.int32)
    keep_ids = jnp.sum(
        jnp.where(restore[:, None, :] == ranks[None, :, None], patch_ids, 0), axis=2
    )

    embedded = project(kept, w_patch) + (b_patch + positions(keep_ids, D_E))
    e_tail = jnp.where(jnp.arange(TAIL)[:, None] == 0, cls_token[None, :], 0.0)
    x0 = jnp.concatenate(
        [embedded, jnp.broadcast_to(e_tail[None], (images, TAIL, D_E))], axis=1
    )
    e_n1, e_sc1, e_inv1 = norm_forward(x0, gains[0], e_shift1)
    e_n1 = low(e_n1)
    e_qkv_bias = jnp.concatenate([e_bq, jnp.zeros_like(e_bq), e_bv])
    e_mixed = low(project(e_n1, e_qkv) + e_qkv_bias)
    e_q = e_mixed[:, :, :D_E]
    e_k = e_mixed[:, :, D_E : 2 * D_E]
    e_v = e_mixed[:, :, 2 * D_E :]
    e_o, e_lse = attend_forward(e_q, e_k, e_v, H_E)
    e_mid = x0 + project(e_o, e_out) + e_bo
    e_n2, e_sc2, e_inv2 = norm_forward(e_mid, gains[1], e_shift2)
    e_n2 = low(e_n2)
    e_hidden = project(e_n2, e_up) + e_bu
    e_gelu, e_slope = gelu_parts(e_hidden)
    e_act = low(e_gelu)
    encoded = e_mid + project_back(e_act, e_down) + e_bd
    e_n3, e_sc3, e_inv3 = norm_forward(encoded, gains[2], e_shift3)
    e_n3 = low(e_n3)
    shrunk = low(project(e_n3, w_embed) + b_embed)

    pick = low(turned[:, :, None] == ranks[None, None, :])
    is_masked = turned >= KEEP
    turned_ids = lax.rem(patch_ids + place * own_count, PATCHES)
    spread = jnp.einsum(
        "ipr,ird->ipd", pick, shrunk[:, :KEEP], preferred_element_type=jnp.float32
    )
    patch_rows = (
        jnp.where(is_masked[..., None], mask_token, spread) + positions(turned_ids, D_D)[None]
    )
    d_tail = jnp.where(
        jnp.arange(TAIL)[None, :, None] == 0,
        shrunk[:, KEEP : KEEP + 1].astype(jnp.float32),
        0.0,
    )
    y0 = jnp.concatenate([patch_rows, d_tail], axis=1)
    d_n1, d_sc1, d_inv1 = norm_forward(y0, gains[3], d_shift1)
    d_n1 = low(d_n1)

    y0_own = y0[:, :own_count]
    n1_own = d_n1[:, :own_count]
    d_q = low(project(n1_own, d_query) + d_bq)
    d_k = low(project(d_n1, d_key))
    d_v = low(project(d_n1, d_value) + d_bv)
    d_o, d_lse = attend_forward(d_q, d_k, d_v, H_D)
    own_masked = (own_restore >= KEEP).astype(jnp.float32)
    own_masked = jnp.broadcast_to(own_masked[..., None], own_masked.shape + (128,))
    d_do, d_dmid, late_grads, mid_sums, bu_sums, bh_sums = dec_middle(
        d_o,
        y0_own,
        pixels,
        own_masked,
        dec_full,
        head_low,
        stack_rows([d_bo, gains[4], d_shift2, d_bd, gains[5], d_shift3]),
        d_bu[None],
        b_head[None],
        2.0 / (PIX * masked_total),
    )
    g_d_bo, g_d_gain2, g_d_shift2, g_d_bd, g_d_gain3, g_d_shift3 = (mid_sums[i] for i in range(6))
    g_d_bu = bu_sums[0]
    g_b_head = bh_sums[0]
    loss_part = jnp.sum(bh_sums[1]) / (PIX * masked_total)
    dec_late = lax.psum_scatter(late_grads, "fsdp", scatter_dimension=0, tiled=True)
    d_dq, d_dk, d_dv = attend_backward(d_q, d_k, d_v, d_lse, d_do, d_o, H_D)
    de_part, g_d_qkv, entry_sums = dec_entry_back(
        y0, d_dq, d_dk, d_dv, d_dmid, turned[:, None, :], dec_full, stack_rows([gains[3], d_shift1])
    )
    g_mask, g_d_shift1, g_d_bq, g_d_bv, g_d_gain1 = (entry_sums[i] for i in range(5))
    dec_early = lax.psum_scatter(g_d_qkv, "fsdp", scatter_dimension=0, tiled=True)
    de_sum = line_sum(de_part, 7, 1)
    dec_late, de_sum = lax.optimization_barrier((dec_late, de_sum))
    de = jnp.concatenate(
        [
            de_sum[: images * KEEP].reshape(images, KEEP, D_D),
            jnp.pad(de_sum[images * KEEP :][:images, None], ((0, 0), (0, TAIL - 1), (0, 0))),
        ],
        axis=1,
    )

    def own_columns(tensor):
        size = tensor.shape[2] // seq_count
        return lax.dynamic_slice_in_dim(tensor, place * size, size, axis=2)

    g_embed = weight_grad(e_n3, own_columns(de))
    g_b_embed = row_sum(de)
    e_up3, g_e_gain3, g_e_shift3 = norm_backward(
        project_back(de, w_embed), e_sc3, e_inv3, gains[2]
    )
    e_up3_low = low(e_up3)
    g_e_down = weight_grad(e_up3_low, own_columns(e_act))
    g_e_bd = row_sum(e_up3)
    e_dhidden = low(project(e_up3_low, e_down) * e_slope)
    g_e_up = weight_grad(e_n2, own_columns(e_dhidden))
    g_e_bu = row_sum(e_dhidden)
    through, g_e_gain2, g_e_shift2 = norm_backward(
        project_back(e_dhidden, e_up), e_sc2, e_inv2, gains[1]
    )
    e_dmid = e_up3 + through
    e_dmid_low = low(e_dmid)
    g_e_out = weight_grad(e_o, own_columns(e_dmid_low))
    g_e_bo = row_sum(e_dmid)
    e_do = low(project_back(e_dmid_low, e_out))
    dec_early, e_do = lax.optimization_barrier((dec_early, e_do))
    dec_grad_all = lax.psum(jnp.concatenate([dec_early, dec_late], axis=1), "seq")
    e_dq, e_dk, e_dv = attend_backward(e_q, e_k, e_v, e_lse, e_do, e_o, H_E)
    g_e_qkv = [weight_grad(e_n1, own_columns(part)) for part in (e_dq, e_dk, e_dv)]
    g_e_bq = row_sum(e_dq)
    g_e_bv = row_sum(e_dv)
    e_dmixed = jnp.concatenate([e_dq, e_dk, e_dv], axis=2)
    through, g_e_gain1, g_e_shift1 = norm_backward(
        project_back(e_dmixed, e_qkv), e_sc1, e_inv1, gains[0]
    )
    dx0 = e_dmid + through
    dx0_patch = dx0[:, :KEEP]
    g_patch = weight_grad(kept, own_columns(low(dx0_patch)))
    g_b_patch = row_sum(dx0_patch)
    g_cls = jnp.sum(dx0[:, KEEP], axis=0)
    enc_grads = jnp.concatenate([g_patch] + g_e_qkv + [g_e_out, g_e_up, g_e_down], axis=1)
    embed_own = lax.psum_scatter(g_embed, "fsdp", scatter_dimension=0, tiled=True)
    embed_all = lax.all_gather(embed_own, "seq", axis=0, tiled=False)

    once = jnp.where(place == 0, 1.0, 0.0)
    enc_bias = [g_b_patch, g_cls, g_e_shift1, g_e_bq, g_e_bv, g_e_bo, g_e_shift2, g_e_bu]
    enc_bias = jnp.concatenate(enc_bias + [g_e_bd, g_e_shift3, g_b_embed]) * once
    dec_bias = [g_mask, g_d_shift1, g_d_bq, g_d_bv, g_d_bo, g_d_shift2, g_d_bu, g_d_bd]
    dec_bias = jnp.concatenate(dec_bias + [g_d_shift3, g_b_head])
    enc_gain = jnp.concatenate([g_e_gain1, g_e_gain2, g_e_gain3]) * once
    dec_gain = jnp.concatenate([g_d_gain1, g_d_gain2, g_d_gain3])
    small = jnp.concatenate([enc_gain, dec_gain, enc_bias, dec_bias, loss_part[None]])
    dec_grad_all, enc_grads = lax.optimization_barrier((dec_grad_all, enc_grads))
    enc_all, small = exchange(enc_grads, small, seq_count, 2)
    dec_grad = dec_grad_all[:, : 4 * D_D + 2 * FF_D]
    head_grad = lax.all_gather(
        dec_grad_all[:, 4 * D_D + 2 * FF_D :], "fsdp", axis=0, tiled=True
    )

    def by_column(gathered, offset, size):
        return [gathered[at, :, offset : offset + size] for at in range(seq_count)]

    quarter_e = D_E // seq_count
    quarter_f = FF_E // seq_count
    spans = []
    for at in range(5):
        spans += by_column(enc_all, at * quarter_e, quarter_e)
    spans += by_column(enc_all, 5 * quarter_e, quarter_f)
    spans += by_column(enc_all, 5 * quarter_e + quarter_f, quarter_f)
    spans = [part.astype(jnp.float32) for part in spans]
    enc_grad = jnp.concatenate(spans + [embed_all[at] for at in range(seq_count)], axis=1)
    n_gain = gain_w.shape[0]
    n_bias = bias_w.shape[0]
    gain_grad = small[:n_gain]
    bias_grad = small[n_gain : n_gain + n_bias]
    loss_total = small[n_gain + n_bias]

    enc_new = adamw(enc_w, enc_m, enc_v, enc_grad, MATRIX_RATE, MATRIX_DECAY)
    dec_new = adamw(dec_w, dec_m, dec_v, dec_grad, MATRIX_RATE, MATRIX_DECAY)
    head_new = adamw(head_w, head_m, head_v, head_grad, MATRIX_RATE, MATRIX_DECAY)
    gain_new = adamw(gain_w, gain_m, gain_v, gain_grad, SMALL_RATE, 0.0)
    bias_new = adamw(bias_w, bias_m, bias_v, bias_grad, SMALL_RATE, 0.0)
    return (loss_total,) + enc_new + dec_new + head_new + gain_new + bias_new


def solution(mesh):
    rows = P("fsdp", None)
    in_specs = (P("fsdp", "seq", None), rows) + (rows,) * 6 + (P(),) * 9
    out_specs = (P(),) + (rows,) * 6 + (P(),) * 9
    return jax.shard_map(shards, mesh=mesh, in_specs=in_specs, out_specs=out_specs, check_vma=False)
```

```python
from functools import partial

import jax
import jax.numpy as jnp
from jax import lax
from jax.experimental import pallas as pl
from jax.experimental.pallas import tpu as pltpu
from jax.sharding import PartitionSpec as P

D_E = 768
H_E = 12
FF_E = 3072
D_D = 512
H_D = 16
FF_D = 2048
PIX = 768
PATCHES = 1024
KEEP = 256
STEP = 5

NORM_EPS = 1e-06
PIXEL_EPS = 1e-06
BETA_ONE = 0.5
BETA_TWO = 0.75
MATRIX_RATE = 0.03
SMALL_RATE = 0.1
MATRIX_DECAY = 0.05
ADAM_EPS = 1e-08

TAIL = 16
E_ROWS = KEEP + TAIL
D_ROWS = PATCHES + TAIL
LOG2E = 1.4426950408889634
MASKED_SCORE = -1e30


def bias_widths():
    return [D_E] * 7 + [FF_E] + [D_E] * 2 + [D_D] * 7 + [FF_D] + [D_D] * 2 + [PIX]


def split_vector(vector, widths):
    pieces = []
    offset = 0
    for span_width in widths:
        pieces.append(vector[offset : offset + span_width])
        offset += span_width
    return pieces


def positions(index_arr, width_dim):
    halves = width_dim // 2
    frequency = 10000.0 ** (-jnp.arange(halves, dtype=jnp.float32) / halves)
    angles = (index_arr.astype(jnp.float32) + 1.0)[..., None] * frequency
    return jnp.concatenate([jnp.sin(angles), jnp.cos(angles)], axis=-1)


def norm_forward(inputs, gain_vec, shift_vec):
    centre = inputs - jnp.mean(inputs, axis=-1, keepdims=True)
    inverse = lax.rsqrt(jnp.mean(centre * centre, axis=-1, keepdims=True) + NORM_EPS)
    scaled = centre * inverse
    return (scaled * gain_vec + shift_vec, scaled, inverse)


def norm_backward(upstream, scaled, inverse, gain_vec):
    weighted = upstream * gain_vec
    inner_part = (
        weighted
        - jnp.mean(weighted, axis=-1, keepdims=True)
        - scaled * jnp.mean(weighted * scaled, axis=-1, keepdims=True)
    )
    return (
        inverse * inner_part,
        jnp.sum(upstream * scaled, axis=(0, 1)),
        jnp.sum(upstream, axis=(0, 1)),
    )


def low(tensor):
    return tensor.astype(jnp.bfloat16)


def project(row_block, weight):
    return jnp.einsum("isd,de->ise", row_block, weight, preferred_element_type=jnp.float32)


def project_back(row_block, weight):
    return jnp.einsum("ise,de->isd", row_block, weight, preferred_element_type=jnp.float32)


def weight_grad(row_block, upstream):
    return jnp.einsum("isd,ise->de", row_block, upstream, preferred_element_type=jnp.float32)


def row_sum(tensor):
    return jnp.sum(tensor.astype(jnp.float32), axis=(0, 1))


def enc_mats_of(full_rows):
    return (
        full_rows[:, D_E : 4 * D_E],
        full_rows[:, 4 * D_E : 5 * D_E],
        full_rows[:, 5 * D_E : 5 * D_E + FF_E],
        full_rows[:, 5 * D_E + FF_E : 5 * D_E + 2 * FF_E],
    )


def dot_f32(left, right, contract):
    return lax.dot_general(
        left, right, (contract, ((), ())), preferred_element_type=jnp.float32
    )


NN = ((1,), (0,))
TN = ((0,), (0,))


def pieces_of(value):
    first = low(value).astype(jnp.float32)
    rest = value - first
    second = low(rest).astype(jnp.float32)
    return first, second, rest - second


def own_span(shape, axis, head, head_dim):
    place = lax.broadcasted_iota(jnp.int32, shape, axis)
    return (place >= head * head_dim) & (place < (head + 1) * head_dim)


def live_tail(rows, scores, other):
    place = lax.broadcasted_iota(jnp.int32, (rows, scores.shape[1]), 0)
    return jnp.where(place < 1, scores, other)


def attend_forward_group(heads, head_dim, q, k, v):
    main = k.shape[0] - TAIL
    scale = head_dim ** (-0.5) * LOG2E
    q_t = q.astype(jnp.float32).T * scale
    q_high = low(q_t)
    q_rest = low(q_t - q_high.astype(jnp.float32))
    k_main = jnp.concatenate([k[:main], k[:main]], axis=1)
    k_tail = jnp.concatenate([k[main:], k[main:]], axis=1)
    v_main = low(v[:main].astype(jnp.float32).T)
    v_tail = v[main:]
    ones = jnp.ones((TAIL, main), jnp.bfloat16)

    def scores_of(head):
        own = own_span(q_t.shape, 0, head, head_dim)
        none = jnp.zeros_like(q_high)
        q_h = jnp.concatenate([jnp.where(own, q_high, none), jnp.where(own, q_rest, none)], axis=0)
        return dot_f32(k_main, q_h, NN), live_tail(TAIL, dot_f32(k_tail, q_h, NN), MASKED_SCORE)

    outs, sums = [], []
    following = scores_of(0)
    for head in range(heads):
        span = slice(head * head_dim, (head + 1) * head_dim)
        s_main, s_tail = following
        if head + 1 < heads:
            following = scores_of(head + 1)
        top = jnp.maximum(
            jnp.max(s_main, axis=0, keepdims=True), jnp.max(s_tail, axis=0, keepdims=True)
        )
        p_main = low(jnp.exp2(s_main - top))
        p_tail = low(jnp.exp2(s_tail - top))
        o_t = dot_f32(jnp.concatenate([v_main[span], ones], axis=0), p_main, NN)
        total = o_t[head_dim : head_dim + 1] + jnp.sum(
            p_tail.astype(jnp.float32), axis=0, keepdims=True
        )
        o_t = o_t[:head_dim] + dot_f32(v_tail, p_tail, TN)[span]
        outs.append(o_t * (1.0 / total))
        sums.append(top + jnp.log2(total))
    return low(jnp.concatenate(outs, axis=0).T), sums


def attend_forward_kernel(heads, head_dim, q_ref, k_ref, v_ref, o_ref, lse_ref):
    o_ref[0], sums = attend_forward_group(heads, head_dim, q_ref[0], k_ref[0], v_ref[0])
    for head in range(heads):
        lse_ref[0, 0, head : head + 1, :] = sums[head]


def attend_backward_group(heads, head_dim, q, k, v, sums, do, o):
    main = k.shape[0] - TAIL
    rows = q.shape[0]
    unit = head_dim ** (-0.5)
    q_t = q.astype(jnp.float32).T * (unit * LOG2E)
    q_high = low(q_t).astype(jnp.float32)
    q_rest = q_t - q_high
    do_t = do.astype(jnp.float32).T
    inner_t = do_t * o.astype(jnp.float32).T
    place = lax.broadcasted_iota(jnp.int32, q_t.shape, 0)

    def with_row(block, offset, value):
        for at, part in enumerate(pieces_of(value)):
            block = jnp.where(place == offset + at, part, block)
        return block

    score_sides, value_sides = [], []
    for head in range(heads):
        own = own_span(q_t.shape, 0, head, head_dim)
        span = slice(head * head_dim, (head + 1) * head_dim)
        other = ((head + 1) % heads) * head_dim
        lse = sums[head]
        inner = jnp.sum(inner_t[span], axis=0, keepdims=True)
        rest = with_row(jnp.where(own, q_rest, 0.0), other, -lse)
        score_sides.append(low(jnp.concatenate([jnp.where(own, q_high, 0.0), rest], axis=0)))
        last = with_row(jnp.zeros_like(do_t), 0, -inner)
        value_sides.append(low(jnp.concatenate([jnp.where(own, do_t, 0.0), last], axis=0)))
    zero = jnp.zeros_like(q)
    q_sides = [jnp.where(own_span(q.shape, 1, h, head_dim), q, zero) for h in range(heads)]
    do_sides = [jnp.where(own_span(q.shape, 1, h, head_dim), do, zero) for h in range(heads)]
    stacked = rows % 128 == 0
    if stacked:
        q_sides = jnp.concatenate(q_sides, axis=0)
        do_sides = jnp.concatenate(do_sides, axis=0)

    def sum_heads(parts, sides):
        if stacked:
            return dot_f32(jnp.concatenate(parts, axis=1), sides, NN)
        terms = [dot_f32(part, side, NN) for part, side in zip(parts, sides)]
        return sum(terms[1:], terms[0])

    k_main = k[:main]
    k_tail = k[main:]
    k_main_t = low(k_main.astype(jnp.float32).T)

    def with_ones(block):
        return jnp.concatenate([block, jnp.ones_like(block)], axis=1)

    def beside_own(block, head):
        own = jnp.where(own_span(block.shape, 1, head, head_dim), block, jnp.ones_like(block))
        return jnp.concatenate([block, own], axis=1)

    v_main = with_ones(v[:main])
    v_tail = with_ones(v[main:])
    dq_parts, p_mains, s_mains, p_tails, s_tails = [], [], [], [], []
    for head in range(heads):
        span = slice(head * head_dim, (head + 1) * head_dim)
        p = jnp.exp2(dot_f32(beside_own(k_main, head), score_sides[head], NN))
        s = low(p * dot_f32(v_main, value_sides[head], NN))
        p_mains.append(low(p))
        s_mains.append(s)
        p = jnp.exp2(dot_f32(beside_own(k_tail, head), score_sides[head], NN))
        p = live_tail(TAIL, p, 0.0)
        s_tail = low(p * dot_f32(v_tail, value_sides[head], NN))
        p_tails.append(low(p))
        s_tails.append(s_tail)
        dq_parts.append(dot_f32(k_main_t[span], s, NN) + dot_f32(k_tail, s_tail, TN)[span])
    dk = [low(sum_heads(part, q_sides) * unit) for part in (s_mains, s_tails)]
    dv = [low(sum_heads(part, do_sides)) for part in (p_mains, p_tails)]
    dq = low(jnp.concatenate(dq_parts, axis=0).T * unit)
    return dq, dk, dv


def attend_backward_kernel(
    heads, head_dim, q_ref, k_ref, v_ref, lse_ref, do_ref, o_ref, dq_ref, dk_ref, dv_ref
):
    main = k_ref.shape[1] - TAIL
    sums = [lse_ref[0, 0, head : head + 1, :] for head in range(heads)]
    dq_ref[0], dk, dv = attend_backward_group(
        heads, head_dim, q_ref[0], k_ref[0], v_ref[0], sums, do_ref[0], o_ref[0]
    )
    dk_ref[0, :main], dk_ref[0, main:] = dk
    dv_ref[0, :main], dv_ref[0, main:] = dv


VMEM_LIMIT = 32 * 1024 * 1024
KERNEL_LIMIT = 58 * 1024 * 1024


def attend_specs(q_rows, k_rows, heads):
    return (
        pl.BlockSpec((1, q_rows, 128), lambda i, g: (i, 0, g)),
        pl.BlockSpec((1, k_rows, 128), lambda i, g: (i, 0, g)),
        pl.BlockSpec((1, 1, heads, q_rows), lambda i, g: (i, g, 0, 0)),
    )


def attend_forward(queries, key_rows, value_rows, head_count):
    images, q_rows, width = queries.shape
    k_rows = key_rows.shape[1]
    head_dim = width // head_count
    heads = 128 // head_dim
    groups = width // 128
    q_spec, k_spec, l_spec = attend_specs(q_rows, k_rows, heads)
    return pl.pallas_call(
        partial(attend_forward_kernel, heads, head_dim),
        grid=(images, groups),
        in_specs=[q_spec, k_spec, k_spec],
        out_specs=[q_spec, l_spec],
        out_shape=[
            jax.ShapeDtypeStruct((images, q_rows, width), jnp.bfloat16),
            jax.ShapeDtypeStruct((images, groups, heads, q_rows), jnp.float32),
        ],
        compiler_params=pltpu.CompilerParams(vmem_limit_bytes=VMEM_LIMIT),
        cost_estimate=pl.CostEstimate(
            flops=16 * images * q_rows * k_rows * width,
            bytes_accessed=4 * images * (q_rows + k_rows) * width,
            transcendentals=images * head_count * q_rows * k_rows,
        ),
    )(queries, key_rows, value_rows)


def attend_backward(queries, key_rows, value_rows, logsum, upstream, attended, head_count):
    images, q_rows, width = queries.shape
    k_rows = key_rows.shape[1]
    head_dim = width // head_count
    heads = 128 // head_dim
    groups = width // 128
    q_spec, k_spec, l_spec = attend_specs(q_rows, k_rows, heads)
    return pl.pallas_call(
        partial(attend_backward_kernel, heads, head_dim),
        grid=(images, groups),
        in_specs=[q_spec, k_spec, k_spec, l_spec, q_spec, q_spec],
        out_specs=[q_spec, k_spec, k_spec],
        out_shape=[
            jax.ShapeDtypeStruct((images, q_rows, width), jnp.bfloat16),
            jax.ShapeDtypeStruct((images, k_rows, width), jnp.bfloat16),
            jax.ShapeDtypeStruct((images, k_rows, width), jnp.bfloat16),
        ],
        compiler_params=pltpu.CompilerParams(vmem_limit_bytes=VMEM_LIMIT),
        cost_estimate=pl.CostEstimate(
            flops=40 * images * q_rows * k_rows * width,
            bytes_accessed=8 * images * (q_rows + k_rows) * width,
            transcendentals=images * head_count * q_rows * k_rows,
        ),
    )(queries, key_rows, value_rows, logsum, upstream, attended)


MESH = pl.DeviceIdType.MESH


def line_sum_kernel(
    chunks, lines, x_ref, o_ref, from_left, from_right, to_left, to_right, send_sem, recv_sem
):
    count = lax.axis_size("seq")
    place = lax.axis_index("seq")
    has_left = place > 0
    has_right = place < count - 1
    rows = x_ref.shape[0] // chunks
    barrier = pltpu.get_barrier_semaphore()

    def greet(to):
        pl.semaphore_signal(barrier, inc=1, device_id={"seq": to}, device_id_type=MESH)

    pl.when(has_left)(lambda: greet(place - 1))
    pl.when(has_right)(lambda: greet(place + 1))
    peers = jnp.where(has_left, 1, 0) + jnp.where(has_right, 1, 0)
    pl.semaphore_wait(barrier, peers)

    def copy(way, at):
        span = pl.ds(pl.multiple_of(at * rows, 16), rows)
        source, target = ((to_right, from_left), (to_left, from_right))[way]
        return pltpu.make_async_remote_copy(
            src_ref=source.at[span],
            dst_ref=target.at[span],
            send_sem=send_sem.at[way, at],
            recv_sem=recv_sem.at[way, at],
            device_id={"seq": place + 1 if way == 0 else place - 1},
            device_id_type=MESH,
        )

    def end_copy(way, at):
        span = pl.ds(at * rows, rows)
        return pltpu.make_async_remote_copy(
            src_ref=x_ref.at[span],
            dst_ref=(from_left, from_right)[way].at[span],
            send_sem=send_sem.at[way, at],
            recv_sem=recv_sem.at[way, at],
            device_id={"seq": place + 1 if way == 0 else place - 1},
            device_id_type=MESH,
        )

    for way, is_end in ((0, jnp.logical_not(has_left)), (1, jnp.logical_not(has_right))):

        @pl.when(is_end)
        def _():
            for at in range(chunks):
                if at >= 2:
                    end_copy(way, at - 2).wait_send()
                end_copy(way, at).start()
            for at in range(chunks - 2, chunks):
                end_copy(way, at).wait_send()

    def span_of(at):
        return pl.ds(pl.multiple_of(at * rows, 16), rows)

    for step in range(chunks + lines - 1):
        from_first = step - place
        from_last = step - (count - 1 - place)

        @pl.when(has_left & (from_first >= 0) & (from_first < chunks))
        def _():
            copy(0, from_first).wait_recv()

            @pl.when(has_right)
            def _():
                span = span_of(from_first)
                to_right[span] = x_ref[span] + from_left[span]
                copy(0, from_first).start()

        @pl.when(has_right & (from_last >= 0) & (from_last < chunks))
        def _():
            copy(1, from_last).wait_recv()

            @pl.when(has_left)
            def _():
                span = span_of(from_last)
                to_left[span] = x_ref[span] + from_right[span]
                copy(1, from_last).start()

    @pl.when(jnp.logical_not(has_left))
    def _():
        o_ref[...] = x_ref[...] + from_right[...]

    @pl.when(jnp.logical_not(has_right))
    def _():
        o_ref[...] = x_ref[...] + from_left[...]

    @pl.when(has_left & has_right)
    def _():
        o_ref[...] = (x_ref[...] + from_left[...]) + from_right[...]
        for at in range(chunks):
            copy(0, at).wait_send()
            copy(1, at).wait_send()


def line_sum(block, chunks, collective_id):
    shape = jax.ShapeDtypeStruct(block.shape, block.dtype)
    buffer = pltpu.VMEM(block.shape, block.dtype)
    return pl.pallas_call(
        partial(line_sum_kernel, chunks, lax.axis_size("seq")),
        out_shape=shape,
        in_specs=[pl.BlockSpec(memory_space=pltpu.VMEM)],
        out_specs=pl.BlockSpec(memory_space=pltpu.VMEM),
        scratch_shapes=[buffer] * 4
        + [pltpu.SemaphoreType.DMA((2, chunks)), pltpu.SemaphoreType.DMA((2, chunks))],
        compiler_params=pltpu.CompilerParams(
            collective_id=collective_id, has_side_effects=True, vmem_limit_bytes=VMEM_LIMIT
        ),
        cost_estimate=pl.CostEstimate(
            flops=0, bytes_accessed=100 * block.size, transcendentals=0
        ),
    )(block)


SMALL_BLOCK = (8, 384)
PLANE = 8


def exchange_kernel(
    table,
    extra,
    g_early,
    g_late,
    small_ref,
    out_early,
    out_late,
    small_out,
    pair_early,
    pair_late,
    send_early,
    send_late,
    recv_early,
    recv_late,
    small_in,
    small_line,
    pair_sems,
    plane_sems,
    line_sems,
    small_plane_sems,
    small_line_sems,
    small_out_sems,
):
    own = lax.axis_index("fsdp")
    place = lax.axis_index("seq")
    line = lax.axis_size("seq")
    core = lax.rem(own, 2)
    chip = lax.div(own, 2)
    partner = own + 1 - 2 * core
    grads = (g_early, g_late)
    pair_ins = (pair_early, pair_late)
    sends = (send_early, send_late)
    recvs = (recv_early, recv_late)
    outs = (out_early, out_late)
    block = g_early.shape[0] // PLANE
    order = range(len(table))

    def plane_peer(step):
        return lax.rem(own + step, PLANE)

    def line_peer(step):
        return lax.rem(place + step, line)

    barrier = pltpu.get_barrier_semaphore()
    for step in range(1, PLANE):
        pl.semaphore_signal(
            barrier, inc=1, device_id={"fsdp": plane_peer(step)}, device_id_type=MESH
        )
    for step in range(1, line):
        pl.semaphore_signal(
            barrier, inc=1, device_id={"seq": line_peer(step)}, device_id_type=MESH
        )
    pl.semaphore_wait(barrier, PLANE - 1 + line - 1)

    def send(source, target, sems, at, device):
        return pltpu.make_async_remote_copy(
            src_ref=source,
            dst_ref=target,
            send_sem=sems.at[(0,) + at],
            recv_sem=sems.at[(1,) + at],
            device_id=device,
            device_id_type=MESH,
        )

    def span_of(at):
        return pl.ds(table[at][1], table[at][2])

    def owned_rows(owner, at):
        start, rows = table[at][1:]
        return pl.ds(pl.multiple_of(owner * block + start, 16), rows)

    def pair_copy(other, at):
        part = table[at][0]
        target = lax.rem(chip + other, 4)
        return send(
            grads[part].at[owned_rows(2 * target + 1 - core, at)],
            pair_ins[part].at[other, span_of(at)],
            pair_sems,
            (other, at),
            {"fsdp": partner},
        )

    def plane_copy(other, at):
        part = table[at][0]
        target = lax.rem(chip + other, 4)
        return send(
            sends[part].at[other - 1, span_of(at)],
            recvs[part].at[other - 1, span_of(at)],
            plane_sems,
            (other - 1, at),
            {"fsdp": 2 * target + core},
        )

    def line_copy(step, at):
        part = outs[table[at][0]].at[place, span_of(at)]
        return send(part, part, line_sems, (step - 1, at), {"seq": line_peer(step)})

    def small_plane_copy(step):
        return send(
            small_ref.at[plane_peer(step)],
            small_in.at[step - 1],
            small_plane_sems,
            (step - 1,),
            {"fsdp": plane_peer(step)},
        )

    def small_line_copy(step):
        part = small_line.at[place]
        return send(part, part, small_line_sems, (step - 1,), {"seq": line_peer(step)})

    def small_out_copy(step):
        part = small_out.at[own]
        return send(part, part, small_out_sems, (step - 1,), {"fsdp": plane_peer(step)})

    for at in order:
        for other in (1, 2, 3, 0):
            pair_copy(other, at).start()
        if at == 0:
            for step in range(1, PLANE):
                small_plane_copy(step).start()
    for at in order:
        part = table[at][0]
        for other in (1, 2, 3, 0):
            pair_copy(other, at).wait_recv()
            if other:
                target = lax.rem(chip + other, 4)
                mine = grads[part][owned_rows(2 * target + core, at)]
                sends[part][other - 1, span_of(at)] = low(mine + pair_ins[part][other, span_of(at)])
                plane_copy(other, at).start()
    for step in range(1, PLANE):
        small_plane_copy(step).wait_recv()
    total = small_ref[own]
    for step in range(1, PLANE):
        total = total + small_in[step - 1]
    small_line[place] = total
    for step in range(1, line):
        small_line_copy(step).start()
    for at in order:
        part = table[at][0]
        total = grads[part][owned_rows(own, at)] + pair_ins[part][0, span_of(at)]
        for other in (1, 2, 3):
            plane_copy(other, at).wait_recv()
            total = total + recvs[part][other - 1, span_of(at)].astype(jnp.float32)
        rounded = low(total)
        if part == 0:
            rest = total[:, -extra:] - rounded[:, -extra:].astype(jnp.float32)
            rounded = jnp.concatenate([rounded, low(rest)], axis=1)
        outs[part][place, span_of(at)] = rounded
        for step in range(1, line):
            line_copy(step, at).start()
    for step in range(1, line):
        small_line_copy(step).wait_recv()
    total = small_line[0]
    for at in range(1, small_line.shape[0]):
        total = total + small_line[at]
    small_out[own] = total
    for step in range(1, PLANE):
        small_out_copy(step).start()
    for step in range(1, PLANE):
        small_out_copy(step).wait()
        small_plane_copy(step).wait_send()
    for step in range(1, line):
        small_line_copy(step).wait_send()
        for at in order:
            line_copy(step, at).wait()
    for at in order:
        for other in range(4):
            pair_copy(other, at).wait_send()
            if other:
                plane_copy(other, at).wait_send()


def exchange(early, late, small, line, extra, collective_id):
    plane = lax.axis_size("fsdp")
    total = early.shape[0]
    if plane != PLANE or total % (PLANE * 48):
        results = []
        for part, rest in ((early, extra), (late, 0)):
            own = lax.psum_scatter(part, "fsdp", scatter_dimension=0, tiled=True)
            rounded = low(own)
            if rest:
                left = own[:, -rest:] - rounded[:, -rest:].astype(jnp.float32)
                rounded = jnp.concatenate([rounded, low(left)], axis=1)
            results.append(lax.all_gather(rounded, "seq", axis=0, tiled=False))
        return results[0], results[1], lax.psum(small, ("fsdp", "seq"))
    block = total // PLANE
    third = block // 3
    table = tuple((0, at * third, third) for at in range(3)) + ((1, 0, block),)
    widths = (early.shape[1], late.shape[1])
    padded = PLANE * SMALL_BLOCK[0] * SMALL_BLOCK[1]
    blocks = jnp.pad(small, (0, padded - small.shape[0])).reshape((PLANE,) + SMALL_BLOCK)
    dma = pltpu.SemaphoreType.DMA
    low_type, f32 = jnp.bfloat16, jnp.float32
    first, second, summed = pl.pallas_call(
        partial(exchange_kernel, table, extra),
        out_shape=[
            jax.ShapeDtypeStruct((line, block, widths[0] + extra), low_type),
            jax.ShapeDtypeStruct((line, block, widths[1]), low_type),
            jax.ShapeDtypeStruct(blocks.shape, f32),
        ],
        in_specs=[pl.BlockSpec(memory_space=pltpu.VMEM)] * 3,
        out_specs=[pl.BlockSpec(memory_space=pltpu.VMEM)] * 3,
        scratch_shapes=[pltpu.VMEM((4, block, width), f32) for width in widths]
        + [pltpu.VMEM((3, block, width), low_type) for width in widths * 2]
        + [
            pltpu.VMEM((PLANE - 1,) + SMALL_BLOCK, f32),
            pltpu.VMEM((line,) + SMALL_BLOCK, f32),
            dma((2, 4, len(table))),
            dma((2, 3, len(table))),
            dma((2, line - 1, len(table))),
            dma((2, PLANE - 1)),
            dma((2, line - 1)),
            dma((2, PLANE - 1)),
        ],
        compiler_params=pltpu.CompilerParams(
            collective_id=collective_id, has_side_effects=True, vmem_limit_bytes=VMEM_LIMIT
        ),
        cost_estimate=pl.CostEstimate(
            flops=0, bytes_accessed=200 * 1024 * 1024, transcendentals=0
        ),
    )(early, late, blocks)
    return first, second, summed.reshape(-1)


def gelu_parts(hidden):
    cdf = 0.5 * (1.0 + lax.erf(hidden * (2.0**-0.5)))
    density = jnp.exp(-0.5 * hidden * hidden) * (0.3989422804014327)
    return hidden * cdf, cdf + hidden * density


NT = ((1,), (1,))


def norm_rows(rows):
    centre = rows - jnp.mean(rows, axis=-1, keepdims=True)
    inverse = lax.rsqrt(jnp.mean(centre * centre, axis=-1, keepdims=True) + NORM_EPS)
    return centre * inverse, inverse


def norm_rows_back(upstream, scaled, inverse, gain):
    weighted = upstream * gain
    inner = (
        weighted
        - jnp.mean(weighted, axis=-1, keepdims=True)
        - scaled * jnp.mean(weighted * scaled, axis=-1, keepdims=True)
    )
    return inverse * inner, column_sum(upstream * scaled), column_sum(upstream)


def column_sum(rows):
    return jnp.sum(rows, axis=0, keepdims=True)


def clear_first(refs):
    @pl.when(pl.program_id(0) == 0)
    def _():
        for ref in refs:
            ref[...] = jnp.zeros_like(ref)


def dec_middle_kernel(
    grad_scale,
    o_ref,
    y_ref,
    pixel_ref,
    masked_ref,
    out_w,
    up_w,
    down_w,
    head_w,
    vec_ref,
    bu_ref,
    bh_ref,
    do_ref,
    dmid_ref,
    grad_ref,
    vec_grad,
    bu_grad,
    bh_grad,
    slope_ref,
    act_ref,
):
    clear_first((grad_ref, vec_grad, bu_grad, bh_grad))
    bo, gain2, shift2, bd, gain3, shift3 = (vec_ref[i : i + 1, :] for i in range(6))
    attended = o_ref[0]
    middle = y_ref[0] + dot_f32(attended, out_w[...], NN) + bo
    scaled2, inverse2 = norm_rows(middle)
    second = low(scaled2 * gain2 + shift2)
    size = 512
    decoded = middle + bd
    for at in range(0, FF_D, size):
        span = slice(at, at + size)
        value, slope = gelu_parts(dot_f32(second, up_w[:, span], NN) + bu_ref[:, span])
        slope_ref[:, span] = slope
        act_ref[:, span] = low(value)
        decoded = decoded + dot_f32(act_ref[:, span], down_w[:, span], NT)
    scaled3, inverse3 = norm_rows(decoded)
    third = low(scaled3 * gain3 + shift3)
    predicted = dot_f32(third, head_w[...], NN) + bh_ref[...]
    pixel = pixel_ref[0].astype(jnp.float32)
    centre = pixel - jnp.mean(pixel, axis=-1, keepdims=True)
    target = centre * lax.rsqrt(
        jnp.sum(centre * centre, axis=-1, keepdims=True) / (PIX - 1) + PIXEL_EPS
    )
    masked = masked_ref[0][:, :1]
    error = (predicted - target) * masked
    pred_grad = error * grad_scale
    pred_low = low(pred_grad)
    bh_grad[0:1, :] += column_sum(pred_grad)
    bh_grad[1:2, :] += column_sum(error * error)
    o_span, u_span = D_D, D_D + FF_D
    h_span = D_D + 2 * FF_D
    grad_ref[:, h_span:] += dot_f32(third, pred_low, TN)
    up3, g_gain3, g_shift3 = norm_rows_back(
        dot_f32(pred_low, head_w[...], NT), scaled3, inverse3, gain3
    )
    up3_low = low(up3)
    back = jnp.zeros_like(up3)
    for at in range(0, FF_D, size):
        span = slice(at, at + size)
        hidden_grad = low(dot_f32(up3_low, down_w[:, span], NN) * slope_ref[:, span])
        grad_ref[:, u_span + at : u_span + at + size] += dot_f32(up3_low, act_ref[:, span], TN)
        grad_ref[:, o_span + at : o_span + at + size] += dot_f32(second, hidden_grad, TN)
        bu_grad[0:1, span] += column_sum(hidden_grad.astype(jnp.float32))
        back = back + dot_f32(hidden_grad, up_w[:, span], NT)
    through, g_gain2, g_shift2 = norm_rows_back(back, scaled2, inverse2, gain2)
    middle_grad = up3 + through
    middle_low = low(middle_grad)
    dmid_ref[0] = middle_grad
    grad_ref[:, :o_span] += dot_f32(attended, middle_low, TN)
    do_ref[0] = low(dot_f32(middle_low, out_w[...], NT))
    sums = (column_sum(middle_grad), g_gain2, g_shift2, column_sum(up3), g_gain3, g_shift3)
    for at, part in enumerate(sums):
        vec_grad[at : at + 1, :] += part


def whole(shape):
    return pl.BlockSpec(shape, lambda i: (0,) * len(shape), pipeline_mode=pl.Buffered(1))


def columns(rows, width, at):
    return pl.BlockSpec((rows, width), lambda i: (0, at), pipeline_mode=pl.Buffered(1))


def per_image(rows, width):
    return pl.BlockSpec((1, rows, width), lambda i: (i, 0, 0))


def dec_middle(attended, y_own, pixels, masked, dec_full, head_low, vectors, bu, bh, grad_scale):
    images, rows, _ = attended.shape
    f32 = jnp.float32
    return pl.pallas_call(
        partial(dec_middle_kernel, grad_scale),
        grid=(images,),
        in_specs=[
            per_image(rows, D_D),
            per_image(rows, D_D),
            per_image(rows, PIX),
            per_image(rows, 128),
            columns(D_D, D_D, 3),
            columns(D_D, FF_D, 1),
            columns(D_D, FF_D, 2),
            whole((D_D, PIX)),
            whole((8, D_D)),
            whole((1, FF_D)),
            whole((1, PIX)),
        ],
        out_specs=[
            per_image(rows, D_D),
            per_image(rows, D_D),
            whole((D_D, D_D + 2 * FF_D + PIX)),
            whole((8, D_D)),
            whole((8, FF_D)),
            whole((8, PIX)),
        ],
        out_shape=[
            jax.ShapeDtypeStruct((images, rows, D_D), jnp.bfloat16),
            jax.ShapeDtypeStruct((images, rows, D_D), f32),
            jax.ShapeDtypeStruct((D_D, D_D + 2 * FF_D + PIX), f32),
            jax.ShapeDtypeStruct((8, D_D), f32),
            jax.ShapeDtypeStruct((8, FF_D), f32),
            jax.ShapeDtypeStruct((8, PIX), f32),
        ],
        scratch_shapes=[pltpu.VMEM((rows, FF_D), f32), pltpu.VMEM((rows, FF_D), jnp.bfloat16)],
        compiler_params=pltpu.CompilerParams(vmem_limit_bytes=44 * 1024 * 1024),
        cost_estimate=pl.CostEstimate(
            flops=12 * images * rows * D_D * (D_D + 2 * FF_D + PIX),
            bytes_accessed=30 * 1024 * 1024,
            transcendentals=2 * images * rows * FF_D,
        ),
    )(
        attended, y_own, pixels, masked, dec_full, dec_full, dec_full, head_low, vectors, bu, bh
    )


def dec_entry_back_kernel(
    y_ref,
    dq_ref,
    dk_ref,
    dv_ref,
    dmid_ref,
    rank_ref,
    q_w,
    k_w,
    v_w,
    vec_ref,
    de_ref,
    grad_ref,
    vec_grad,
    cls_ref,
):
    image = pl.program_id(0)
    clear_first((grad_ref, vec_grad, cls_ref))
    gain, shift = vec_ref[0:1, :], vec_ref[1:2, :]
    scaled, inverse = norm_rows(y_ref[0])
    normed = low(scaled * gain + shift)
    dq, dk, dv = dq_ref[0], dk_ref[0], dv_ref[0]
    own = dq.shape[0]
    grad_ref[:, :D_D] += dot_f32(normed[:own], dq, TN)
    grad_ref[:, D_D : 2 * D_D] += dot_f32(normed, dk, TN)
    grad_ref[:, 2 * D_D :] += dot_f32(normed, dv, TN)
    up = dot_f32(dk, k_w[...], NT) + dot_f32(dv, v_w[...], NT)
    up = jnp.concatenate([up[:own] + dot_f32(dq, q_w[...], NT), up[own:]], axis=0)
    back, g_gain, g_shift = norm_rows_back(up, scaled, inverse, gain)
    back = jnp.concatenate([back[:own] + dmid_ref[0], back[own:]], axis=0)
    patches = back[:PATCHES]
    high = low(patches)
    rest = low(patches - high.astype(jnp.float32))
    ranks = rank_ref[0]
    at = lax.broadcasted_iota(jnp.int32, (KEEP, PATCHES), 0)
    pick = low(jnp.where(at == ranks, 1.0, 0.0))
    hidden = low(jnp.where(jnp.broadcast_to(ranks, (16, PATCHES)) >= KEEP, 1.0, 0.0))
    de_ref[pl.ds(pl.multiple_of(image * KEEP, KEEP), KEEP)] = low(dot_f32(pick, high, NN))
    g_mask = dot_f32(hidden, high, NN) + dot_f32(hidden, rest, NN)
    cls_ref[pl.ds(image, 1), :] = back[PATCHES : PATCHES + 1]
    sums = (
        g_mask[0:1],
        g_shift,
        column_sum(dq.astype(jnp.float32)),
        column_sum(dv.astype(jnp.float32)),
        g_gain,
    )
    for at, part in enumerate(sums):
        vec_grad[at : at + 1, :] += part

    @pl.when(image == pl.num_programs(0) - 1)
    def _():
        de_ref[de_ref.shape[0] - TAIL :] = low(cls_ref[...])


def dec_entry_back(y0, dq, dk, dv, dmid, ranks, dec_full, vectors):
    images, rows, _ = y0.shape
    own = dq.shape[1]
    f32 = jnp.float32
    return pl.pallas_call(
        dec_entry_back_kernel,
        grid=(images,),
        in_specs=[
            per_image(rows, D_D),
            per_image(own, D_D),
            per_image(rows, D_D),
            per_image(rows, D_D),
            per_image(own, D_D),
            per_image(1, PATCHES),
            columns(D_D, D_D, 0),
            columns(D_D, D_D, 1),
            columns(D_D, D_D, 2),
            whole((8, D_D)),
        ],
        out_specs=[whole((images * KEEP + TAIL, D_D)), whole((D_D, 3 * D_D)), whole((8, D_D))],
        out_shape=[
            jax.ShapeDtypeStruct((images * KEEP + TAIL, D_D), jnp.bfloat16),
            jax.ShapeDtypeStruct((D_D, 3 * D_D), f32),
            jax.ShapeDtypeStruct((8, D_D), f32),
        ],
        scratch_shapes=[pltpu.VMEM((TAIL, D_D), f32)],
        compiler_params=pltpu.CompilerParams(vmem_limit_bytes=44 * 1024 * 1024),
        cost_estimate=pl.CostEstimate(
            flops=12 * images * rows * D_D * D_D * 2,
            bytes_accessed=24 * 1024 * 1024,
            transcendentals=0,
        ),
    )(y0, dq, dk, dv, dmid, ranks, dec_full, dec_full, dec_full, vectors)


E_HEADS = 128 * H_E // D_E
E_DIM = D_E // H_E
E_OUT = 4 * D_E
E_UP = 5 * D_E
E_DOWN = E_UP + FF_E
E_EMBED = E_DOWN + FF_E
SIZE = 768


def tail_rows(first):
    at = lax.broadcasted_iota(jnp.int32, (TAIL, first.shape[1]), 0)
    return jnp.where(at == 0, first, 0.0)


def encoder_kernel(
    kept_ref,
    place_ref,
    w_ref,
    vec_ref,
    bu_ref,
    be_ref,
    x_ref,
    mid_ref,
    enc_ref,
    qkv_ref,
    lse_ref,
    o_ref,
    slope_ref,
    act_ref,
    e_ref,
):
    (gain1, gain2, gain3, cls, shift1, bq, bv, bo, shift2, bd, shift3) = (
        vec_ref[i : i + 1, :] for i in range(11)
    )
    rows = dot_f32(kept_ref[0], w_ref[:, :D_E], NN) + place_ref[0]
    x_ref[0] = jnp.concatenate([rows, tail_rows(cls)], axis=0)
    scaled, _ = norm_rows(x_ref[0])
    normed = low(scaled * gain1 + shift1)
    for at, bias in enumerate((bq, None, bv)):
        value = dot_f32(normed, w_ref[:, (at + 1) * D_E : (at + 2) * D_E], NN)
        qkv_ref[0, :, at * D_E : (at + 1) * D_E] = low(value if bias is None else value + bias)
    for group in range(D_E // 128):
        parts = [
            qkv_ref[0, :, at * D_E + group * 128 : at * D_E + (group + 1) * 128] for at in range(3)
        ]
        out, sums = attend_forward_group(E_HEADS, E_DIM, *parts)
        o_ref[0, :, group * 128 : (group + 1) * 128] = out
        for head in range(E_HEADS):
            at = group * E_HEADS + head
            lse_ref[0, at : at + 1, :] = sums[head]
    middle = x_ref[0] + dot_f32(o_ref[0], w_ref[:, E_OUT:E_UP], NN) + bo
    mid_ref[0] = middle
    scaled, _ = norm_rows(middle)
    second = low(scaled * gain2 + shift2)
    encoded = middle + bd
    for at in range(0, FF_E, SIZE):
        span = slice(at, at + SIZE)
        hidden = dot_f32(second, w_ref[:, E_UP + at : E_UP + at + SIZE], NN) + bu_ref[:, span]
        value, slope = gelu_parts(hidden)
        slope_ref[0, :, span] = slope
        act_ref[0, :, span] = low(value)
        encoded = encoded + dot_f32(
            act_ref[0, :, span], w_ref[:, E_DOWN + at : E_DOWN + at + SIZE], NT
        )
    enc_ref[0] = encoded
    scaled, _ = norm_rows(encoded)
    third = low(scaled * gain3 + shift3)
    e_ref[0] = low(dot_f32(third, w_ref[:, E_EMBED:], NN) + be_ref[...])


def encoder(kept, placed, enc_full, vectors, bu, be):
    images = kept.shape[0]
    f32, low_type = jnp.float32, jnp.bfloat16
    shapes = [
        ((E_ROWS, D_E), f32),
        ((E_ROWS, D_E), f32),
        ((E_ROWS, D_E), f32),
        ((E_ROWS, 3 * D_E), low_type),
        ((H_E, E_ROWS), f32),
        ((E_ROWS, D_E), low_type),
        ((E_ROWS, FF_E), f32),
        ((E_ROWS, FF_E), low_type),
        ((E_ROWS, D_D), low_type),
    ]
    return pl.pallas_call(
        encoder_kernel,
        grid=(images,),
        in_specs=[
            per_image(KEEP, D_E),
            per_image(KEEP, D_E),
            whole(enc_full.shape),
            whole((16, D_E)),
            whole((1, FF_E)),
            whole((1, D_D)),
        ],
        out_specs=[per_image(*shape) for shape, _ in shapes],
        out_shape=[jax.ShapeDtypeStruct((images,) + shape, kind) for shape, kind in shapes],
        compiler_params=pltpu.CompilerParams(vmem_limit_bytes=KERNEL_LIMIT),
        cost_estimate=pl.CostEstimate(
            flops=2 * images * E_ROWS * enc_full.size,
            bytes_accessed=40 * 1024 * 1024,
            transcendentals=2 * images * E_ROWS * FF_E,
        ),
    )(kept, placed, enc_full, vectors, bu, be)


def turn_quarter(value, place):
    width = value.shape[1]
    quarter = width // 4
    turned = pltpu.roll(value, lax.rem(width - quarter * place, width), axis=1)
    return low(turned[:, :quarter])


def encoder_back_kernel(
    place_ref,
    de_ref,
    cls_ref,
    mid_ref,
    enc_ref,
    o_ref,
    slope_ref,
    act_ref,
    w_ref,
    vec_ref,
    do_ref,
    dmid_ref,
    grad_ref,
    vec_grad,
    bu_grad,
    be_grad,
    de_all,
    hidden_all,
):
    image = pl.program_id(0)
    place = place_ref[0]
    clear_first((grad_ref, vec_grad, bu_grad, be_grad))
    gain2, gain3, shift2, shift3 = (vec_ref[i : i + 1, :] for i in range(4))
    at = lax.broadcasted_iota(jnp.int32, (TAIL, D_D), 0)
    cls = column_sum(jnp.where(at == image, cls_ref[...].astype(jnp.float32), 0.0))
    de_all[:KEEP] = de_ref[...]
    de_all[KEEP:] = low(tail_rows(cls))
    de = de_all[...]
    be_grad[0:1, :] += column_sum(de.astype(jnp.float32))
    scaled3, inverse3 = norm_rows(enc_ref[0])
    third = low(scaled3 * gain3 + shift3)
    quarter = FF_E // 4
    first = D_E // 4
    small = D_D // 4
    grad_ref[:, first + 2 * quarter :] += dot_f32(
        third, de_all[:, pl.ds(pl.multiple_of(place * small, small), small)], TN
    )
    up3, g_gain3, g_shift3 = norm_rows_back(
        dot_f32(de, w_ref[:, E_EMBED:], NT), scaled3, inverse3, gain3
    )
    up3_low = low(up3)
    scaled2, inverse2 = norm_rows(mid_ref[0])
    second = low(scaled2 * gain2 + shift2)
    own_hidden = pl.ds(pl.multiple_of(place * quarter, quarter), quarter)
    back = jnp.zeros_like(up3)
    for at in range(0, FF_E, SIZE):
        span = slice(at, at + SIZE)
        hidden = dot_f32(up3_low, w_ref[:, E_DOWN + at : E_DOWN + at + SIZE], NN)
        hidden = low(hidden * slope_ref[0, :, span])
        hidden_all[:, span] = hidden
        bu_grad[0:1, span] += column_sum(hidden.astype(jnp.float32))
        back = back + dot_f32(hidden, w_ref[:, E_UP + at : E_UP + at + SIZE], NT)
    grad_ref[:, first : first + quarter] += dot_f32(second, hidden_all[:, own_hidden], TN)
    grad_ref[:, first + quarter : first + 2 * quarter] += dot_f32(
        up3_low, act_ref[0, :, own_hidden], TN
    )
    through, g_gain2, g_shift2 = norm_rows_back(back, scaled2, inverse2, gain2)
    middle_grad = up3 + through
    dmid_ref[0] = middle_grad
    grad_ref[:, :first] += dot_f32(o_ref[0], turn_quarter(middle_grad, place), TN)
    do_ref[0] = low(dot_f32(low(middle_grad), w_ref[:, E_OUT:E_UP], NT))
    sums = (column_sum(middle_grad), g_shift2, column_sum(up3), g_shift3, g_gain2, g_gain3)
    for at, part in enumerate(sums):
        vec_grad[at : at + 1, :] += part


def scalar_spec():
    return pl.BlockSpec(memory_space=pltpu.SMEM)


def encoder_back(place, de_sum, saved, enc_full, vectors):
    mid, enc, o, slope, act = saved
    images = mid.shape[0]
    f32 = jnp.float32
    width = D_E // 4 + FF_E // 2 + D_D // 4
    return pl.pallas_call(
        encoder_back_kernel,
        grid=(images,),
        in_specs=[
            scalar_spec(),
            pl.BlockSpec((KEEP, D_D), lambda i: (i, 0)),
            pl.BlockSpec((TAIL, D_D), lambda i: (images * KEEP // TAIL, 0)),
            per_image(E_ROWS, D_E),
            per_image(E_ROWS, D_E),
            per_image(E_ROWS, D_E),
            per_image(E_ROWS, FF_E),
            per_image(E_ROWS, FF_E),
            whole(enc_full.shape),
            whole((8, D_E)),
        ],
        out_specs=[
            per_image(E_ROWS, D_E),
            per_image(E_ROWS, D_E),
            whole((D_E, width)),
            whole((8, D_E)),
            whole((8, FF_E)),
            whole((8, D_D)),
        ],
        out_shape=[
            jax.ShapeDtypeStruct((images, E_ROWS, D_E), jnp.bfloat16),
            jax.ShapeDtypeStruct((images, E_ROWS, D_E), f32),
            jax.ShapeDtypeStruct((D_E, width), f32),
            jax.ShapeDtypeStruct((8, D_E), f32),
            jax.ShapeDtypeStruct((8, FF_E), f32),
            jax.ShapeDtypeStruct((8, D_D), f32),
        ],
        scratch_shapes=[
            pltpu.VMEM((E_ROWS, D_D), jnp.bfloat16),
            pltpu.VMEM((E_ROWS, FF_E), jnp.bfloat16),
        ],
        compiler_params=pltpu.CompilerParams(vmem_limit_bytes=KERNEL_LIMIT),
        cost_estimate=pl.CostEstimate(
            flops=3 * images * E_ROWS * enc_full.size,
            bytes_accessed=50 * 1024 * 1024,
            transcendentals=0,
        ),
    )(place, de_sum, de_sum, mid, enc, o, slope, act, enc_full, vectors)


def encoder_entry_back_kernel(
    place_ref,
    kept_ref,
    x_ref,
    qkv_ref,
    lse_ref,
    o_ref,
    do_ref,
    dmid_ref,
    w_ref,
    vec_ref,
    grad_ref,
    vec_grad,
    dqkv_ref,
):
    place = place_ref[0]
    clear_first((grad_ref, vec_grad))
    gain1, shift1 = (vec_ref[i : i + 1, :] for i in range(2))
    for group in range(D_E // 128):
        span = slice(group * 128, (group + 1) * 128)
        parts = [
            qkv_ref[0, :, at * D_E + group * 128 : at * D_E + (group + 1) * 128] for at in range(3)
        ]
        sums = [
            lse_ref[0, group * E_HEADS + head : group * E_HEADS + head + 1, :]
            for head in range(E_HEADS)
        ]
        dq, dk, dv = attend_backward_group(
            E_HEADS, E_DIM, *parts, sums, do_ref[0, :, span], o_ref[0, :, span]
        )
        dqkv_ref[:, group * 128 : (group + 1) * 128] = dq
        for at, pair in ((1, dk), (2, dv)):
            lanes = slice(at * D_E + group * 128, at * D_E + (group + 1) * 128)
            dqkv_ref[:KEEP, lanes], dqkv_ref[KEEP:, lanes] = pair
    scaled, inverse = norm_rows(x_ref[0])
    normed = low(scaled * gain1 + shift1)
    quarter = D_E // 4
    sums = []
    for at in range(3):
        part = dqkv_ref[:, at * D_E : (at + 1) * D_E].astype(jnp.float32)
        if at != 1:
            sums.append(column_sum(part))
        grad_ref[:, (at + 1) * quarter : (at + 2) * quarter] += dot_f32(
            normed, turn_quarter(part, place), TN
        )
    through, g_gain1, g_shift1 = norm_rows_back(
        dot_f32(dqkv_ref[...], w_ref[:, D_E : 4 * D_E], NT), scaled, inverse, gain1
    )
    back = dmid_ref[0] + through
    patches = back[:KEEP]
    grad_ref[:, :quarter] += dot_f32(kept_ref[0], turn_quarter(patches, place), TN)
    sums = [column_sum(patches), back[KEEP : KEEP + 1], g_shift1] + sums + [g_gain1]
    for at, part in enumerate(sums):
        vec_grad[at : at + 1, :] += part


def encoder_entry_back(place, kept, saved, do, dmid, enc_full, vectors):
    x0, qkv, lse, o = saved
    images = kept.shape[0]
    f32 = jnp.float32
    return pl.pallas_call(
        encoder_entry_back_kernel,
        grid=(images,),
        in_specs=[
            scalar_spec(),
            per_image(KEEP, D_E),
            per_image(E_ROWS, D_E),
            per_image(E_ROWS, 3 * D_E),
            per_image(H_E, E_ROWS),
            per_image(E_ROWS, D_E),
            per_image(E_ROWS, D_E),
            per_image(E_ROWS, D_E),
            columns(D_E, 5 * D_E, 0),
            whole((8, D_E)),
        ],
        out_specs=[whole((D_E, D_E)), whole((8, D_E))],
        out_shape=[
            jax.ShapeDtypeStruct((D_E, D_E), f32),
            jax.ShapeDtypeStruct((8, D_E), f32),
        ],
        scratch_shapes=[pltpu.VMEM((E_ROWS, 3 * D_E), jnp.bfloat16)],
        compiler_params=pltpu.CompilerParams(vmem_limit_bytes=KERNEL_LIMIT),
        cost_estimate=pl.CostEstimate(
            flops=8 * images * E_ROWS * D_E * 4 * D_E,
            bytes_accessed=20 * 1024 * 1024,
            transcendentals=images * H_E * E_ROWS * E_ROWS,
        ),
    )(place, kept, x0, qkv, lse, o, do, dmid, enc_full, vectors)


def stack_rows(parts, count=8):
    rows = jnp.stack(parts)
    return jnp.pad(rows, ((0, count - len(parts)), (0, 0)))


def adamw(weight, moment_one, moment_two, gradient, step_rate, decay_rate):
    moment_one = BETA_ONE * moment_one + (1 - BETA_ONE) * gradient
    moment_two = BETA_TWO * moment_two + (1 - BETA_TWO) * gradient * gradient
    fixed_one = moment_one / (1 - BETA_ONE**STEP)
    fixed_two = moment_two / (1 - BETA_TWO**STEP)
    weight = weight - step_rate * (
        fixed_one / (jnp.sqrt(fixed_two) + ADAM_EPS) + decay_rate * weight
    )
    return (moment_one, moment_two, weight)


def shards(
    pixels,
    restore,
    enc_w,
    enc_m,
    enc_v,
    dec_w,
    dec_m,
    dec_v,
    head_w,
    head_m,
    head_v,
    gain_w,
    gain_m,
    gain_v,
    bias_w,
    bias_m,
    bias_v,
):
    seq_count = lax.axis_size("seq")
    place = lax.axis_index("seq")
    images, own_count, _ = pixels.shape
    masked_total = images * lax.axis_size("fsdp") * (PATCHES - KEEP)

    enc_full = lax.all_gather(low(enc_w), "fsdp", axis=0, tiled=True)
    dec_full = lax.all_gather(low(dec_w), "fsdp", axis=0, tiled=True)
    head_low = low(head_w)
    d_query = dec_full[:, :D_D]
    d_key = dec_full[:, D_D : 2 * D_D]
    d_value = dec_full[:, 2 * D_D : 3 * D_D]

    pieces = split_vector(bias_w, bias_widths())
    gains = split_vector(gain_w, [D_E, D_E, D_E, D_D, D_D, D_D])
    (b_patch, cls_token, e_shift1, e_bq, e_bv, e_bo, e_shift2, e_bu, e_bd, e_shift3) = pieces[:10]
    (b_embed, mask_token, d_shift1, d_bq, d_bv, d_bo, d_shift2, d_bu, d_bd, d_shift3) = pieces[
        10:20
    ]
    b_head = pieces[20]

    ranks = jnp.arange(KEEP, dtype=jnp.int32)
    turned = lax.dynamic_slice_in_dim(
        jnp.concatenate([restore, restore], axis=1), place * own_count, PATCHES, axis=1
    )
    own_restore = turned[:, :own_count]
    own_pick = low(own_restore[:, None, :] == ranks[None, :, None])
    own_kept = jnp.einsum("irp,ipd->ird", own_pick, pixels, preferred_element_type=jnp.float32)
    kept = line_sum(low(own_kept).reshape(images * KEEP, PIX), 8, 0).reshape(images, KEEP, PIX)
    patch_ids = jnp.arange(PATCHES, dtype=jnp.int32)
    keep_ids = jnp.sum(
        jnp.where(restore[:, None, :] == ranks[None, :, None], patch_ids, 0), axis=2
    )

    x0, e_mid, encoded, e_mixed, e_lse, e_o, e_slope, e_act, shrunk = encoder(
        kept,
        b_patch + positions(keep_ids, D_E),
        enc_full,
        stack_rows(
            gains[:3] + [cls_token, e_shift1, e_bq, e_bv, e_bo, e_shift2, e_bd, e_shift3], 16
        ),
        e_bu[None],
        b_embed[None],
    )

    pick = low(turned[:, :, None] == ranks[None, None, :])
    is_masked = turned >= KEEP
    turned_ids = lax.rem(patch_ids + place * own_count, PATCHES)
    spread = jnp.einsum(
        "ipr,ird->ipd", pick, shrunk[:, :KEEP], preferred_element_type=jnp.float32
    )
    patch_rows = (
        jnp.where(is_masked[..., None], mask_token, spread) + positions(turned_ids, D_D)[None]
    )
    d_tail = jnp.where(
        jnp.arange(TAIL)[None, :, None] == 0,
        shrunk[:, KEEP : KEEP + 1].astype(jnp.float32),
        0.0,
    )
    y0 = jnp.concatenate([patch_rows, d_tail], axis=1)
    d_n1, d_sc1, d_inv1 = norm_forward(y0, gains[3], d_shift1)
    d_n1 = low(d_n1)

    y0_own = y0[:, :own_count]
    n1_own = d_n1[:, :own_count]
    d_q = low(project(n1_own, d_query) + d_bq)
    d_k = low(project(d_n1, d_key))
    d_v = low(project(d_n1, d_value) + d_bv)
    d_o, d_lse = attend_forward(d_q, d_k, d_v, H_D)
    own_masked = (own_restore >= KEEP).astype(jnp.float32)
    own_masked = jnp.broadcast_to(own_masked[..., None], own_masked.shape + (128,))
    d_do, d_dmid, late_grads, mid_sums, bu_sums, bh_sums = dec_middle(
        d_o,
        y0_own,
        pixels,
        own_masked,
        dec_full,
        head_low,
        stack_rows([d_bo, gains[4], d_shift2, d_bd, gains[5], d_shift3]),
        d_bu[None],
        b_head[None],
        2.0 / (PIX * masked_total),
    )
    g_d_bo, g_d_gain2, g_d_shift2, g_d_bd, g_d_gain3, g_d_shift3 = (mid_sums[i] for i in range(6))
    g_d_bu = bu_sums[0]
    g_b_head = bh_sums[0]
    loss_part = jnp.sum(bh_sums[1]) / (PIX * masked_total)
    dec_late = lax.psum_scatter(late_grads, "fsdp", scatter_dimension=0, tiled=True)
    d_dq, d_dk, d_dv = attend_backward(d_q, d_k, d_v, d_lse, d_do, d_o, H_D)
    de_part, g_d_qkv, entry_sums = dec_entry_back(
        y0, d_dq, d_dk, d_dv, d_dmid, turned[:, None, :], dec_full, stack_rows([gains[3], d_shift1])
    )
    g_mask, g_d_shift1, g_d_bq, g_d_bv, g_d_gain1 = (entry_sums[i] for i in range(5))
    dec_early = lax.psum_scatter(g_d_qkv, "fsdp", scatter_dimension=0, tiled=True)
    de_sum = line_sum(de_part, 7, 1)
    dec_late, de_sum = lax.optimization_barrier((dec_late, de_sum))

    place_word = place[None].astype(jnp.int32)
    e_do, e_dmid, early_grads, back_sums, bu_sums, be_sums = encoder_back(
        place_word,
        de_sum,
        (e_mid, encoded, e_o, e_slope, e_act),
        enc_full,
        stack_rows([gains[1], gains[2], e_shift2, e_shift3]),
    )
    g_e_bo, g_e_shift2, g_e_bd, g_e_shift3, g_e_gain2, g_e_gain3 = (back_sums[i] for i in range(6))
    g_e_bu = bu_sums[0]
    g_b_embed = be_sums[0]
    dec_early, e_do = lax.optimization_barrier((dec_early, e_do))
    dec_grad_all = lax.psum(jnp.concatenate([dec_early, dec_late], axis=1), "seq")
    late_grads, entry_sums = encoder_entry_back(
        place_word,
        kept,
        (x0, e_mixed, e_lse, e_o),
        e_do,
        e_dmid,
        enc_full,
        stack_rows([gains[0], e_shift1]),
    )
    g_b_patch, g_cls, g_e_shift1, g_e_bq, g_e_bv, g_e_gain1 = (entry_sums[i] for i in range(6))

    once = jnp.where(place == 0, 1.0, 0.0)
    enc_bias = [g_b_patch, g_cls, g_e_shift1, g_e_bq, g_e_bv, g_e_bo, g_e_shift2, g_e_bu]
    enc_bias = jnp.concatenate(enc_bias + [g_e_bd, g_e_shift3, g_b_embed]) * once
    dec_bias = [g_mask, g_d_shift1, g_d_bq, g_d_bv, g_d_bo, g_d_shift2, g_d_bu, g_d_bd]
    dec_bias = jnp.concatenate(dec_bias + [g_d_shift3, g_b_head])
    enc_gain = jnp.concatenate([g_e_gain1, g_e_gain2, g_e_gain3]) * once
    dec_gain = jnp.concatenate([g_d_gain1, g_d_gain2, g_d_gain3])
    small = jnp.concatenate([enc_gain, dec_gain, enc_bias, dec_bias, loss_part[None]])
    embed_cols = D_D // seq_count
    early_all, late_all, small = exchange(
        early_grads, late_grads, small, seq_count, embed_cols, 2
    )
    dec_grad = dec_grad_all[:, : 4 * D_D + 2 * FF_D]
    head_grad = lax.all_gather(
        dec_grad_all[:, 4 * D_D + 2 * FF_D :], "fsdp", axis=0, tiled=True
    )

    def by_column(gathered, offset, size):
        return [gathered[at, :, offset : offset + size] for at in range(seq_count)]

    quarter_e = D_E // seq_count
    quarter_f = FF_E // seq_count
    spans = []
    for at in range(4):
        spans += by_column(late_all, at * quarter_e, quarter_e)
    spans += by_column(early_all, 0, quarter_e)
    spans += by_column(early_all, quarter_e, quarter_f)
    spans += by_column(early_all, quarter_e + quarter_f, quarter_f)
    spans = [part.astype(jnp.float32) for part in spans]
    offset = quarter_e + 2 * quarter_f
    rounded = by_column(early_all, offset, embed_cols)
    rests = by_column(early_all, offset + embed_cols, embed_cols)
    spans += [a.astype(jnp.float32) + b.astype(jnp.float32) for a, b in zip(rounded, rests)]
    enc_grad = jnp.concatenate(spans, axis=1)
    n_gain = gain_w.shape[0]
    n_bias = bias_w.shape[0]
    gain_grad = small[:n_gain]
    bias_grad = small[n_gain : n_gain + n_bias]
    loss_total = small[n_gain + n_bias]

    enc_new = adamw(enc_w, enc_m, enc_v, enc_grad, MATRIX_RATE, MATRIX_DECAY)
    dec_new = adamw(dec_w, dec_m, dec_v, dec_grad, MATRIX_RATE, MATRIX_DECAY)
    head_new = adamw(head_w, head_m, head_v, head_grad, MATRIX_RATE, MATRIX_DECAY)
    gain_new = adamw(gain_w, gain_m, gain_v, gain_grad, SMALL_RATE, 0.0)
    bias_new = adamw(bias_w, bias_m, bias_v, bias_grad, SMALL_RATE, 0.0)
    return (loss_total,) + enc_new + dec_new + head_new + gain_new + bias_new


def solution(mesh):
    rows = P("fsdp", None)
    in_specs = (P("fsdp", "seq", None), rows) + (rows,) * 6 + (P(),) * 9
    out_specs = (P(),) + (rows,) * 6 + (P(),) * 9
    return jax.shard_map(shards, mesh=mesh, in_specs=in_specs, out_specs=out_specs, check_vma=False)
```

```python
from functools import partial

import jax
import jax.numpy as jnp
from jax import lax
from jax.experimental import pallas as pl
from jax.experimental.pallas import tpu as pltpu
from jax.sharding import PartitionSpec as P

D_E = 768
H_E = 12
FF_E = 3072
D_D = 512
H_D = 16
FF_D = 2048
PIX = 768
PATCHES = 1024
KEEP = 256
STEP = 5

NORM_EPS = 1e-06
PIXEL_EPS = 1e-06
BETA_ONE = 0.5
BETA_TWO = 0.75
MATRIX_RATE = 0.03
SMALL_RATE = 0.1
MATRIX_DECAY = 0.05
ADAM_EPS = 1e-08

TAIL = 16
E_ROWS = KEEP + TAIL
D_ROWS = PATCHES + TAIL
LOG2E = 1.4426950408889634
MASKED_SCORE = -1e30


def bias_widths():
    return [D_E] * 7 + [FF_E] + [D_E] * 2 + [D_D] * 7 + [FF_D] + [D_D] * 2 + [PIX]


def split_vector(vector, widths):
    pieces = []
    offset = 0
    for span_width in widths:
        pieces.append(vector[offset : offset + span_width])
        offset += span_width
    return pieces


def positions(index_arr, width_dim):
    halves = width_dim // 2
    frequency = 10000.0 ** (-jnp.arange(halves, dtype=jnp.float32) / halves)
    angles = (index_arr.astype(jnp.float32) + 1.0)[..., None] * frequency
    return jnp.concatenate([jnp.sin(angles), jnp.cos(angles)], axis=-1)


def norm_forward(inputs, gain_vec, shift_vec):
    centre = inputs - jnp.mean(inputs, axis=-1, keepdims=True)
    inverse = lax.rsqrt(jnp.mean(centre * centre, axis=-1, keepdims=True) + NORM_EPS)
    scaled = centre * inverse
    return (scaled * gain_vec + shift_vec, scaled, inverse)


def norm_backward(upstream, scaled, inverse, gain_vec):
    weighted = upstream * gain_vec
    inner_part = (
        weighted
        - jnp.mean(weighted, axis=-1, keepdims=True)
        - scaled * jnp.mean(weighted * scaled, axis=-1, keepdims=True)
    )
    return (
        inverse * inner_part,
        jnp.sum(upstream * scaled, axis=(0, 1)),
        jnp.sum(upstream, axis=(0, 1)),
    )


def low(tensor):
    return tensor.astype(jnp.bfloat16)


def project(row_block, weight):
    return jnp.einsum("isd,de->ise", row_block, weight, preferred_element_type=jnp.float32)


def project_back(row_block, weight):
    return jnp.einsum("ise,de->isd", row_block, weight, preferred_element_type=jnp.float32)


def weight_grad(row_block, upstream):
    return jnp.einsum("isd,ise->de", row_block, upstream, preferred_element_type=jnp.float32)


def row_sum(tensor):
    return jnp.sum(tensor.astype(jnp.float32), axis=(0, 1))


def enc_mats_of(full_rows):
    return (
        full_rows[:, D_E : 4 * D_E],
        full_rows[:, 4 * D_E : 5 * D_E],
        full_rows[:, 5 * D_E : 5 * D_E + FF_E],
        full_rows[:, 5 * D_E + FF_E : 5 * D_E + 2 * FF_E],
    )


def dot_f32(left, right, contract):
    return lax.dot_general(
        left, right, (contract, ((), ())), preferred_element_type=jnp.float32
    )


NN = ((1,), (0,))
TN = ((0,), (0,))


def pieces_of(value):
    first = low(value).astype(jnp.float32)
    rest = value - first
    second = low(rest).astype(jnp.float32)
    return first, second, rest - second


def own_span(shape, axis, head, head_dim):
    place = lax.broadcasted_iota(jnp.int32, shape, axis)
    return (place >= head * head_dim) & (place < (head + 1) * head_dim)


def live_tail(rows, scores, other):
    place = lax.broadcasted_iota(jnp.int32, (rows, scores.shape[1]), 0)
    return jnp.where(place < 1, scores, other)


def attend_forward_group(heads, head_dim, q, k, v):
    main = k.shape[0] - TAIL
    scale = head_dim ** (-0.5) * LOG2E
    q_t = q.astype(jnp.float32).T * scale
    q_high = low(q_t)
    q_rest = low(q_t - q_high.astype(jnp.float32))
    k_main = jnp.concatenate([k[:main], k[:main]], axis=1)
    k_tail = jnp.concatenate([k[main:], k[main:]], axis=1)
    v_main = low(v[:main].astype(jnp.float32).T)
    v_tail = v[main:]
    ones = jnp.ones((TAIL, main), jnp.bfloat16)

    def scores_of(head):
        own = own_span(q_t.shape, 0, head, head_dim)
        none = jnp.zeros_like(q_high)
        q_h = jnp.concatenate([jnp.where(own, q_high, none), jnp.where(own, q_rest, none)], axis=0)
        return dot_f32(k_main, q_h, NN), live_tail(TAIL, dot_f32(k_tail, q_h, NN), MASKED_SCORE)

    outs, sums = [], []
    following = scores_of(0)
    for head in range(heads):
        span = slice(head * head_dim, (head + 1) * head_dim)
        s_main, s_tail = following
        if head + 1 < heads:
            following = scores_of(head + 1)
        top = jnp.maximum(
            jnp.max(s_main, axis=0, keepdims=True), jnp.max(s_tail, axis=0, keepdims=True)
        )
        p_main = low(jnp.exp2(s_main - top))
        p_tail = low(jnp.exp2(s_tail - top))
        o_t = dot_f32(jnp.concatenate([v_main[span], ones], axis=0), p_main, NN)
        total = o_t[head_dim : head_dim + 1] + jnp.sum(
            p_tail.astype(jnp.float32), axis=0, keepdims=True
        )
        o_t = o_t[:head_dim] + dot_f32(v_tail, p_tail, TN)[span]
        outs.append(o_t * (1.0 / total))
        sums.append(top + jnp.log2(total))
    return low(jnp.concatenate(outs, axis=0).T), sums


def attend_forward_kernel(heads, head_dim, q_ref, k_ref, v_ref, o_ref, lse_ref):
    o_ref[0], sums = attend_forward_group(heads, head_dim, q_ref[0], k_ref[0], v_ref[0])
    for head in range(heads):
        lse_ref[0, 0, head : head + 1, :] = sums[head]


def attend_backward_group(heads, head_dim, q, k, v, sums, do, o):
    main = k.shape[0] - TAIL
    rows = q.shape[0]
    unit = head_dim ** (-0.5)
    q_t = q.astype(jnp.float32).T * (unit * LOG2E)
    q_high = low(q_t).astype(jnp.float32)
    q_rest = q_t - q_high
    do_t = do.astype(jnp.float32).T
    inner_t = do_t * o.astype(jnp.float32).T
    place = lax.broadcasted_iota(jnp.int32, q_t.shape, 0)

    def with_row(block, offset, value):
        for at, part in enumerate(pieces_of(value)):
            block = jnp.where(place == offset + at, part, block)
        return block

    score_sides, value_sides = [], []
    for head in range(heads):
        own = own_span(q_t.shape, 0, head, head_dim)
        span = slice(head * head_dim, (head + 1) * head_dim)
        other = ((head + 1) % heads) * head_dim
        lse = sums[head]
        inner = jnp.sum(inner_t[span], axis=0, keepdims=True)
        rest = with_row(jnp.where(own, q_rest, 0.0), other, -lse)
        score_sides.append(low(jnp.concatenate([jnp.where(own, q_high, 0.0), rest], axis=0)))
        last = with_row(jnp.zeros_like(do_t), 0, -inner)
        value_sides.append(low(jnp.concatenate([jnp.where(own, do_t, 0.0), last], axis=0)))
    zero = jnp.zeros_like(q)
    q_sides = [jnp.where(own_span(q.shape, 1, h, head_dim), q, zero) for h in range(heads)]
    do_sides = [jnp.where(own_span(q.shape, 1, h, head_dim), do, zero) for h in range(heads)]
    stacked = rows % 128 == 0
    if stacked:
        q_sides = jnp.concatenate(q_sides, axis=0)
        do_sides = jnp.concatenate(do_sides, axis=0)

    def sum_heads(parts, sides):
        if stacked:
            return dot_f32(jnp.concatenate(parts, axis=1), sides, NN)
        terms = [dot_f32(part, side, NN) for part, side in zip(parts, sides)]
        return sum(terms[1:], terms[0])

    k_main = k[:main]
    k_tail = k[main:]
    k_main_t = low(k_main.astype(jnp.float32).T)

    def with_ones(block):
        return jnp.concatenate([block, jnp.ones_like(block)], axis=1)

    def beside_own(block, head):
        own = jnp.where(own_span(block.shape, 1, head, head_dim), block, jnp.ones_like(block))
        return jnp.concatenate([block, own], axis=1)

    v_main = with_ones(v[:main])
    v_tail = with_ones(v[main:])
    dq_parts, p_mains, s_mains, p_tails, s_tails = [], [], [], [], []
    for head in range(heads):
        span = slice(head * head_dim, (head + 1) * head_dim)
        p = jnp.exp2(dot_f32(beside_own(k_main, head), score_sides[head], NN))
        s = low(p * dot_f32(v_main, value_sides[head], NN))
        p_mains.append(low(p))
        s_mains.append(s)
        p = jnp.exp2(dot_f32(beside_own(k_tail, head), score_sides[head], NN))
        p = live_tail(TAIL, p, 0.0)
        s_tail = low(p * dot_f32(v_tail, value_sides[head], NN))
        p_tails.append(low(p))
        s_tails.append(s_tail)
        dq_parts.append(dot_f32(k_main_t[span], s, NN) + dot_f32(k_tail, s_tail, TN)[span])
    dk = [low(sum_heads(part, q_sides) * unit) for part in (s_mains, s_tails)]
    dv = [low(sum_heads(part, do_sides)) for part in (p_mains, p_tails)]
    dq = low(jnp.concatenate(dq_parts, axis=0).T * unit)
    return dq, dk, dv


def attend_backward_kernel(
    heads, head_dim, q_ref, k_ref, v_ref, lse_ref, do_ref, o_ref, dq_ref, dk_ref, dv_ref
):
    main = k_ref.shape[1] - TAIL
    sums = [lse_ref[0, 0, head : head + 1, :] for head in range(heads)]
    dq_ref[0], dk, dv = attend_backward_group(
        heads, head_dim, q_ref[0], k_ref[0], v_ref[0], sums, do_ref[0], o_ref[0]
    )
    dk_ref[0, :main], dk_ref[0, main:] = dk
    dv_ref[0, :main], dv_ref[0, main:] = dv


VMEM_LIMIT = 32 * 1024 * 1024
KERNEL_LIMIT = 58 * 1024 * 1024


def attend_specs(q_rows, k_rows, heads):
    return (
        pl.BlockSpec((1, q_rows, 128), lambda i, g: (i, 0, g)),
        pl.BlockSpec((1, k_rows, 128), lambda i, g: (i, 0, g)),
        pl.BlockSpec((1, 1, heads, q_rows), lambda i, g: (i, g, 0, 0)),
    )


def attend_forward(queries, key_rows, value_rows, head_count):
    images, q_rows, width = queries.shape
    k_rows = key_rows.shape[1]
    head_dim = width // head_count
    heads = 128 // head_dim
    groups = width // 128
    q_spec, k_spec, l_spec = attend_specs(q_rows, k_rows, heads)
    return pl.pallas_call(
        partial(attend_forward_kernel, heads, head_dim),
        grid=(images, groups),
        in_specs=[q_spec, k_spec, k_spec],
        out_specs=[q_spec, l_spec],
        out_shape=[
            jax.ShapeDtypeStruct((images, q_rows, width), jnp.bfloat16),
            jax.ShapeDtypeStruct((images, groups, heads, q_rows), jnp.float32),
        ],
        compiler_params=pltpu.CompilerParams(vmem_limit_bytes=VMEM_LIMIT),
        cost_estimate=pl.CostEstimate(
            flops=16 * images * q_rows * k_rows * width,
            bytes_accessed=4 * images * (q_rows + k_rows) * width,
            transcendentals=images * head_count * q_rows * k_rows,
        ),
    )(queries, key_rows, value_rows)


def attend_backward(queries, key_rows, value_rows, logsum, upstream, attended, head_count):
    images, q_rows, width = queries.shape
    k_rows = key_rows.shape[1]
    head_dim = width // head_count
    heads = 128 // head_dim
    groups = width // 128
    q_spec, k_spec, l_spec = attend_specs(q_rows, k_rows, heads)
    return pl.pallas_call(
        partial(attend_backward_kernel, heads, head_dim),
        grid=(images, groups),
        in_specs=[q_spec, k_spec, k_spec, l_spec, q_spec, q_spec],
        out_specs=[q_spec, k_spec, k_spec],
        out_shape=[
            jax.ShapeDtypeStruct((images, q_rows, width), jnp.bfloat16),
            jax.ShapeDtypeStruct((images, k_rows, width), jnp.bfloat16),
            jax.ShapeDtypeStruct((images, k_rows, width), jnp.bfloat16),
        ],
        compiler_params=pltpu.CompilerParams(vmem_limit_bytes=VMEM_LIMIT),
        cost_estimate=pl.CostEstimate(
            flops=40 * images * q_rows * k_rows * width,
            bytes_accessed=8 * images * (q_rows + k_rows) * width,
            transcendentals=images * head_count * q_rows * k_rows,
        ),
    )(queries, key_rows, value_rows, logsum, upstream, attended)


MESH = pl.DeviceIdType.MESH


def line_sum_kernel(
    chunks, lines, x_ref, o_ref, from_left, from_right, to_left, to_right, send_sem, recv_sem
):
    count = lax.axis_size("seq")
    place = lax.axis_index("seq")
    has_left = place > 0
    has_right = place < count - 1
    rows = x_ref.shape[0] // chunks
    barrier = pltpu.get_barrier_semaphore()

    def greet(to):
        pl.semaphore_signal(barrier, inc=1, device_id={"seq": to}, device_id_type=MESH)

    pl.when(has_left)(lambda: greet(place - 1))
    pl.when(has_right)(lambda: greet(place + 1))
    peers = jnp.where(has_left, 1, 0) + jnp.where(has_right, 1, 0)
    pl.semaphore_wait(barrier, peers)

    def copy(way, at):
        span = pl.ds(pl.multiple_of(at * rows, 16), rows)
        source, target = ((to_right, from_left), (to_left, from_right))[way]
        return pltpu.make_async_remote_copy(
            src_ref=source.at[span],
            dst_ref=target.at[span],
            send_sem=send_sem.at[way, at],
            recv_sem=recv_sem.at[way, at],
            device_id={"seq": place + 1 if way == 0 else place - 1},
            device_id_type=MESH,
        )

    def end_copy(way, at):
        span = pl.ds(at * rows, rows)
        return pltpu.make_async_remote_copy(
            src_ref=x_ref.at[span],
            dst_ref=(from_left, from_right)[way].at[span],
            send_sem=send_sem.at[way, at],
            recv_sem=recv_sem.at[way, at],
            device_id={"seq": place + 1 if way == 0 else place - 1},
            device_id_type=MESH,
        )

    for way, is_end in ((0, jnp.logical_not(has_left)), (1, jnp.logical_not(has_right))):

        @pl.when(is_end)
        def _():
            for at in range(chunks):
                if at >= 2:
                    end_copy(way, at - 2).wait_send()
                end_copy(way, at).start()
            for at in range(chunks - 2, chunks):
                end_copy(way, at).wait_send()

    def span_of(at):
        return pl.ds(pl.multiple_of(at * rows, 16), rows)

    for step in range(chunks + lines - 1):
        from_first = step - place
        from_last = step - (count - 1 - place)

        @pl.when(has_left & (from_first >= 0) & (from_first < chunks))
        def _():
            copy(0, from_first).wait_recv()

            @pl.when(has_right)
            def _():
                span = span_of(from_first)
                to_right[span] = x_ref[span] + from_left[span]
                copy(0, from_first).start()

        @pl.when(has_right & (from_last >= 0) & (from_last < chunks))
        def _():
            copy(1, from_last).wait_recv()

            @pl.when(has_left)
            def _():
                span = span_of(from_last)
                to_left[span] = x_ref[span] + from_right[span]
                copy(1, from_last).start()

    @pl.when(jnp.logical_not(has_left))
    def _():
        o_ref[...] = x_ref[...] + from_right[...]

    @pl.when(jnp.logical_not(has_right))
    def _():
        o_ref[...] = x_ref[...] + from_left[...]

    @pl.when(has_left & has_right)
    def _():
        o_ref[...] = (x_ref[...] + from_left[...]) + from_right[...]
        for at in range(chunks):
            copy(0, at).wait_send()
            copy(1, at).wait_send()


GATHER_CHUNKS = 6
KEPT_CHUNKS = 8


def start_kernel(
    lines,
    w_ref,
    x_ref,
    full_ref,
    o_ref,
    from_left,
    from_right,
    to_left,
    to_right,
    own_sem,
    ring_sems,
    pair_sems,
    send_sem,
    recv_sem,
):
    own = lax.axis_index("fsdp")
    place = lax.axis_index("seq")
    core = lax.rem(own, 2)
    at_x = lax.rem(lax.div(own, 2), 2)
    at_y = lax.div(own, 4)
    odd = lax.rem(place, 2)
    by_x = 2 - 4 * at_x
    by_y = 4 - 8 * at_y
    ahead = own + (1 - odd) * by_x + odd * by_y
    aside = own + odd * by_x + (1 - odd) * by_y
    across = own + by_x + by_y
    partner = own + 1 - 2 * core
    over = place + 1 - 2 * odd
    has_left = place > 0
    has_right = place < lines - 1
    block = w_ref.shape[0]
    rows = block // GATHER_CHUNKS
    kept_rows = x_ref.shape[0] // KEPT_CHUNKS
    barrier = pltpu.get_barrier_semaphore()

    def greet(device):
        pl.semaphore_signal(barrier, inc=1, device_id=device, device_id_type=MESH)

    for device in (ahead, aside, partner):
        greet({"fsdp": device})
    pl.when(has_left)(lambda: greet({"seq": place - 1}))
    pl.when(has_right)(lambda: greet({"seq": place + 1}))
    peers = jnp.where(has_left, 1, 0) + jnp.where(has_right, 1, 0)
    pl.semaphore_wait(barrier, peers + 3)

    def span_of(owner, at):
        return pl.ds(pl.multiple_of(owner * block + at * rows, 16), rows)

    def copy_of(source, target, sems, at, device):
        return pltpu.make_async_remote_copy(
            src_ref=source,
            dst_ref=target,
            send_sem=sems.at[(0,) + at],
            recv_sem=sems.at[(1,) + at],
            device_id=device,
            device_id_type=MESH,
        )

    def own_rows(at):
        return w_ref.at[pl.ds(at * rows, rows)]

    def ahead_copy(at):
        target = full_ref.at[span_of(own, at)]
        return copy_of(own_rows(at), target, ring_sems, (0, at), {"fsdp": ahead})

    def aside_copy(at):
        part = full_ref.at[span_of(ahead, at)]
        return copy_of(part, part, ring_sems, (1, at), {"fsdp": aside})

    def over_copy(at):
        part = full_ref.at[span_of(ahead, at)]
        return copy_of(part, part, ring_sems, (2, at), {"seq": over})

    def pair_copy(kind, at):
        target = full_ref.at[span_of((own, ahead, across, aside)[kind], at)]
        source = own_rows(at) if kind == 0 else target
        return copy_of(source, target, pair_sems, (kind, at), {"fsdp": partner})

    def keep_copy(at):
        return pltpu.make_async_copy(
            own_rows(at), full_ref.at[span_of(own, at)], own_sem.at[at]
        )

    def send_own(at):
        ahead_copy(at).start()
        pair_copy(0, at).start()
        keep_copy(at).start()

    def kept_span(at):
        return pl.ds(pl.multiple_of(at * kept_rows, 16), kept_rows)

    def kept_copy(way, at, source=None):
        span = kept_span(at)
        source = (to_right, to_left)[way] if source is None else source
        return pltpu.make_async_remote_copy(
            src_ref=source.at[span],
            dst_ref=(from_left, from_right)[way].at[span],
            send_sem=send_sem.at[way, at],
            recv_sem=recv_sem.at[way, at],
            device_id={"seq": place + 1 if way == 0 else place - 1},
            device_id_type=MESH,
        )

    def kept_step(step):
        if step < KEPT_CHUNKS:
            pl.when(jnp.logical_not(has_left))(lambda: kept_copy(0, step, x_ref).start())
            pl.when(jnp.logical_not(has_right))(lambda: kept_copy(1, step, x_ref).start())
        from_first = step - place
        from_last = step - (lines - 1 - place)

        @pl.when(has_left & (from_first >= 0) & (from_first < KEPT_CHUNKS))
        def _():
            kept_copy(0, from_first).wait_recv()

            @pl.when(has_right)
            def _():
                span = kept_span(from_first)
                to_right[span] = x_ref[span] + from_left[span]
                kept_copy(0, from_first).start()

        @pl.when(has_right & (from_last >= 0) & (from_last < KEPT_CHUNKS))
        def _():
            kept_copy(1, from_last).wait_recv()

            @pl.when(has_left)
            def _():
                span = kept_span(from_last)
                to_left[span] = x_ref[span] + from_right[span]
                kept_copy(1, from_last).start()

    send_own(0)
    send_own(1)
    kept_steps = list(range(KEPT_CHUNKS + lines - 1))
    for at in range(GATHER_CHUNKS):
        ahead_copy(at).wait_recv()
        aside_copy(at).start()
        over_copy(at).start()
        pair_copy(1, at).start()
        if at + 2 < GATHER_CHUNKS:
            send_own(at + 2)
        for _ in range(2):
            if kept_steps:
                kept_step(kept_steps.pop(0))
        if at:
            aside_copy(at - 1).wait_recv()
            pair_copy(2, at - 1).start()
            over_copy(at - 1).wait_recv()
            pair_copy(3, at - 1).start()
    last = GATHER_CHUNKS - 1
    aside_copy(last).wait_recv()
    pair_copy(2, last).start()
    over_copy(last).wait_recv()
    pair_copy(3, last).start()
    for step in kept_steps:
        kept_step(step)

    @pl.when(jnp.logical_not(has_left))
    def _():
        o_ref[...] = x_ref[...] + from_right[...]
        for at in range(KEPT_CHUNKS):
            kept_copy(0, at, x_ref).wait_send()

    @pl.when(jnp.logical_not(has_right))
    def _():
        o_ref[...] = x_ref[...] + from_left[...]
        for at in range(KEPT_CHUNKS):
            kept_copy(1, at, x_ref).wait_send()

    @pl.when(has_left & has_right)
    def _():
        o_ref[...] = (x_ref[...] + from_left[...]) + from_right[...]
        for at in range(KEPT_CHUNKS):
            kept_copy(0, at).wait_send()
            kept_copy(1, at).wait_send()

    for at in range(GATHER_CHUNKS):
        keep_copy(at).wait()
        ahead_copy(at).wait_send()
        aside_copy(at).wait_send()
        over_copy(at).wait_send()
        for kind in range(4):
            pair_copy(kind, at).wait()


def start_gather(own_w, own_kept, collective_id):
    plane = lax.axis_size("fsdp")
    lines = lax.axis_size("seq")
    block, width = own_w.shape
    if plane != PLANE or block % (16 * GATHER_CHUNKS) or lines % 2:
        return lax.all_gather(own_w, "fsdp", axis=0, tiled=True), line_sum(
            own_kept, KEPT_CHUNKS, collective_id
        )
    buffer = pltpu.VMEM(own_kept.shape, own_kept.dtype)
    dma = pltpu.SemaphoreType.DMA
    return pl.pallas_call(
        partial(start_kernel, lines),
        out_shape=[
            jax.ShapeDtypeStruct((PLANE * block, width), own_w.dtype),
            jax.ShapeDtypeStruct(own_kept.shape, own_kept.dtype),
        ],
        in_specs=[pl.BlockSpec(memory_space=pl.ANY), pl.BlockSpec(memory_space=pltpu.VMEM)],
        out_specs=[pl.BlockSpec(memory_space=pl.ANY), pl.BlockSpec(memory_space=pltpu.VMEM)],
        scratch_shapes=[buffer] * 4
        + [
            dma((GATHER_CHUNKS,)),
            dma((2, 3, GATHER_CHUNKS)),
            dma((2, 4, GATHER_CHUNKS)),
            dma((2, KEPT_CHUNKS)),
            dma((2, KEPT_CHUNKS)),
        ],
        compiler_params=pltpu.CompilerParams(
            collective_id=collective_id, has_side_effects=True, vmem_limit_bytes=VMEM_LIMIT
        ),
        cost_estimate=pl.CostEstimate(
            flops=0, bytes_accessed=200 * 1024 * 1024, transcendentals=0
        ),
    )(own_w, own_kept)


def line_sum(block, chunks, collective_id):
    shape = jax.ShapeDtypeStruct(block.shape, block.dtype)
    buffer = pltpu.VMEM(block.shape, block.dtype)
    return pl.pallas_call(
        partial(line_sum_kernel, chunks, lax.axis_size("seq")),
        out_shape=shape,
        in_specs=[pl.BlockSpec(memory_space=pltpu.VMEM)],
        out_specs=pl.BlockSpec(memory_space=pltpu.VMEM),
        scratch_shapes=[buffer] * 4
        + [pltpu.SemaphoreType.DMA((2, chunks)), pltpu.SemaphoreType.DMA((2, chunks))],
        compiler_params=pltpu.CompilerParams(
            collective_id=collective_id, has_side_effects=True, vmem_limit_bytes=VMEM_LIMIT
        ),
        cost_estimate=pl.CostEstimate(
            flops=0, bytes_accessed=100 * block.size, transcendentals=0
        ),
    )(block)


SMALL_BLOCK = (8, 384)
PLANE = 8


def exchange_kernel(
    table,
    extra,
    g_early,
    g_late,
    small_ref,
    dec_ref,
    head_ref,
    out_early,
    out_late,
    small_out,
    dec_out,
    head_out,
    pair_early,
    pair_late,
    send_early,
    send_late,
    recv_early,
    recv_late,
    small_in,
    small_line,
    dec_pair,
    dec_send,
    dec_recv,
    dec_sum,
    dec_line,
    dec_pair_sems,
    dec_plane_sems,
    dec_split_sems,
    dec_line_sems,
    head_sems,
    pair_sems,
    plane_sems,
    line_sems,
    small_plane_sems,
    small_line_sems,
    small_out_sems,
):
    own = lax.axis_index("fsdp")
    place = lax.axis_index("seq")
    line = lax.axis_size("seq")
    core = lax.rem(own, 2)
    chip = lax.div(own, 2)
    partner = own + 1 - 2 * core
    grads = (g_early, g_late)
    pair_ins = (pair_early, pair_late)
    sends = (send_early, send_late)
    recvs = (recv_early, recv_late)
    outs = (out_early, out_late)
    block = g_early.shape[0] // PLANE
    order = range(len(table))

    def plane_peer(step):
        return lax.rem(own + step, PLANE)

    def line_peer(step):
        return lax.rem(place + step, line)

    barrier = pltpu.get_barrier_semaphore()
    for step in range(1, PLANE):
        pl.semaphore_signal(
            barrier, inc=1, device_id={"fsdp": plane_peer(step)}, device_id_type=MESH
        )
    for step in range(1, line):
        pl.semaphore_signal(
            barrier, inc=1, device_id={"seq": line_peer(step)}, device_id_type=MESH
        )
    pl.semaphore_wait(barrier, PLANE - 1 + line - 1)

    def send(source, target, sems, at, device):
        return pltpu.make_async_remote_copy(
            src_ref=source,
            dst_ref=target,
            send_sem=sems.at[(0,) + at],
            recv_sem=sems.at[(1,) + at],
            device_id=device,
            device_id_type=MESH,
        )

    def span_of(at):
        return pl.ds(table[at][1], table[at][2])

    def owned_rows(owner, at):
        start, rows = table[at][1:]
        return pl.ds(pl.multiple_of(owner * block + start, 16), rows)

    def pair_copy(other, at):
        part = table[at][0]
        target = lax.rem(chip + other, 4)
        return send(
            grads[part].at[owned_rows(2 * target + 1 - core, at)],
            pair_ins[part].at[other, span_of(at)],
            pair_sems,
            (other, at),
            {"fsdp": partner},
        )

    def plane_copy(other, at):
        part = table[at][0]
        target = lax.rem(chip + other, 4)
        return send(
            sends[part].at[other - 1, span_of(at)],
            recvs[part].at[other - 1, span_of(at)],
            plane_sems,
            (other - 1, at),
            {"fsdp": 2 * target + core},
        )

    def line_copy(step, at):
        part = outs[table[at][0]].at[place, span_of(at)]
        return send(part, part, line_sems, (step - 1, at), {"seq": line_peer(step)})

    def small_plane_copy(step):
        return send(
            small_ref.at[plane_peer(step)],
            small_in.at[step - 1],
            small_plane_sems,
            (step - 1,),
            {"fsdp": plane_peer(step)},
        )

    def small_line_copy(step):
        part = small_line.at[place]
        return send(part, part, small_line_sems, (step - 1,), {"seq": line_peer(step)})

    def small_out_copy(step):
        part = small_out.at[own]
        return send(part, part, small_out_sems, (step - 1,), {"fsdp": plane_peer(step)})

    dec_rows = dec_ref.shape[0] // PLANE
    dec_part = dec_rows // line

    def dec_span(owner):
        return pl.ds(pl.multiple_of(owner * dec_rows, 16), dec_rows)

    def dec_pair_copy(other):
        target = lax.rem(chip + other, 4)
        return send(
            dec_ref.at[dec_span(2 * target + 1 - core)],
            dec_pair.at[other],
            dec_pair_sems,
            (other,),
            {"fsdp": partner},
        )

    def dec_plane_copy(other):
        target = lax.rem(chip + other, 4)
        return send(
            dec_send.at[other - 1],
            dec_recv.at[other - 1],
            dec_plane_sems,
            (other - 1,),
            {"fsdp": 2 * target + core},
        )

    def quarter_of(at):
        return pl.ds(pl.multiple_of(at * dec_part, 16), dec_part)

    def dec_split_copy(step):
        to = line_peer(step)
        return send(
            dec_sum.at[quarter_of(to)],
            dec_line.at[place],
            dec_split_sems,
            (step - 1,),
            {"seq": to},
        )

    def dec_line_copy(step):
        part = dec_out.at[quarter_of(place)]
        return send(part, part, dec_line_sems, (step - 1,), {"seq": line_peer(step)})

    head_rows = head_ref.shape[0]

    def head_copy(step):
        target = head_out.at[pl.ds(pl.multiple_of(own * head_rows, 16), head_rows)]
        return send(head_ref, target, head_sems, (step - 1,), {"fsdp": plane_peer(step)})

    for other in (1, 2, 3, 0):
        dec_pair_copy(other).start()
    for at in order:
        for other in (1, 2, 3, 0):
            pair_copy(other, at).start()
        if at == 0:
            for step in range(1, PLANE):
                small_plane_copy(step).start()
    for other in (1, 2, 3, 0):
        dec_pair_copy(other).wait_recv()
        if other:
            target = lax.rem(chip + other, 4)
            dec_send[other - 1] = dec_ref[dec_span(2 * target + core)] + dec_pair[other]
            dec_plane_copy(other).start()
    for at in order:
        part = table[at][0]
        for other in (1, 2, 3, 0):
            pair_copy(other, at).wait_recv()
            if other:
                target = lax.rem(chip + other, 4)
                mine = grads[part][owned_rows(2 * target + core, at)]
                sends[part][other - 1, span_of(at)] = low(mine + pair_ins[part][other, span_of(at)])
                plane_copy(other, at).start()
    for step in range(1, PLANE):
        small_plane_copy(step).wait_recv()
    total = small_ref[own]
    for step in range(1, PLANE):
        total = total + small_in[step - 1]
    small_line[place] = total
    for step in range(1, line):
        small_line_copy(step).start()
    total = dec_ref[dec_span(own)] + dec_pair[0]
    for other in (1, 2, 3):
        dec_plane_copy(other).wait_recv()
        total = total + dec_recv[other - 1]
    dec_sum[...] = total
    for step in range(1, line):
        dec_split_copy(step).start()
    for step in range(1, PLANE):
        head_copy(step).start()
    head_out[pl.ds(pl.multiple_of(own * head_rows, 16), head_rows)] = head_ref[...]
    for at in order:
        part = table[at][0]
        total = grads[part][owned_rows(own, at)] + pair_ins[part][0, span_of(at)]
        for other in (1, 2, 3):
            plane_copy(other, at).wait_recv()
            total = total + recvs[part][other - 1, span_of(at)].astype(jnp.float32)
        rounded = low(total)
        if part == 0:
            rest = total[:, -extra:] - rounded[:, -extra:].astype(jnp.float32)
            rounded = jnp.concatenate([rounded, low(rest)], axis=1)
        outs[part][place, span_of(at)] = rounded
        for step in range(1, line):
            line_copy(step, at).start()
        if at == 0:
            dec_line[place] = dec_sum[quarter_of(place)]
            for step in range(1, line):
                dec_split_copy(step).wait_recv()
            total = dec_line[0]
            for other in range(1, dec_line.shape[0]):
                total = total + dec_line[other]
            dec_out[quarter_of(place)] = total
            for step in range(1, line):
                dec_line_copy(step).start()
    for step in range(1, line):
        small_line_copy(step).wait_recv()
    total = small_line[0]
    for at in range(1, small_line.shape[0]):
        total = total + small_line[at]
    small_out[own] = total
    for step in range(1, PLANE):
        small_out_copy(step).start()
    for step in range(1, PLANE):
        small_out_copy(step).wait()
        small_plane_copy(step).wait_send()
        head_copy(step).wait()
    for other in range(4):
        dec_pair_copy(other).wait_send()
        if other:
            dec_plane_copy(other).wait_send()
    for step in range(1, line):
        dec_split_copy(step).wait_send()
        dec_line_copy(step).wait()
        small_line_copy(step).wait_send()
        for at in order:
            line_copy(step, at).wait()
    for at in order:
        for other in range(4):
            pair_copy(other, at).wait_send()
            if other:
                plane_copy(other, at).wait_send()


def exchange(early, late, small, dec, head_own, line, extra, collective_id):
    plane = lax.axis_size("fsdp")
    total = early.shape[0]
    dec_rows = dec.shape[0] // plane
    if plane != PLANE or total % (PLANE * 48) or dec_rows % (16 * line):
        results = []
        for part, rest in ((early, extra), (late, 0)):
            own = lax.psum_scatter(part, "fsdp", scatter_dimension=0, tiled=True)
            rounded = low(own)
            if rest:
                left = own[:, -rest:] - rounded[:, -rest:].astype(jnp.float32)
                rounded = jnp.concatenate([rounded, low(left)], axis=1)
            results.append(lax.all_gather(rounded, "seq", axis=0, tiled=False))
        dec_sum = lax.psum(
            lax.psum_scatter(dec, "fsdp", scatter_dimension=0, tiled=True), "seq"
        )
        head_all = lax.all_gather(head_own, "fsdp", axis=0, tiled=True)
        return results[0], results[1], lax.psum(small, ("fsdp", "seq")), dec_sum, head_all
    block = total // PLANE
    third = block // 3
    table = tuple((0, at * third, third) for at in range(3)) + ((1, 0, block),)
    widths = (early.shape[1], late.shape[1])
    padded = PLANE * SMALL_BLOCK[0] * SMALL_BLOCK[1]
    blocks = jnp.pad(small, (0, padded - small.shape[0])).reshape((PLANE,) + SMALL_BLOCK)
    dma = pltpu.SemaphoreType.DMA
    low_type, f32 = jnp.bfloat16, jnp.float32
    dec_cols = dec.shape[1]
    first, second, summed, dec_sum, head_all = pl.pallas_call(
        partial(exchange_kernel, table, extra),
        out_shape=[
            jax.ShapeDtypeStruct((line, block, widths[0] + extra), low_type),
            jax.ShapeDtypeStruct((line, block, widths[1]), low_type),
            jax.ShapeDtypeStruct(blocks.shape, f32),
            jax.ShapeDtypeStruct((dec_rows, dec_cols), f32),
            jax.ShapeDtypeStruct((PLANE * head_own.shape[0], head_own.shape[1]), f32),
        ],
        in_specs=[pl.BlockSpec(memory_space=pltpu.VMEM)] * 5,
        out_specs=[pl.BlockSpec(memory_space=pltpu.VMEM)] * 5,
        scratch_shapes=[pltpu.VMEM((4, block, width), f32) for width in widths]
        + [pltpu.VMEM((3, block, width), low_type) for width in widths * 2]
        + [
            pltpu.VMEM((PLANE - 1,) + SMALL_BLOCK, f32),
            pltpu.VMEM((line,) + SMALL_BLOCK, f32),
            pltpu.VMEM((4, dec_rows, dec_cols), f32),
            pltpu.VMEM((3, dec_rows, dec_cols), f32),
            pltpu.VMEM((3, dec_rows, dec_cols), f32),
            pltpu.VMEM((dec_rows, dec_cols), f32),
            pltpu.VMEM((line, dec_rows // line, dec_cols), f32),
            dma((2, 4)),
            dma((2, 3)),
            dma((2, line - 1)),
            dma((2, line - 1)),
            dma((2, PLANE - 1)),
            dma((2, 4, len(table))),
            dma((2, 3, len(table))),
            dma((2, line - 1, len(table))),
            dma((2, PLANE - 1)),
            dma((2, line - 1)),
            dma((2, PLANE - 1)),
        ],
        compiler_params=pltpu.CompilerParams(
            collective_id=collective_id, has_side_effects=True, vmem_limit_bytes=VMEM_LIMIT
        ),
        cost_estimate=pl.CostEstimate(
            flops=0, bytes_accessed=200 * 1024 * 1024, transcendentals=0
        ),
    )(early, late, blocks, dec, head_own)
    return first, second, summed.reshape(-1), dec_sum, head_all


def gelu_parts(hidden):
    cdf = 0.5 * (1.0 + lax.erf(hidden * (2.0**-0.5)))
    density = jnp.exp(-0.5 * hidden * hidden) * (0.3989422804014327)
    return hidden * cdf, cdf + hidden * density


NT = ((1,), (1,))


def norm_rows(rows):
    centre = rows - jnp.mean(rows, axis=-1, keepdims=True)
    inverse = lax.rsqrt(jnp.mean(centre * centre, axis=-1, keepdims=True) + NORM_EPS)
    return centre * inverse, inverse


def norm_rows_back(upstream, scaled, inverse, gain):
    weighted = upstream * gain
    inner = (
        weighted
        - jnp.mean(weighted, axis=-1, keepdims=True)
        - scaled * jnp.mean(weighted * scaled, axis=-1, keepdims=True)
    )
    return inverse * inner, column_sum(upstream * scaled), column_sum(upstream)


def column_sum(rows):
    return jnp.sum(rows, axis=0, keepdims=True)


def clear_first(refs):
    @pl.when(pl.program_id(0) == 0)
    def _():
        for ref in refs:
            ref[...] = jnp.zeros_like(ref)


def dec_middle_kernel(
    grad_scale,
    o_ref,
    y_ref,
    pixel_ref,
    masked_ref,
    out_w,
    up_w,
    down_w,
    head_w,
    vec_ref,
    bu_ref,
    bh_ref,
    do_ref,
    dmid_ref,
    grad_ref,
    vec_grad,
    bu_grad,
    bh_grad,
    slope_ref,
    act_ref,
):
    clear_first((grad_ref, vec_grad, bu_grad, bh_grad))
    bo, gain2, shift2, bd, gain3, shift3 = (vec_ref[i : i + 1, :] for i in range(6))
    attended = o_ref[0]
    middle = y_ref[0] + dot_f32(attended, out_w[...], NN) + bo
    scaled2, inverse2 = norm_rows(middle)
    second = low(scaled2 * gain2 + shift2)
    size = 512
    decoded = middle + bd
    for at in range(0, FF_D, size):
        span = slice(at, at + size)
        value, slope = gelu_parts(dot_f32(second, up_w[:, span], NN) + bu_ref[:, span])
        slope_ref[:, span] = slope
        act_ref[:, span] = low(value)
        decoded = decoded + dot_f32(act_ref[:, span], down_w[:, span], NT)
    scaled3, inverse3 = norm_rows(decoded)
    third = low(scaled3 * gain3 + shift3)
    predicted = dot_f32(third, head_w[...], NN) + bh_ref[...]
    pixel = pixel_ref[0].astype(jnp.float32)
    centre = pixel - jnp.mean(pixel, axis=-1, keepdims=True)
    target = centre * lax.rsqrt(
        jnp.sum(centre * centre, axis=-1, keepdims=True) / (PIX - 1) + PIXEL_EPS
    )
    masked = masked_ref[0][:, :1]
    error = (predicted - target) * masked
    pred_grad = error * grad_scale
    pred_low = low(pred_grad)
    bh_grad[0:1, :] += column_sum(pred_grad)
    bh_grad[1:2, :] += column_sum(error * error)
    o_span, u_span = D_D, D_D + FF_D
    h_span = D_D + 2 * FF_D
    grad_ref[:, h_span:] += dot_f32(third, pred_low, TN)
    up3, g_gain3, g_shift3 = norm_rows_back(
        dot_f32(pred_low, head_w[...], NT), scaled3, inverse3, gain3
    )
    up3_low = low(up3)
    back = jnp.zeros_like(up3)
    for at in range(0, FF_D, size):
        span = slice(at, at + size)
        hidden_grad = low(dot_f32(up3_low, down_w[:, span], NN) * slope_ref[:, span])
        grad_ref[:, u_span + at : u_span + at + size] += dot_f32(up3_low, act_ref[:, span], TN)
        grad_ref[:, o_span + at : o_span + at + size] += dot_f32(second, hidden_grad, TN)
        bu_grad[0:1, span] += column_sum(hidden_grad.astype(jnp.float32))
        back = back + dot_f32(hidden_grad, up_w[:, span], NT)
    through, g_gain2, g_shift2 = norm_rows_back(back, scaled2, inverse2, gain2)
    middle_grad = up3 + through
    middle_low = low(middle_grad)
    dmid_ref[0] = middle_grad
    grad_ref[:, :o_span] += dot_f32(attended, middle_low, TN)
    do_ref[0] = low(dot_f32(middle_low, out_w[...], NT))
    sums = (column_sum(middle_grad), g_gain2, g_shift2, column_sum(up3), g_gain3, g_shift3)
    for at, part in enumerate(sums):
        vec_grad[at : at + 1, :] += part


def whole(shape):
    return pl.BlockSpec(shape, lambda i: (0,) * len(shape), pipeline_mode=pl.Buffered(1))


def columns(rows, width, at):
    return pl.BlockSpec((rows, width), lambda i: (0, at), pipeline_mode=pl.Buffered(1))


def per_image(rows, width):
    return pl.BlockSpec((1, rows, width), lambda i: (i, 0, 0))


def dec_middle(attended, y_own, pixels, masked, dec_full, head_low, vectors, bu, bh, grad_scale):
    images, rows, _ = attended.shape
    f32 = jnp.float32
    return pl.pallas_call(
        partial(dec_middle_kernel, grad_scale),
        grid=(images,),
        in_specs=[
            per_image(rows, D_D),
            per_image(rows, D_D),
            per_image(rows, PIX),
            per_image(rows, 128),
            columns(D_D, D_D, 3),
            columns(D_D, FF_D, 1),
            columns(D_D, FF_D, 2),
            whole((D_D, PIX)),
            whole((8, D_D)),
            whole((1, FF_D)),
            whole((1, PIX)),
        ],
        out_specs=[
            per_image(rows, D_D),
            per_image(rows, D_D),
            whole((D_D, D_D + 2 * FF_D + PIX)),
            whole((8, D_D)),
            whole((8, FF_D)),
            whole((8, PIX)),
        ],
        out_shape=[
            jax.ShapeDtypeStruct((images, rows, D_D), jnp.bfloat16),
            jax.ShapeDtypeStruct((images, rows, D_D), f32),
            jax.ShapeDtypeStruct((D_D, D_D + 2 * FF_D + PIX), f32),
            jax.ShapeDtypeStruct((8, D_D), f32),
            jax.ShapeDtypeStruct((8, FF_D), f32),
            jax.ShapeDtypeStruct((8, PIX), f32),
        ],
        scratch_shapes=[pltpu.VMEM((rows, FF_D), f32), pltpu.VMEM((rows, FF_D), jnp.bfloat16)],
        compiler_params=pltpu.CompilerParams(vmem_limit_bytes=44 * 1024 * 1024),
        cost_estimate=pl.CostEstimate(
            flops=12 * images * rows * D_D * (D_D + 2 * FF_D + PIX),
            bytes_accessed=30 * 1024 * 1024,
            transcendentals=2 * images * rows * FF_D,
        ),
    )(
        attended, y_own, pixels, masked, dec_full, dec_full, dec_full, head_low, vectors, bu, bh
    )


def dec_entry_kernel(e_ref, rank_ref, place_ref, q_w, k_w, v_w, vec_ref, y_ref, q_ref, k_ref, v_ref):
    mask_token, gain, shift, bq, bv = (vec_ref[i : i + 1, :] for i in range(5))
    ranks = jnp.broadcast_to(rank_ref[0], (E_ROWS, PATCHES))
    at = lax.broadcasted_iota(jnp.int32, (E_ROWS, PATCHES), 0)
    hidden = (at >= KEEP) & (at < KEEP + 3) & (ranks >= KEEP)
    pick = low(jnp.where(((at == ranks) & (at < KEEP)) | hidden, 1.0, 0.0))
    place = lax.broadcasted_iota(jnp.int32, (TAIL, D_D), 0)
    token = jnp.zeros((TAIL, D_D), jnp.float32)
    for row, part in enumerate(pieces_of(mask_token)):
        token = jnp.where(place == row, part, token)
    source = jnp.concatenate([e_ref[0, :KEEP], low(token)], axis=0)
    y_ref[0, :PATCHES] = dot_f32(pick, source, TN) + place_ref[...]
    cls = column_sum(jnp.where(place == 0, e_ref[0, KEEP:].astype(jnp.float32), 0.0))
    y_ref[0, PATCHES:] = tail_rows(cls)
    scaled, _ = norm_rows(y_ref[0])
    normed = low(scaled * gain + shift)
    q_ref[0] = low(dot_f32(normed[: q_ref.shape[1]], q_w[...], NN) + bq)
    k_ref[0] = low(dot_f32(normed, k_w[...], NN))
    v_ref[0] = low(dot_f32(normed, v_w[...], NN) + bv)


def dec_entry(shrunk, ranks, placed, dec_full, vectors, own):
    images = shrunk.shape[0]
    kinds = [(D_ROWS, jnp.float32), (own, jnp.bfloat16), (D_ROWS, jnp.bfloat16)]
    kinds.append(kinds[2])
    return pl.pallas_call(
        dec_entry_kernel,
        grid=(images,),
        in_specs=[
            per_image(E_ROWS, D_D),
            per_image(1, PATCHES),
            whole((PATCHES, D_D)),
            columns(D_D, D_D, 0),
            columns(D_D, D_D, 1),
            columns(D_D, D_D, 2),
            whole((8, D_D)),
        ],
        out_specs=[per_image(rows, D_D) for rows, _ in kinds],
        out_shape=[jax.ShapeDtypeStruct((images, rows, D_D), kind) for rows, kind in kinds],
        compiler_params=pltpu.CompilerParams(vmem_limit_bytes=44 * 1024 * 1024),
        cost_estimate=pl.CostEstimate(
            flops=4 * images * D_ROWS * D_D * D_D * 2,
            bytes_accessed=20 * 1024 * 1024,
            transcendentals=0,
        ),
    )(shrunk, ranks, placed, dec_full, dec_full, dec_full, vectors)


def dec_entry_back_kernel(
    y_ref,
    dq_ref,
    dk_ref,
    dv_ref,
    dmid_ref,
    rank_ref,
    q_w,
    k_w,
    v_w,
    vec_ref,
    de_ref,
    grad_ref,
    vec_grad,
    cls_ref,
):
    image = pl.program_id(0)
    clear_first((grad_ref, vec_grad, cls_ref))
    gain, shift = vec_ref[0:1, :], vec_ref[1:2, :]
    scaled, inverse = norm_rows(y_ref[0])
    normed = low(scaled * gain + shift)
    dq, dk, dv = dq_ref[0], dk_ref[0], dv_ref[0]
    own = dq.shape[0]
    grad_ref[:, :D_D] += dot_f32(normed[:own], dq, TN)
    grad_ref[:, D_D : 2 * D_D] += dot_f32(normed, dk, TN)
    grad_ref[:, 2 * D_D :] += dot_f32(normed, dv, TN)
    up = dot_f32(dk, k_w[...], NT) + dot_f32(dv, v_w[...], NT)
    up = jnp.concatenate([up[:own] + dot_f32(dq, q_w[...], NT), up[own:]], axis=0)
    back, g_gain, g_shift = norm_rows_back(up, scaled, inverse, gain)
    back = jnp.concatenate([back[:own] + dmid_ref[0], back[own:]], axis=0)
    patches = back[:PATCHES]
    high = low(patches)
    rest = low(patches - high.astype(jnp.float32))
    ranks = rank_ref[0]
    at = lax.broadcasted_iota(jnp.int32, (KEEP, PATCHES), 0)
    pick = low(jnp.where(at == ranks, 1.0, 0.0))
    hidden = low(jnp.where(jnp.broadcast_to(ranks, (16, PATCHES)) >= KEEP, 1.0, 0.0))
    de_ref[pl.ds(pl.multiple_of(image * KEEP, KEEP), KEEP)] = low(dot_f32(pick, high, NN))
    g_mask = dot_f32(hidden, high, NN) + dot_f32(hidden, rest, NN)
    cls_ref[pl.ds(image, 1), :] = back[PATCHES : PATCHES + 1]
    sums = (
        g_mask[0:1],
        g_shift,
        column_sum(dq.astype(jnp.float32)),
        column_sum(dv.astype(jnp.float32)),
        g_gain,
    )
    for at, part in enumerate(sums):
        vec_grad[at : at + 1, :] += part

    @pl.when(image == pl.num_programs(0) - 1)
    def _():
        de_ref[de_ref.shape[0] - TAIL :] = low(cls_ref[...])


def dec_entry_back(y0, dq, dk, dv, dmid, ranks, dec_full, vectors):
    images, rows, _ = y0.shape
    own = dq.shape[1]
    f32 = jnp.float32
    return pl.pallas_call(
        dec_entry_back_kernel,
        grid=(images,),
        in_specs=[
            per_image(rows, D_D),
            per_image(own, D_D),
            per_image(rows, D_D),
            per_image(rows, D_D),
            per_image(own, D_D),
            per_image(1, PATCHES),
            columns(D_D, D_D, 0),
            columns(D_D, D_D, 1),
            columns(D_D, D_D, 2),
            whole((8, D_D)),
        ],
        out_specs=[whole((images * KEEP + TAIL, D_D)), whole((D_D, 3 * D_D)), whole((8, D_D))],
        out_shape=[
            jax.ShapeDtypeStruct((images * KEEP + TAIL, D_D), jnp.bfloat16),
            jax.ShapeDtypeStruct((D_D, 3 * D_D), f32),
            jax.ShapeDtypeStruct((8, D_D), f32),
        ],
        scratch_shapes=[pltpu.VMEM((TAIL, D_D), f32)],
        compiler_params=pltpu.CompilerParams(vmem_limit_bytes=44 * 1024 * 1024),
        cost_estimate=pl.CostEstimate(
            flops=12 * images * rows * D_D * D_D * 2,
            bytes_accessed=24 * 1024 * 1024,
            transcendentals=0,
        ),
    )(y0, dq, dk, dv, dmid, ranks, dec_full, dec_full, dec_full, vectors)


E_HEADS = 128 * H_E // D_E
E_DIM = D_E // H_E
E_OUT = 4 * D_E
E_UP = 5 * D_E
E_DOWN = E_UP + FF_E
E_EMBED = E_DOWN + FF_E
SIZE = 768


def tail_rows(first):
    at = lax.broadcasted_iota(jnp.int32, (TAIL, first.shape[1]), 0)
    return jnp.where(at == 0, first, 0.0)


def encoder_kernel(
    kept_ref,
    place_ref,
    w_ref,
    vec_ref,
    bu_ref,
    be_ref,
    x_ref,
    mid_ref,
    enc_ref,
    qkv_ref,
    lse_ref,
    o_ref,
    slope_ref,
    act_ref,
    e_ref,
):
    (gain1, gain2, gain3, cls, shift1, bq, bv, bo, shift2, bd, shift3) = (
        vec_ref[i : i + 1, :] for i in range(11)
    )
    rows = dot_f32(kept_ref[0], w_ref[:, :D_E], NN) + place_ref[0]
    x_ref[0] = jnp.concatenate([rows, tail_rows(cls)], axis=0)
    scaled, _ = norm_rows(x_ref[0])
    normed = low(scaled * gain1 + shift1)
    for at, bias in enumerate((bq, None, bv)):
        value = dot_f32(normed, w_ref[:, (at + 1) * D_E : (at + 2) * D_E], NN)
        qkv_ref[0, :, at * D_E : (at + 1) * D_E] = low(value if bias is None else value + bias)
    for group in range(D_E // 128):
        parts = [
            qkv_ref[0, :, at * D_E + group * 128 : at * D_E + (group + 1) * 128] for at in range(3)
        ]
        out, sums = attend_forward_group(E_HEADS, E_DIM, *parts)
        o_ref[0, :, group * 128 : (group + 1) * 128] = out
        for head in range(E_HEADS):
            at = group * E_HEADS + head
            lse_ref[0, at : at + 1, :] = sums[head]
    middle = x_ref[0] + dot_f32(o_ref[0], w_ref[:, E_OUT:E_UP], NN) + bo
    mid_ref[0] = middle
    scaled, _ = norm_rows(middle)
    second = low(scaled * gain2 + shift2)
    encoded = middle + bd
    for at in range(0, FF_E, SIZE):
        span = slice(at, at + SIZE)
        hidden = dot_f32(second, w_ref[:, E_UP + at : E_UP + at + SIZE], NN) + bu_ref[:, span]
        value, slope = gelu_parts(hidden)
        slope_ref[0, :, span] = slope
        act_ref[0, :, span] = low(value)
        encoded = encoded + dot_f32(
            act_ref[0, :, span], w_ref[:, E_DOWN + at : E_DOWN + at + SIZE], NT
        )
    enc_ref[0] = encoded
    scaled, _ = norm_rows(encoded)
    third = low(scaled * gain3 + shift3)
    e_ref[0] = low(dot_f32(third, w_ref[:, E_EMBED:], NN) + be_ref[...])


def encoder(kept, placed, enc_full, vectors, bu, be):
    images = kept.shape[0]
    f32, low_type = jnp.float32, jnp.bfloat16
    shapes = [
        ((E_ROWS, D_E), f32),
        ((E_ROWS, D_E), f32),
        ((E_ROWS, D_E), f32),
        ((E_ROWS, 3 * D_E), low_type),
        ((H_E, E_ROWS), f32),
        ((E_ROWS, D_E), low_type),
        ((E_ROWS, FF_E), f32),
        ((E_ROWS, FF_E), low_type),
        ((E_ROWS, D_D), low_type),
    ]
    return pl.pallas_call(
        encoder_kernel,
        grid=(images,),
        in_specs=[
            per_image(KEEP, D_E),
            per_image(KEEP, D_E),
            whole(enc_full.shape),
            whole((16, D_E)),
            whole((1, FF_E)),
            whole((1, D_D)),
        ],
        out_specs=[per_image(*shape) for shape, _ in shapes],
        out_shape=[jax.ShapeDtypeStruct((images,) + shape, kind) for shape, kind in shapes],
        compiler_params=pltpu.CompilerParams(vmem_limit_bytes=KERNEL_LIMIT),
        cost_estimate=pl.CostEstimate(
            flops=2 * images * E_ROWS * enc_full.size,
            bytes_accessed=40 * 1024 * 1024,
            transcendentals=2 * images * E_ROWS * FF_E,
        ),
    )(kept, placed, enc_full, vectors, bu, be)


def turn_quarter(value, place):
    width = value.shape[1]
    quarter = width // 4
    turned = pltpu.roll(value, lax.rem(width - quarter * place, width), axis=1)
    return low(turned[:, :quarter])


def encoder_back_kernel(
    place_ref,
    de_ref,
    cls_ref,
    mid_ref,
    enc_ref,
    o_ref,
    slope_ref,
    act_ref,
    w_ref,
    vec_ref,
    do_ref,
    dmid_ref,
    grad_ref,
    vec_grad,
    bu_grad,
    be_grad,
    de_all,
    hidden_all,
):
    image = pl.program_id(0)
    place = place_ref[0]
    clear_first((grad_ref, vec_grad, bu_grad, be_grad))
    gain2, gain3, shift2, shift3 = (vec_ref[i : i + 1, :] for i in range(4))
    at = lax.broadcasted_iota(jnp.int32, (TAIL, D_D), 0)
    cls = column_sum(jnp.where(at == image, cls_ref[...].astype(jnp.float32), 0.0))
    de_all[:KEEP] = de_ref[...]
    de_all[KEEP:] = low(tail_rows(cls))
    de = de_all[...]
    be_grad[0:1, :] += column_sum(de.astype(jnp.float32))
    scaled3, inverse3 = norm_rows(enc_ref[0])
    third = low(scaled3 * gain3 + shift3)
    quarter = FF_E // 4
    first = D_E // 4
    small = D_D // 4
    grad_ref[:, first + 2 * quarter :] += dot_f32(
        third, de_all[:, pl.ds(pl.multiple_of(place * small, small), small)], TN
    )
    up3, g_gain3, g_shift3 = norm_rows_back(
        dot_f32(de, w_ref[:, E_EMBED:], NT), scaled3, inverse3, gain3
    )
    up3_low = low(up3)
    scaled2, inverse2 = norm_rows(mid_ref[0])
    second = low(scaled2 * gain2 + shift2)
    own_hidden = pl.ds(pl.multiple_of(place * quarter, quarter), quarter)
    back = jnp.zeros_like(up3)
    for at in range(0, FF_E, SIZE):
        span = slice(at, at + SIZE)
        hidden = dot_f32(up3_low, w_ref[:, E_DOWN + at : E_DOWN + at + SIZE], NN)
        hidden = low(hidden * slope_ref[0, :, span])
        hidden_all[:, span] = hidden
        bu_grad[0:1, span] += column_sum(hidden.astype(jnp.float32))
        back = back + dot_f32(hidden, w_ref[:, E_UP + at : E_UP + at + SIZE], NT)
    grad_ref[:, first : first + quarter] += dot_f32(second, hidden_all[:, own_hidden], TN)
    grad_ref[:, first + quarter : first + 2 * quarter] += dot_f32(
        up3_low, act_ref[0, :, own_hidden], TN
    )
    through, g_gain2, g_shift2 = norm_rows_back(back, scaled2, inverse2, gain2)
    middle_grad = up3 + through
    dmid_ref[0] = middle_grad
    grad_ref[:, :first] += dot_f32(o_ref[0], turn_quarter(middle_grad, place), TN)
    do_ref[0] = low(dot_f32(low(middle_grad), w_ref[:, E_OUT:E_UP], NT))
    sums = (column_sum(middle_grad), g_shift2, column_sum(up3), g_shift3, g_gain2, g_gain3)
    for at, part in enumerate(sums):
        vec_grad[at : at + 1, :] += part


def scalar_spec():
    return pl.BlockSpec(memory_space=pltpu.SMEM)


def encoder_back(place, de_sum, saved, enc_full, vectors):
    mid, enc, o, slope, act = saved
    images = mid.shape[0]
    f32 = jnp.float32
    width = D_E // 4 + FF_E // 2 + D_D // 4
    return pl.pallas_call(
        encoder_back_kernel,
        grid=(images,),
        in_specs=[
            scalar_spec(),
            pl.BlockSpec((KEEP, D_D), lambda i: (i, 0)),
            pl.BlockSpec((TAIL, D_D), lambda i: (images * KEEP // TAIL, 0)),
            per_image(E_ROWS, D_E),
            per_image(E_ROWS, D_E),
            per_image(E_ROWS, D_E),
            per_image(E_ROWS, FF_E),
            per_image(E_ROWS, FF_E),
            whole(enc_full.shape),
            whole((8, D_E)),
        ],
        out_specs=[
            per_image(E_ROWS, D_E),
            per_image(E_ROWS, D_E),
            whole((D_E, width)),
            whole((8, D_E)),
            whole((8, FF_E)),
            whole((8, D_D)),
        ],
        out_shape=[
            jax.ShapeDtypeStruct((images, E_ROWS, D_E), jnp.bfloat16),
            jax.ShapeDtypeStruct((images, E_ROWS, D_E), f32),
            jax.ShapeDtypeStruct((D_E, width), f32),
            jax.ShapeDtypeStruct((8, D_E), f32),
            jax.ShapeDtypeStruct((8, FF_E), f32),
            jax.ShapeDtypeStruct((8, D_D), f32),
        ],
        scratch_shapes=[
            pltpu.VMEM((E_ROWS, D_D), jnp.bfloat16),
            pltpu.VMEM((E_ROWS, FF_E), jnp.bfloat16),
        ],
        compiler_params=pltpu.CompilerParams(vmem_limit_bytes=KERNEL_LIMIT),
        cost_estimate=pl.CostEstimate(
            flops=3 * images * E_ROWS * enc_full.size,
            bytes_accessed=50 * 1024 * 1024,
            transcendentals=0,
        ),
    )(place, de_sum, de_sum, mid, enc, o, slope, act, enc_full, vectors)


def encoder_entry_back_kernel(
    place_ref,
    kept_ref,
    x_ref,
    qkv_ref,
    lse_ref,
    o_ref,
    do_ref,
    dmid_ref,
    w_ref,
    vec_ref,
    grad_ref,
    vec_grad,
    dqkv_ref,
):
    place = place_ref[0]
    clear_first((grad_ref, vec_grad))
    gain1, shift1 = (vec_ref[i : i + 1, :] for i in range(2))
    for group in range(D_E // 128):
        span = slice(group * 128, (group + 1) * 128)
        parts = [
            qkv_ref[0, :, at * D_E + group * 128 : at * D_E + (group + 1) * 128] for at in range(3)
        ]
        sums = [
            lse_ref[0, group * E_HEADS + head : group * E_HEADS + head + 1, :]
            for head in range(E_HEADS)
        ]
        dq, dk, dv = attend_backward_group(
            E_HEADS, E_DIM, *parts, sums, do_ref[0, :, span], o_ref[0, :, span]
        )
        dqkv_ref[:, group * 128 : (group + 1) * 128] = dq
        for at, pair in ((1, dk), (2, dv)):
            lanes = slice(at * D_E + group * 128, at * D_E + (group + 1) * 128)
            dqkv_ref[:KEEP, lanes], dqkv_ref[KEEP:, lanes] = pair
    scaled, inverse = norm_rows(x_ref[0])
    normed = low(scaled * gain1 + shift1)
    quarter = D_E // 4
    sums = []
    for at in range(3):
        part = dqkv_ref[:, at * D_E : (at + 1) * D_E].astype(jnp.float32)
        if at != 1:
            sums.append(column_sum(part))
        grad_ref[:, (at + 1) * quarter : (at + 2) * quarter] += dot_f32(
            normed, turn_quarter(part, place), TN
        )
    through, g_gain1, g_shift1 = norm_rows_back(
        dot_f32(dqkv_ref[...], w_ref[:, D_E : 4 * D_E], NT), scaled, inverse, gain1
    )
    back = dmid_ref[0] + through
    patches = back[:KEEP]
    grad_ref[:, :quarter] += dot_f32(kept_ref[0], turn_quarter(patches, place), TN)
    sums = [column_sum(patches), back[KEEP : KEEP + 1], g_shift1] + sums + [g_gain1]
    for at, part in enumerate(sums):
        vec_grad[at : at + 1, :] += part


def encoder_entry_back(place, kept, saved, do, dmid, enc_full, vectors):
    x0, qkv, lse, o = saved
    images = kept.shape[0]
    f32 = jnp.float32
    return pl.pallas_call(
        encoder_entry_back_kernel,
        grid=(images,),
        in_specs=[
            scalar_spec(),
            per_image(KEEP, D_E),
            per_image(E_ROWS, D_E),
            per_image(E_ROWS, 3 * D_E),
            per_image(H_E, E_ROWS),
            per_image(E_ROWS, D_E),
            per_image(E_ROWS, D_E),
            per_image(E_ROWS, D_E),
            columns(D_E, 5 * D_E, 0),
            whole((8, D_E)),
        ],
        out_specs=[whole((D_E, D_E)), whole((8, D_E))],
        out_shape=[
            jax.ShapeDtypeStruct((D_E, D_E), f32),
            jax.ShapeDtypeStruct((8, D_E), f32),
        ],
        scratch_shapes=[pltpu.VMEM((E_ROWS, 3 * D_E), jnp.bfloat16)],
        compiler_params=pltpu.CompilerParams(vmem_limit_bytes=KERNEL_LIMIT),
        cost_estimate=pl.CostEstimate(
            flops=8 * images * E_ROWS * D_E * 4 * D_E,
            bytes_accessed=20 * 1024 * 1024,
            transcendentals=images * H_E * E_ROWS * E_ROWS,
        ),
    )(place, kept, x0, qkv, lse, o, do, dmid, enc_full, vectors)


def stack_rows(parts, count=8):
    rows = jnp.stack(parts)
    return jnp.pad(rows, ((0, count - len(parts)), (0, 0)))


def adamw(weight, moment_one, moment_two, gradient, step_rate, decay_rate):
    moment_one = BETA_ONE * moment_one + (1 - BETA_ONE) * gradient
    moment_two = BETA_TWO * moment_two + (1 - BETA_TWO) * gradient * gradient
    fixed_one = moment_one / (1 - BETA_ONE**STEP)
    fixed_two = moment_two / (1 - BETA_TWO**STEP)
    weight = weight - step_rate * (
        fixed_one / (jnp.sqrt(fixed_two) + ADAM_EPS) + decay_rate * weight
    )
    return (moment_one, moment_two, weight)


def enc_update_kernel(w_ref, m_ref, v_ref, early_ref, late_ref, m_out, v_out, w_out):
    lines = early_ref.shape[0]
    quarter_e, quarter_f, quarter_d = D_E // lines, FF_E // lines, D_D // lines
    pieces = [(late_ref, at * quarter_e, quarter_e) for at in range(4)]
    pieces += [
        (early_ref, 0, quarter_e),
        (early_ref, quarter_e, quarter_f),
        (early_ref, quarter_e + quarter_f, quarter_f),
        (early_ref, quarter_e + 2 * quarter_f, quarter_d),
    ]
    start = 0
    for number, (ref, offset, size) in enumerate(pieces):
        parts = [ref[at, :, offset : offset + size].astype(jnp.float32) for at in range(lines)]
        if number == len(pieces) - 1:
            rests = [ref[at, :, offset + size : offset + 2 * size] for at in range(lines)]
            parts = [a + b.astype(jnp.float32) for a, b in zip(parts, rests)]
        span = slice(start, start + lines * size)
        start += lines * size
        m_out[:, span], v_out[:, span], w_out[:, span] = adamw(
            w_ref[:, span],
            m_ref[:, span],
            v_ref[:, span],
            jnp.concatenate(parts, axis=1),
            MATRIX_RATE,
            MATRIX_DECAY,
        )


def enc_update(weight, moment_one, moment_two, early, late):
    rows, cols = weight.shape
    lines = early.shape[0]
    step = 16 if rows % 16 == 0 else rows
    plain = pl.BlockSpec((step, cols), lambda i: (i, 0))
    return pl.pallas_call(
        enc_update_kernel,
        grid=(rows // step,),
        in_specs=[plain] * 3
        + [
            pl.BlockSpec((lines, step, part.shape[2]), lambda i: (0, i, 0))
            for part in (early, late)
        ],
        out_specs=[plain] * 3,
        out_shape=[jax.ShapeDtypeStruct(weight.shape, jnp.float32)] * 3,
        compiler_params=pltpu.CompilerParams(vmem_limit_bytes=VMEM_LIMIT),
        cost_estimate=pl.CostEstimate(
            flops=20 * weight.size, bytes_accessed=26 * weight.size, transcendentals=0
        ),
    )(weight, moment_one, moment_two, early, late)


def shards(
    pixels,
    restore,
    enc_w,
    enc_m,
    enc_v,
    dec_w,
    dec_m,
    dec_v,
    head_w,
    head_m,
    head_v,
    gain_w,
    gain_m,
    gain_v,
    bias_w,
    bias_m,
    bias_v,
):
    seq_count = lax.axis_size("seq")
    place = lax.axis_index("seq")
    images, own_count, _ = pixels.shape
    masked_total = images * lax.axis_size("fsdp") * (PATCHES - KEEP)

    enc_low = low(enc_w)
    dec_full = lax.all_gather(low(dec_w), "fsdp", axis=0, tiled=True)
    head_low = low(head_w)

    pieces = split_vector(bias_w, bias_widths())
    gains = split_vector(gain_w, [D_E, D_E, D_E, D_D, D_D, D_D])
    (b_patch, cls_token, e_shift1, e_bq, e_bv, e_bo, e_shift2, e_bu, e_bd, e_shift3) = pieces[:10]
    (b_embed, mask_token, d_shift1, d_bq, d_bv, d_bo, d_shift2, d_bu, d_bd, d_shift3) = pieces[
        10:20
    ]
    b_head = pieces[20]

    ranks = jnp.arange(KEEP, dtype=jnp.int32)
    turned = lax.dynamic_slice_in_dim(
        jnp.concatenate([restore, restore], axis=1), place * own_count, PATCHES, axis=1
    )
    own_restore = turned[:, :own_count]
    own_pick = low(own_restore[:, None, :] == ranks[None, :, None])
    own_kept = jnp.einsum("irp,ipd->ird", own_pick, pixels, preferred_element_type=jnp.float32)
    enc_full, kept = start_gather(enc_low, low(own_kept).reshape(images * KEEP, PIX), 0)
    kept = kept.reshape(images, KEEP, PIX)
    patch_ids = jnp.arange(PATCHES, dtype=jnp.int32)
    keep_ids = jnp.sum(
        jnp.where(restore[:, None, :] == ranks[None, :, None], patch_ids, 0), axis=2
    )

    x0, e_mid, encoded, e_mixed, e_lse, e_o, e_slope, e_act, shrunk = encoder(
        kept,
        b_patch + positions(keep_ids, D_E),
        enc_full,
        stack_rows(
            gains[:3] + [cls_token, e_shift1, e_bq, e_bv, e_bo, e_shift2, e_bd, e_shift3], 16
        ),
        e_bu[None],
        b_embed[None],
    )

    turned_ids = lax.rem(patch_ids + place * own_count, PATCHES)
    ranks_row = turned[:, None, :]
    y0, d_q, d_k, d_v = dec_entry(
        shrunk,
        ranks_row,
        positions(turned_ids, D_D),
        dec_full,
        stack_rows([mask_token, gains[3], d_shift1, d_bq, d_bv]),
        own_count,
    )
    y0_own = y0[:, :own_count]
    d_o, d_lse = attend_forward(d_q, d_k, d_v, H_D)
    own_masked = (own_restore >= KEEP).astype(jnp.float32)
    own_masked = jnp.broadcast_to(own_masked[..., None], own_masked.shape + (128,))
    d_do, d_dmid, late_grads, mid_sums, bu_sums, bh_sums = dec_middle(
        d_o,
        y0_own,
        pixels,
        own_masked,
        dec_full,
        head_low,
        stack_rows([d_bo, gains[4], d_shift2, d_bd, gains[5], d_shift3]),
        d_bu[None],
        b_head[None],
        2.0 / (PIX * masked_total),
    )
    g_d_bo, g_d_gain2, g_d_shift2, g_d_bd, g_d_gain3, g_d_shift3 = (mid_sums[i] for i in range(6))
    g_d_bu = bu_sums[0]
    g_b_head = bh_sums[0]
    loss_part = jnp.sum(bh_sums[1]) / (PIX * masked_total)
    dec_late = lax.psum_scatter(late_grads, "fsdp", scatter_dimension=0, tiled=True)
    d_dq, d_dk, d_dv = attend_backward(d_q, d_k, d_v, d_lse, d_do, d_o, H_D)
    de_part, g_d_qkv, entry_sums = dec_entry_back(
        y0, d_dq, d_dk, d_dv, d_dmid, ranks_row, dec_full, stack_rows([gains[3], d_shift1])
    )
    g_mask, g_d_shift1, g_d_bq, g_d_bv, g_d_gain1 = (entry_sums[i] for i in range(5))
    de_sum = line_sum(de_part, 7, 1)
    dec_late, de_sum = lax.optimization_barrier((dec_late, de_sum))
    dec_late = lax.psum(dec_late, "seq")

    place_word = place[None].astype(jnp.int32)
    e_do, e_dmid, early_grads, back_sums, bu_sums, be_sums = encoder_back(
        place_word,
        de_sum,
        (e_mid, encoded, e_o, e_slope, e_act),
        enc_full,
        stack_rows([gains[1], gains[2], e_shift2, e_shift3]),
    )
    g_e_bo, g_e_shift2, g_e_bd, g_e_shift3, g_e_gain2, g_e_gain3 = (back_sums[i] for i in range(6))
    g_e_bu = bu_sums[0]
    g_b_embed = be_sums[0]
    late_grads, entry_sums = encoder_entry_back(
        place_word,
        kept,
        (x0, e_mixed, e_lse, e_o),
        e_do,
        e_dmid,
        enc_full,
        stack_rows([gains[0], e_shift1]),
    )
    g_b_patch, g_cls, g_e_shift1, g_e_bq, g_e_bv, g_e_gain1 = (entry_sums[i] for i in range(6))

    once = jnp.where(place == 0, 1.0, 0.0)
    enc_bias = [g_b_patch, g_cls, g_e_shift1, g_e_bq, g_e_bv, g_e_bo, g_e_shift2, g_e_bu]
    enc_bias = jnp.concatenate(enc_bias + [g_e_bd, g_e_shift3, g_b_embed]) * once
    dec_bias = [g_mask, g_d_shift1, g_d_bq, g_d_bv, g_d_bo, g_d_shift2, g_d_bu, g_d_bd]
    dec_bias = jnp.concatenate(dec_bias + [g_d_shift3, g_b_head])
    enc_gain = jnp.concatenate([g_e_gain1, g_e_gain2, g_e_gain3]) * once
    dec_gain = jnp.concatenate([g_d_gain1, g_d_gain2, g_d_gain3])
    small = jnp.concatenate([enc_gain, dec_gain, enc_bias, dec_bias, loss_part[None]])
    embed_cols = D_D // seq_count
    dec_late, late_grads = lax.optimization_barrier((dec_late, late_grads))
    early_all, late_all, small, dec_early, head_grad = exchange(
        early_grads,
        late_grads,
        small,
        g_d_qkv,
        dec_late[:, D_D + 2 * FF_D :],
        seq_count,
        embed_cols,
        2,
    )
    dec_grad = jnp.concatenate([dec_early, dec_late[:, : D_D + 2 * FF_D]], axis=1)
    n_gain = gain_w.shape[0]
    n_bias = bias_w.shape[0]
    gain_grad = small[:n_gain]
    bias_grad = small[n_gain : n_gain + n_bias]
    loss_total = small[n_gain + n_bias]

    enc_new = tuple(enc_update(enc_w, enc_m, enc_v, early_all, late_all))
    dec_new = adamw(dec_w, dec_m, dec_v, dec_grad, MATRIX_RATE, MATRIX_DECAY)
    head_new = adamw(head_w, head_m, head_v, head_grad, MATRIX_RATE, MATRIX_DECAY)
    gain_new = adamw(gain_w, gain_m, gain_v, gain_grad, SMALL_RATE, 0.0)
    bias_new = adamw(bias_w, bias_m, bias_v, bias_grad, SMALL_RATE, 0.0)
    return (loss_total,) + enc_new + dec_new + head_new + gain_new + bias_new


def solution(mesh):
    rows = P("fsdp", None)
    in_specs = (P("fsdp", "seq", None), rows) + (rows,) * 6 + (P(),) * 9
    out_specs = (P(),) + (rows,) * 6 + (P(),) * 9
    return jax.shard_map(shards, mesh=mesh, in_specs=in_specs, out_specs=out_specs, check_vma=False)
```

```python
from functools import partial

import jax
import jax.numpy as jnp
from jax import lax
from jax.experimental import pallas as pl
from jax.experimental.pallas import tpu as pltpu
from jax.sharding import PartitionSpec as P

D_E = 768
H_E = 12
FF_E = 3072
D_D = 512
H_D = 16
FF_D = 2048
PIX = 768
PATCHES = 1024
KEEP = 256
STEP = 5

NORM_EPS = 1e-06
PIXEL_EPS = 1e-06
BETA_ONE = 0.5
BETA_TWO = 0.75
MATRIX_RATE = 0.03
SMALL_RATE = 0.1
MATRIX_DECAY = 0.05
ADAM_EPS = 1e-08

TAIL = 16
E_ROWS = KEEP + TAIL
D_ROWS = PATCHES + TAIL
LOG2E = 1.4426950408889634
MASKED_SCORE = -1e30


def bias_widths():
    return [D_E] * 7 + [FF_E] + [D_E] * 2 + [D_D] * 7 + [FF_D] + [D_D] * 2 + [PIX]


def split_vector(vector, widths):
    pieces = []
    offset = 0
    for span_width in widths:
        pieces.append(vector[offset : offset + span_width])
        offset += span_width
    return pieces


def positions(index_arr, width_dim):
    halves = width_dim // 2
    frequency = 10000.0 ** (-jnp.arange(halves, dtype=jnp.float32) / halves)
    angles = (index_arr.astype(jnp.float32) + 1.0)[..., None] * frequency
    return jnp.concatenate([jnp.sin(angles), jnp.cos(angles)], axis=-1)


def norm_forward(inputs, gain_vec, shift_vec):
    centre = inputs - jnp.mean(inputs, axis=-1, keepdims=True)
    inverse = lax.rsqrt(jnp.mean(centre * centre, axis=-1, keepdims=True) + NORM_EPS)
    scaled = centre * inverse
    return (scaled * gain_vec + shift_vec, scaled, inverse)


def norm_backward(upstream, scaled, inverse, gain_vec):
    weighted = upstream * gain_vec
    inner_part = (
        weighted
        - jnp.mean(weighted, axis=-1, keepdims=True)
        - scaled * jnp.mean(weighted * scaled, axis=-1, keepdims=True)
    )
    return (
        inverse * inner_part,
        jnp.sum(upstream * scaled, axis=(0, 1)),
        jnp.sum(upstream, axis=(0, 1)),
    )


def low(tensor):
    return tensor.astype(jnp.bfloat16)


def project(row_block, weight):
    return jnp.einsum("isd,de->ise", row_block, weight, preferred_element_type=jnp.float32)


def project_back(row_block, weight):
    return jnp.einsum("ise,de->isd", row_block, weight, preferred_element_type=jnp.float32)


def weight_grad(row_block, upstream):
    return jnp.einsum("isd,ise->de", row_block, upstream, preferred_element_type=jnp.float32)


def row_sum(tensor):
    return jnp.sum(tensor.astype(jnp.float32), axis=(0, 1))


def enc_mats_of(full_rows):
    return (
        full_rows[:, D_E : 4 * D_E],
        full_rows[:, 4 * D_E : 5 * D_E],
        full_rows[:, 5 * D_E : 5 * D_E + FF_E],
        full_rows[:, 5 * D_E + FF_E : 5 * D_E + 2 * FF_E],
    )


def dot_f32(left, right, contract):
    return lax.dot_general(
        left, right, (contract, ((), ())), preferred_element_type=jnp.float32
    )


NN = ((1,), (0,))
TN = ((0,), (0,))


def pieces_of(value):
    first = low(value).astype(jnp.float32)
    rest = value - first
    second = low(rest).astype(jnp.float32)
    return first, second, rest - second


def own_span(shape, axis, head, head_dim):
    place = lax.broadcasted_iota(jnp.int32, shape, axis)
    return (place >= head * head_dim) & (place < (head + 1) * head_dim)


def live_tail(rows, scores, other):
    place = lax.broadcasted_iota(jnp.int32, (rows, scores.shape[1]), 0)
    return jnp.where(place < 1, scores, other)


def attend_forward_group(heads, head_dim, q, k, v):
    main = k.shape[0] - TAIL
    scale = head_dim ** (-0.5) * LOG2E
    q_t = q.astype(jnp.float32).T * scale
    q_high = low(q_t)
    q_rest = low(q_t - q_high.astype(jnp.float32))
    k_main = jnp.concatenate([k[:main], k[:main]], axis=1)
    k_tail = jnp.concatenate([k[main:], k[main:]], axis=1)
    v_main = low(v[:main].astype(jnp.float32).T)
    v_tail = v[main:]
    ones = jnp.ones((TAIL, main), jnp.bfloat16)

    def scores_of(head):
        own = own_span(q_t.shape, 0, head, head_dim)
        none = jnp.zeros_like(q_high)
        q_h = jnp.concatenate([jnp.where(own, q_high, none), jnp.where(own, q_rest, none)], axis=0)
        return dot_f32(k_main, q_h, NN), live_tail(TAIL, dot_f32(k_tail, q_h, NN), MASKED_SCORE)

    outs, sums = [], []
    following = scores_of(0)
    for head in range(heads):
        span = slice(head * head_dim, (head + 1) * head_dim)
        s_main, s_tail = following
        if head + 1 < heads:
            following = scores_of(head + 1)
        top = jnp.maximum(
            jnp.max(s_main, axis=0, keepdims=True), jnp.max(s_tail, axis=0, keepdims=True)
        )
        p_main = low(jnp.exp2(s_main - top))
        p_tail = low(jnp.exp2(s_tail - top))
        o_t = dot_f32(jnp.concatenate([v_main[span], ones], axis=0), p_main, NN)
        total = o_t[head_dim : head_dim + 1] + jnp.sum(
            p_tail.astype(jnp.float32), axis=0, keepdims=True
        )
        o_t = o_t[:head_dim] + dot_f32(v_tail, p_tail, TN)[span]
        outs.append(o_t * (1.0 / total))
        sums.append(top + jnp.log2(total))
    return low(jnp.concatenate(outs, axis=0).T), sums


def attend_forward_kernel(heads, head_dim, q_ref, k_ref, v_ref, o_ref, lse_ref):
    o_ref[0], sums = attend_forward_group(heads, head_dim, q_ref[0], k_ref[0], v_ref[0])
    for head in range(heads):
        lse_ref[0, 0, head : head + 1, :] = sums[head]


def attend_backward_group(heads, head_dim, q, k, v, sums, do, o):
    main = k.shape[0] - TAIL
    rows = q.shape[0]
    unit = head_dim ** (-0.5)
    q_t = q.astype(jnp.float32).T * (unit * LOG2E)
    q_high = low(q_t).astype(jnp.float32)
    q_rest = q_t - q_high
    do_t = do.astype(jnp.float32).T
    inner_t = do_t * o.astype(jnp.float32).T
    place = lax.broadcasted_iota(jnp.int32, q_t.shape, 0)

    def with_row(block, offset, value):
        for at, part in enumerate(pieces_of(value)):
            block = jnp.where(place == offset + at, part, block)
        return block

    score_sides, value_sides = [], []
    for head in range(heads):
        own = own_span(q_t.shape, 0, head, head_dim)
        span = slice(head * head_dim, (head + 1) * head_dim)
        other = ((head + 1) % heads) * head_dim
        lse = sums[head]
        inner = jnp.sum(inner_t[span], axis=0, keepdims=True)
        rest = with_row(jnp.where(own, q_rest, 0.0), other, -lse)
        score_sides.append(low(jnp.concatenate([jnp.where(own, q_high, 0.0), rest], axis=0)))
        last = with_row(jnp.zeros_like(do_t), 0, -inner)
        value_sides.append(low(jnp.concatenate([jnp.where(own, do_t, 0.0), last], axis=0)))
    zero = jnp.zeros_like(q)
    q_sides = [jnp.where(own_span(q.shape, 1, h, head_dim), q, zero) for h in range(heads)]
    do_sides = [jnp.where(own_span(q.shape, 1, h, head_dim), do, zero) for h in range(heads)]
    stacked = rows % 128 == 0
    if stacked:
        q_sides = jnp.concatenate(q_sides, axis=0)
        do_sides = jnp.concatenate(do_sides, axis=0)

    def sum_heads(parts, sides):
        if stacked:
            return dot_f32(jnp.concatenate(parts, axis=1), sides, NN)
        terms = [dot_f32(part, side, NN) for part, side in zip(parts, sides)]
        return sum(terms[1:], terms[0])

    k_main = k[:main]
    k_tail = k[main:]
    k_main_t = low(k_main.astype(jnp.float32).T)

    def with_ones(block):
        return jnp.concatenate([block, jnp.ones_like(block)], axis=1)

    def beside_own(block, head):
        own = jnp.where(own_span(block.shape, 1, head, head_dim), block, jnp.ones_like(block))
        return jnp.concatenate([block, own], axis=1)

    v_main = with_ones(v[:main])
    v_tail = with_ones(v[main:])
    dq_parts, p_mains, s_mains, p_tails, s_tails = [], [], [], [], []
    for head in range(heads):
        span = slice(head * head_dim, (head + 1) * head_dim)
        p = jnp.exp2(dot_f32(beside_own(k_main, head), score_sides[head], NN))
        s = low(p * dot_f32(v_main, value_sides[head], NN))
        p_mains.append(low(p))
        s_mains.append(s)
        p = jnp.exp2(dot_f32(beside_own(k_tail, head), score_sides[head], NN))
        p = live_tail(TAIL, p, 0.0)
        s_tail = low(p * dot_f32(v_tail, value_sides[head], NN))
        p_tails.append(low(p))
        s_tails.append(s_tail)
        dq_parts.append(dot_f32(k_main_t[span], s, NN) + dot_f32(k_tail, s_tail, TN)[span])
    dk = [low(sum_heads(part, q_sides) * unit) for part in (s_mains, s_tails)]
    dv = [low(sum_heads(part, do_sides)) for part in (p_mains, p_tails)]
    dq = low(jnp.concatenate(dq_parts, axis=0).T * unit)
    return dq, dk, dv


def attend_backward_kernel(
    heads, head_dim, q_ref, k_ref, v_ref, lse_ref, do_ref, o_ref, dq_ref, dk_ref, dv_ref
):
    main = k_ref.shape[1] - TAIL
    sums = [lse_ref[0, 0, head : head + 1, :] for head in range(heads)]
    dq_ref[0], dk, dv = attend_backward_group(
        heads, head_dim, q_ref[0], k_ref[0], v_ref[0], sums, do_ref[0], o_ref[0]
    )
    dk_ref[0, :main], dk_ref[0, main:] = dk
    dv_ref[0, :main], dv_ref[0, main:] = dv


VMEM_LIMIT = 60 * 1024 * 1024
COPY_LIMIT = 32 * 1024 * 1024


def attend_specs(q_rows, k_rows, heads):
    return (
        pl.BlockSpec((1, q_rows, 128), lambda i, g: (i, 0, g)),
        pl.BlockSpec((1, k_rows, 128), lambda i, g: (i, 0, g)),
        pl.BlockSpec((1, 1, heads, q_rows), lambda i, g: (i, g, 0, 0)),
    )


def attend_forward(queries, key_rows, value_rows, head_count):
    images, q_rows, width = queries.shape
    k_rows = key_rows.shape[1]
    head_dim = width // head_count
    heads = 128 // head_dim
    groups = width // 128
    q_spec, k_spec, l_spec = attend_specs(q_rows, k_rows, heads)
    return pl.pallas_call(
        partial(attend_forward_kernel, heads, head_dim),
        grid=(images, groups),
        in_specs=[q_spec, k_spec, k_spec],
        out_specs=[q_spec, l_spec],
        out_shape=[
            jax.ShapeDtypeStruct((images, q_rows, width), jnp.bfloat16),
            jax.ShapeDtypeStruct((images, groups, heads, q_rows), jnp.float32),
        ],
        compiler_params=pltpu.CompilerParams(vmem_limit_bytes=VMEM_LIMIT),
        cost_estimate=pl.CostEstimate(
            flops=16 * images * q_rows * k_rows * width,
            bytes_accessed=4 * images * (q_rows + k_rows) * width,
            transcendentals=images * head_count * q_rows * k_rows,
        ),
    )(queries, key_rows, value_rows)


def attend_backward(queries, key_rows, value_rows, logsum, upstream, attended, head_count):
    images, q_rows, width = queries.shape
    k_rows = key_rows.shape[1]
    head_dim = width // head_count
    heads = 128 // head_dim
    groups = width // 128
    q_spec, k_spec, l_spec = attend_specs(q_rows, k_rows, heads)
    return pl.pallas_call(
        partial(attend_backward_kernel, heads, head_dim),
        grid=(images, groups),
        in_specs=[q_spec, k_spec, k_spec, l_spec, q_spec, q_spec],
        out_specs=[q_spec, k_spec, k_spec],
        out_shape=[
            jax.ShapeDtypeStruct((images, q_rows, width), jnp.bfloat16),
            jax.ShapeDtypeStruct((images, k_rows, width), jnp.bfloat16),
            jax.ShapeDtypeStruct((images, k_rows, width), jnp.bfloat16),
        ],
        compiler_params=pltpu.CompilerParams(vmem_limit_bytes=VMEM_LIMIT),
        cost_estimate=pl.CostEstimate(
            flops=40 * images * q_rows * k_rows * width,
            bytes_accessed=8 * images * (q_rows + k_rows) * width,
            transcendentals=images * head_count * q_rows * k_rows,
        ),
    )(queries, key_rows, value_rows, logsum, upstream, attended)


MESH = pl.DeviceIdType.MESH


def line_sum_kernel(
    chunks, lines, x_ref, o_ref, from_left, from_right, to_left, to_right, send_sem, recv_sem
):
    count = lax.axis_size("seq")
    place = lax.axis_index("seq")
    has_left = place > 0
    has_right = place < count - 1
    rows = x_ref.shape[0] // chunks
    barrier = pltpu.get_barrier_semaphore()

    def greet(to):
        pl.semaphore_signal(barrier, inc=1, device_id={"seq": to}, device_id_type=MESH)

    pl.when(has_left)(lambda: greet(place - 1))
    pl.when(has_right)(lambda: greet(place + 1))
    peers = jnp.where(has_left, 1, 0) + jnp.where(has_right, 1, 0)
    pl.semaphore_wait(barrier, peers)

    def copy(way, at):
        span = pl.ds(pl.multiple_of(at * rows, 16), rows)
        source, target = ((to_right, from_left), (to_left, from_right))[way]
        return pltpu.make_async_remote_copy(
            src_ref=source.at[span],
            dst_ref=target.at[span],
            send_sem=send_sem.at[way, at],
            recv_sem=recv_sem.at[way, at],
            device_id={"seq": place + 1 if way == 0 else place - 1},
            device_id_type=MESH,
        )

    def end_copy(way, at):
        span = pl.ds(at * rows, rows)
        return pltpu.make_async_remote_copy(
            src_ref=x_ref.at[span],
            dst_ref=(from_left, from_right)[way].at[span],
            send_sem=send_sem.at[way, at],
            recv_sem=recv_sem.at[way, at],
            device_id={"seq": place + 1 if way == 0 else place - 1},
            device_id_type=MESH,
        )

    for way, is_end in ((0, jnp.logical_not(has_left)), (1, jnp.logical_not(has_right))):

        @pl.when(is_end)
        def _():
            for at in range(chunks):
                if at >= 2:
                    end_copy(way, at - 2).wait_send()
                end_copy(way, at).start()
            for at in range(chunks - 2, chunks):
                end_copy(way, at).wait_send()

    def span_of(at):
        return pl.ds(pl.multiple_of(at * rows, 16), rows)

    for step in range(chunks + lines - 1):
        from_first = step - place
        from_last = step - (count - 1 - place)

        @pl.when(has_left & (from_first >= 0) & (from_first < chunks))
        def _():
            copy(0, from_first).wait_recv()

            @pl.when(has_right)
            def _():
                span = span_of(from_first)
                to_right[span] = x_ref[span] + from_left[span]
                copy(0, from_first).start()

        @pl.when(has_right & (from_last >= 0) & (from_last < chunks))
        def _():
            copy(1, from_last).wait_recv()

            @pl.when(has_left)
            def _():
                span = span_of(from_last)
                to_left[span] = x_ref[span] + from_right[span]
                copy(1, from_last).start()

    @pl.when(jnp.logical_not(has_left))
    def _():
        o_ref[...] = x_ref[...] + from_right[...]

    @pl.when(jnp.logical_not(has_right))
    def _():
        o_ref[...] = x_ref[...] + from_left[...]

    @pl.when(has_left & has_right)
    def _():
        o_ref[...] = (x_ref[...] + from_left[...]) + from_right[...]
        for at in range(chunks):
            copy(0, at).wait_send()
            copy(1, at).wait_send()


GATHER_WAYS = ("shared",) * 4 + ("within", "swapped")
GATHER_CHUNKS = len(GATHER_WAYS)
KEPT_CHUNKS = 8
PLACE_ROWS = 128


def start_kernel(
    lines,
    w_ref,
    x_ref,
    kept_ids,
    patch_ids,
    wide_ref,
    narrow_ref,
    bias_ref,
    full_ref,
    o_ref,
    wide_out,
    narrow_out,
    from_left,
    from_right,
    to_left,
    to_right,
    own_sem,
    ring_sems,
    pair_sems,
    send_sem,
    recv_sem,
):
    own = lax.axis_index("fsdp")
    place = lax.axis_index("seq")
    core = lax.rem(own, 2)
    at_x = lax.rem(lax.div(own, 2), 2)
    at_y = lax.div(own, 4)
    odd = lax.rem(place, 2)
    by_x = 2 - 4 * at_x
    by_y = 4 - 8 * at_y
    first = own + (1 - odd) * by_x + odd * by_y
    second = own + odd * by_x + (1 - odd) * by_y
    across = own + by_x + by_y
    partner = own + 1 - 2 * core
    over = place + 1 - 2 * odd
    has_left = place > 0
    has_right = place < lines - 1
    block = w_ref.shape[0]
    rows = block // GATHER_CHUNKS
    kept_rows = x_ref.shape[0] // KEPT_CHUNKS
    barrier = pltpu.get_barrier_semaphore()

    def greet(device):
        pl.semaphore_signal(barrier, inc=1, device_id=device, device_id_type=MESH)

    for device in (first, second, partner):
        greet({"fsdp": device})
    pl.when(has_left)(lambda: greet({"seq": place - 1}))
    pl.when(has_right)(lambda: greet({"seq": place + 1}))
    peers = jnp.where(has_left, 1, 0) + jnp.where(has_right, 1, 0)
    pl.semaphore_wait(barrier, peers + 3)

    def span_of(owner, at):
        return pl.ds(pl.multiple_of(owner * block + at * rows, 16), rows)

    def copy_of(source, target, sems, at, device):
        return pltpu.make_async_remote_copy(
            src_ref=source,
            dst_ref=target,
            send_sem=sems.at[(0,) + at],
            recv_sem=sems.at[(1,) + at],
            device_id=device,
            device_id_type=MESH,
        )

    def own_rows(at):
        return w_ref.at[pl.ds(at * rows, rows)]

    def ahead(at):
        return second if GATHER_WAYS[at] == "swapped" else first

    def aside(at):
        return first if GATHER_WAYS[at] == "swapped" else second

    def ahead_copy(at):
        target = full_ref.at[span_of(own, at)]
        return copy_of(own_rows(at), target, ring_sems, (0, at), {"fsdp": ahead(at)})

    def relay_copy(at):
        part = full_ref.at[span_of(ahead(at), at)]
        return copy_of(part, part, ring_sems, (1, at), {"fsdp": aside(at)})

    def third_copy(at):
        if GATHER_WAYS[at] == "shared":
            part = full_ref.at[span_of(ahead(at), at)]
            return copy_of(part, part, ring_sems, (2, at), {"seq": over})
        target = full_ref.at[span_of(own, at)]
        return copy_of(own_rows(at), target, ring_sems, (2, at), {"fsdp": aside(at)})

    def pair_copy(kind, at):
        owner = (own, ahead(at), across, aside(at))[kind]
        target = full_ref.at[span_of(owner, at)]
        source = own_rows(at) if kind == 0 else target
        return copy_of(source, target, pair_sems, (kind, at), {"fsdp": partner})

    def keep_copy(at):
        return pltpu.make_async_copy(
            own_rows(at), full_ref.at[span_of(own, at)], own_sem.at[at]
        )

    def send_own(at):
        ahead_copy(at).start()
        if GATHER_WAYS[at] != "shared":
            third_copy(at).start()
        pair_copy(0, at).start()
        keep_copy(at).start()

    def receive_rest(at):
        relay_copy(at).wait_recv()
        pair_copy(2, at).start()
        third_copy(at).wait_recv()
        pair_copy(3, at).start()

    def kept_span(at):
        return pl.ds(pl.multiple_of(at * kept_rows, 16), kept_rows)

    def kept_copy(way, at, source=None):
        span = kept_span(at)
        source = (to_right, to_left)[way] if source is None else source
        return pltpu.make_async_remote_copy(
            src_ref=source.at[span],
            dst_ref=(from_left, from_right)[way].at[span],
            send_sem=send_sem.at[way, at],
            recv_sem=recv_sem.at[way, at],
            device_id={"seq": place + 1 if way == 0 else place - 1},
            device_id_type=MESH,
        )

    def kept_step(step):
        if step < KEPT_CHUNKS:
            pl.when(jnp.logical_not(has_left))(lambda: kept_copy(0, step, x_ref).start())
            pl.when(jnp.logical_not(has_right))(lambda: kept_copy(1, step, x_ref).start())
        from_first = step - place
        from_last = step - (lines - 1 - place)

        @pl.when(has_left & (from_first >= 0) & (from_first < KEPT_CHUNKS))
        def _():
            kept_copy(0, from_first).wait_recv()

            @pl.when(has_right)
            def _():
                span = kept_span(from_first)
                to_right[span] = x_ref[span] + from_left[span]
                kept_copy(0, from_first).start()

        @pl.when(has_right & (from_last >= 0) & (from_last < KEPT_CHUNKS))
        def _():
            kept_copy(1, from_last).wait_recv()

            @pl.when(has_left)
            def _():
                span = kept_span(from_last)
                to_left[span] = x_ref[span] + from_right[span]
                kept_copy(1, from_last).start()

    def write_positions(at):
        span = slice(at * PLACE_ROWS, (at + 1) * PLACE_ROWS)
        for ids, scale, out, bias in (
            (kept_ids, wide_ref, wide_out, bias_ref),
            (patch_ids, narrow_ref, narrow_out, None),
        ):
            if span.start < ids.shape[0]:
                half = scale.shape[1]
                angles = (ids[span, :].astype(jnp.float32) + 1.0) * scale[...]
                for part, lanes in (
                    (jnp.sin(angles), slice(0, half)),
                    (jnp.cos(angles), slice(half, 2 * half)),
                ):
                    out[span, lanes] = part if bias is None else part + bias[:, lanes]

    send_own(0)
    send_own(1)
    kept_steps = list(range(KEPT_CHUNKS + lines - 1))
    place_steps = list(range(max(kept_ids.shape[0], patch_ids.shape[0]) // PLACE_ROWS))
    for at in range(GATHER_CHUNKS):
        for _ in range(2):
            if kept_steps:
                kept_step(kept_steps.pop(0))
        if place_steps:
            write_positions(place_steps.pop(0))
        ahead_copy(at).wait_recv()
        relay_copy(at).start()
        if GATHER_WAYS[at] == "shared":
            third_copy(at).start()
        pair_copy(1, at).start()
        if at + 2 < GATHER_CHUNKS:
            send_own(at + 2)
        if at:
            receive_rest(at - 1)
    for step in place_steps:
        write_positions(step)
    receive_rest(GATHER_CHUNKS - 1)
    for step in kept_steps:
        kept_step(step)

    @pl.when(jnp.logical_not(has_left))
    def _():
        o_ref[...] = x_ref[...] + from_right[...]
        for at in range(KEPT_CHUNKS):
            kept_copy(0, at, x_ref).wait_send()

    @pl.when(jnp.logical_not(has_right))
    def _():
        o_ref[...] = x_ref[...] + from_left[...]
        for at in range(KEPT_CHUNKS):
            kept_copy(1, at, x_ref).wait_send()

    @pl.when(has_left & has_right)
    def _():
        o_ref[...] = (x_ref[...] + from_left[...]) + from_right[...]
        for at in range(KEPT_CHUNKS):
            kept_copy(0, at).wait_send()
            kept_copy(1, at).wait_send()

    for at in range(GATHER_CHUNKS):
        keep_copy(at).wait()
        ahead_copy(at).wait_send()
        relay_copy(at).wait_send()
        third_copy(at).wait_send()
        for kind in range(4):
            pair_copy(kind, at).wait()


def frequencies(width_dim):
    halves = width_dim // 2
    return 10000.0 ** (-jnp.arange(halves, dtype=jnp.float32) / halves)


def start_gather(own_w, own_kept, kept_ids, patch_ids, bias, collective_id):
    plane = lax.axis_size("fsdp")
    lines = lax.axis_size("seq")
    block, width = own_w.shape
    if plane != PLANE or block % (16 * GATHER_CHUNKS) or lines % 2:
        return (
            lax.all_gather(own_w, "fsdp", axis=0, tiled=True),
            line_sum(own_kept, KEPT_CHUNKS, collective_id),
            positions(kept_ids, D_E) + bias,
            positions(patch_ids, D_D),
        )
    buffer = pltpu.VMEM(own_kept.shape, own_kept.dtype)
    dma = pltpu.SemaphoreType.DMA
    vmem = pl.BlockSpec(memory_space=pltpu.VMEM)
    anywhere = pl.BlockSpec(memory_space=pl.ANY)
    return pl.pallas_call(
        partial(start_kernel, lines),
        out_shape=[
            jax.ShapeDtypeStruct((PLANE * block, width), own_w.dtype),
            jax.ShapeDtypeStruct(own_kept.shape, own_kept.dtype),
            jax.ShapeDtypeStruct((kept_ids.shape[0], D_E), jnp.float32),
            jax.ShapeDtypeStruct((patch_ids.shape[0], D_D), jnp.float32),
        ],
        in_specs=[anywhere] + [vmem] * 6,
        out_specs=[anywhere] + [vmem] * 3,
        scratch_shapes=[buffer] * 4
        + [
            dma((GATHER_CHUNKS,)),
            dma((2, 3, GATHER_CHUNKS)),
            dma((2, 4, GATHER_CHUNKS)),
            dma((2, KEPT_CHUNKS)),
            dma((2, KEPT_CHUNKS)),
        ],
        compiler_params=pltpu.CompilerParams(
            collective_id=collective_id, has_side_effects=True, vmem_limit_bytes=COPY_LIMIT
        ),
        cost_estimate=pl.CostEstimate(
            flops=0, bytes_accessed=200 * 1024 * 1024, transcendentals=0
        ),
    )(
        own_w,
        own_kept,
        kept_ids[:, None],
        patch_ids[:, None],
        frequencies(D_E)[None],
        frequencies(D_D)[None],
        bias[None],
    )


def line_sum(block, chunks, collective_id):
    shape = jax.ShapeDtypeStruct(block.shape, block.dtype)
    buffer = pltpu.VMEM(block.shape, block.dtype)
    return pl.pallas_call(
        partial(line_sum_kernel, chunks, lax.axis_size("seq")),
        out_shape=shape,
        in_specs=[pl.BlockSpec(memory_space=pltpu.VMEM)],
        out_specs=pl.BlockSpec(memory_space=pltpu.VMEM),
        scratch_shapes=[buffer] * 4
        + [pltpu.SemaphoreType.DMA((2, chunks)), pltpu.SemaphoreType.DMA((2, chunks))],
        compiler_params=pltpu.CompilerParams(
            collective_id=collective_id, has_side_effects=True, vmem_limit_bytes=COPY_LIMIT
        ),
        cost_estimate=pl.CostEstimate(
            flops=0, bytes_accessed=100 * block.size, transcendentals=0
        ),
    )(block)


SMALL_BLOCK = (8, 768)
PLANE = 8


def send(source, target, sems, at, device):
    return pltpu.make_async_remote_copy(
        src_ref=source,
        dst_ref=target,
        send_sem=sems.at[(0,) + at],
        recv_sem=sems.at[(1,) + at],
        device_id=device,
        device_id_type=MESH,
    )


def greet_all():
    own, place = lax.axis_index("fsdp"), lax.axis_index("seq")
    line = lax.axis_size("seq")
    barrier = pltpu.get_barrier_semaphore()
    for step in range(1, PLANE):
        device = {"fsdp": lax.rem(own + step, PLANE)}
        pl.semaphore_signal(barrier, inc=1, device_id=device, device_id_type=MESH)
    for step in range(1, line):
        device = {"seq": lax.rem(place + step, line)}
        pl.semaphore_signal(barrier, inc=1, device_id=device, device_id_type=MESH)
    pl.semaphore_wait(barrier, PLANE - 1 + line - 1)


class PlaneSum:
    def __init__(self, grad, pair_in, out, into, pair_sems, plane_sems):
        self.grad, self.pair_in, self.out, self.into = grad, pair_in, out, into
        self.pair_sems, self.plane_sems = pair_sems, plane_sems
        self.own = lax.axis_index("fsdp")
        self.core = lax.rem(self.own, 2)
        self.chip = lax.div(self.own, 2)
        self.rows = grad.shape[0] // PLANE

    @staticmethod
    def scratch(rows, width, kind):
        dma = pltpu.SemaphoreType.DMA
        return [
            pltpu.VMEM((4, rows, width), jnp.float32),
            pltpu.VMEM((3, rows, width), kind),
            pltpu.VMEM((3, rows, width), kind),
            dma((2, 4)),
            dma((2, 3)),
        ]

    def rows_of(self, owner):
        return pl.ds(pl.multiple_of(owner * self.rows, 16), self.rows)

    def target(self, other):
        return lax.rem(self.chip + other, 4)

    def pair_copy(self, other):
        owner = 2 * self.target(other) + 1 - self.core
        partner = self.own + 1 - 2 * self.core
        return send(
            self.grad.at[self.rows_of(owner)],
            self.pair_in.at[other],
            self.pair_sems,
            (other,),
            {"fsdp": partner},
        )

    def plane_copy(self, other):
        owner = 2 * self.target(other) + self.core
        at = other - 1
        return send(self.out.at[at], self.into.at[at], self.plane_sems, (at,), {"fsdp": owner})

    def start(self):
        for other in (3, 1, 2, 0):
            self.pair_copy(other).start()

    def pass_on(self):
        for other in (3, 1, 2):
            self.pair_copy(other).wait_recv()
            owner = 2 * self.target(other) + self.core
            both = self.grad[self.rows_of(owner)] + self.pair_in[other]
            self.out[other - 1] = both.astype(self.out.dtype)
            self.plane_copy(other).start()

    def total(self):
        self.pair_copy(0).wait_recv()
        total = self.grad[self.rows_of(self.own)] + self.pair_in[0]
        for other in (1, 2, 3):
            self.plane_copy(other).wait_recv()
            total = total + self.into[other - 1].astype(jnp.float32)
        return total

    def finish(self):
        for other in range(4):
            self.pair_copy(other).wait_send()
            if other:
                self.plane_copy(other).wait_send()


class LineGather:
    def __init__(self, slots, sems):
        self.slots, self.sems = slots, sems
        self.place = lax.axis_index("seq")
        self.line = lax.axis_size("seq")

    def copy(self, step):
        part = self.slots.at[self.place]
        to = lax.rem(self.place + step, self.line)
        return send(part, part, self.sems, (step - 1,), {"seq": to})

    def start(self, value):
        self.slots[self.place] = value
        for step in range(1, self.line):
            self.copy(step).start()

    def wait_recv(self):
        for step in range(1, self.line):
            self.copy(step).wait_recv()

    def finish(self):
        for step in range(1, self.line):
            self.copy(step).wait_send()


class LineSum:
    def __init__(self, block, parts, result, split_sems, line_sems):
        self.block, self.parts, self.result = block, parts, result
        self.split_sems, self.line_sems = split_sems, line_sems
        self.place = lax.axis_index("seq")
        self.line = lax.axis_size("seq")
        self.rows = block.shape[0] // parts.shape[0]

    @staticmethod
    def scratch(rows, width, line):
        dma = pltpu.SemaphoreType.DMA
        return [
            pltpu.VMEM((rows, width), jnp.float32),
            pltpu.VMEM((line, rows // line, width), jnp.float32),
            pltpu.VMEM((rows, width), jnp.float32),
            dma((2, line - 1)),
            dma((2, line - 1)),
        ]

    def quarter(self, at):
        return pl.ds(pl.multiple_of(at * self.rows, 8), self.rows)

    def split_copy(self, step):
        to = lax.rem(self.place + step, self.line)
        source = self.block.at[self.quarter(to)]
        return send(source, self.parts.at[self.place], self.split_sems, (step - 1,), {"seq": to})

    def line_copy(self, step):
        to = lax.rem(self.place + step, self.line)
        part = self.result.at[self.quarter(self.place)]
        return send(part, part, self.line_sems, (step - 1,), {"seq": to})

    def start(self, value):
        self.block[...] = value
        self.parts[self.place] = self.block[self.quarter(self.place)]
        for step in range(1, self.line):
            self.split_copy(step).start()

    def spread(self):
        for step in range(1, self.line):
            self.split_copy(step).wait_recv()
        total = self.parts[0]
        for at in range(1, self.parts.shape[0]):
            total = total + self.parts[at]
        self.result[self.quarter(self.place)] = total
        for step in range(1, self.line):
            self.line_copy(step).start()

    def finish(self):
        for step in range(1, self.line):
            self.line_copy(step).wait()
            self.split_copy(step).wait_send()


def exchange_kernel(
    g_ref,
    small_ref,
    head_ref,
    out_ref,
    small_out,
    head_out,
    pair_in,
    plane_out,
    plane_in,
    pair_sems,
    plane_sems,
    small_in,
    small_line,
    line_sems,
    small_plane_sems,
    small_line_sems,
    small_out_sems,
    head_sems,
    head_pair_sems,
):
    own = lax.axis_index("fsdp")
    core = lax.rem(own, 2)
    partner = own + 1 - 2 * core
    chip = lax.div(own, 2)
    greet_all()
    plane = PlaneSum(g_ref, pair_in, plane_out, plane_in, pair_sems, plane_sems)
    line = LineGather(out_ref, line_sems)
    small_all = LineGather(small_line, small_line_sems)

    def peer(step):
        return lax.rem(own + step, PLANE)

    def small_plane_copy(step):
        return send(
            small_ref.at[peer(step)],
            small_in.at[step - 1],
            small_plane_sems,
            (step - 1,),
            {"fsdp": peer(step)},
        )

    def small_out_copy(step):
        part = small_out.at[own]
        return send(part, part, small_out_sems, (step - 1,), {"fsdp": peer(step)})

    head_rows = head_ref.shape[0]

    def head_span(owner):
        return pl.ds(pl.multiple_of(owner * head_rows, 16), head_rows)

    def head_copy(other):
        to = 2 * lax.rem(chip + other, 4) + core
        return send(
            head_ref, head_out.at[head_span(own)], head_sems, (other - 1,), {"fsdp": to}
        )

    def head_pair_copy(other):
        span = head_span(2 * lax.rem(chip + 4 - other, 4) + core)
        source = head_out.at[span] if other else head_ref
        return send(source, head_out.at[span], head_pair_sems, (other,), {"fsdp": partner})

    plane.start()
    for step in range(1, PLANE):
        small_plane_copy(step).start()
    plane.pass_on()
    for step in range(1, PLANE):
        small_plane_copy(step).wait_recv()
    total = small_ref[own]
    for step in range(1, PLANE):
        total = total + small_in[step - 1]
    small_all.start(total)
    for other in (3, 1, 2):
        head_copy(other).start()
    head_pair_copy(0).start()
    head_out[head_span(own)] = head_ref[...]
    line.start(low(plane.total()))
    small_all.wait_recv()
    total = small_line[0]
    for at in range(1, small_line.shape[0]):
        total = total + small_line[at]
    small_out[own] = total
    for step in range(1, PLANE):
        small_out_copy(step).start()
    for other in (1, 2, 3):
        head_copy(other).wait_recv()
        head_pair_copy(other).start()
    line.wait_recv()
    for step in range(1, PLANE):
        small_out_copy(step).wait()
        small_plane_copy(step).wait_send()
    for other in range(4):
        head_pair_copy(other).wait()
        if other:
            head_copy(other).wait_send()
    plane.finish()
    line.finish()
    small_all.finish()


def plane_fits(rows):
    line = lax.axis_size("seq")
    return lax.axis_size("fsdp") == PLANE and rows % (PLANE * 16) == 0 and line == 4


def exchange(late, small, head_own, line, collective_id):
    if not plane_fits(late.shape[0]):
        own = lax.psum_scatter(late, "fsdp", scatter_dimension=0, tiled=True)
        return (
            lax.all_gather(low(own), "seq", axis=0, tiled=False),
            lax.psum(small, ("fsdp", "seq")),
            lax.all_gather(head_own, "fsdp", axis=0, tiled=True),
        )
    rows, width = late.shape[0] // PLANE, late.shape[1]
    blocks = small.reshape((PLANE,) + SMALL_BLOCK)
    dma = pltpu.SemaphoreType.DMA
    vmem = pl.BlockSpec(memory_space=pltpu.VMEM)
    gathered, summed, head_all = pl.pallas_call(
        exchange_kernel,
        out_shape=[
            jax.ShapeDtypeStruct((line, rows, width), jnp.bfloat16),
            jax.ShapeDtypeStruct(blocks.shape, jnp.float32),
            jax.ShapeDtypeStruct((PLANE * head_own.shape[0], head_own.shape[1]), jnp.float32),
        ],
        in_specs=[vmem] * 3,
        out_specs=[vmem] * 3,
        scratch_shapes=PlaneSum.scratch(rows, width, jnp.bfloat16)
        + [
            pltpu.VMEM((PLANE - 1,) + SMALL_BLOCK, jnp.float32),
            pltpu.VMEM((line,) + SMALL_BLOCK, jnp.float32),
            dma((2, line - 1)),
            dma((2, PLANE - 1)),
            dma((2, line - 1)),
            dma((2, PLANE - 1)),
            dma((2, 3)),
            dma((2, 4)),
        ],
        compiler_params=pltpu.CompilerParams(
            collective_id=collective_id, has_side_effects=True, vmem_limit_bytes=COPY_LIMIT
        ),
        cost_estimate=pl.CostEstimate(
            flops=0, bytes_accessed=100 * 1024 * 1024, transcendentals=0
        ),
    )(late, blocks, head_own)
    return gathered, summed.reshape(small.shape), head_all


def gelu_parts(hidden):
    cdf = 0.5 * (1.0 + lax.erf(hidden * (2.0**-0.5)))
    density = jnp.exp(-0.5 * hidden * hidden) * (0.3989422804014327)
    return hidden * cdf, cdf + hidden * density


NT = ((1,), (1,))


def norm_rows(rows):
    centre = rows - jnp.mean(rows, axis=-1, keepdims=True)
    inverse = lax.rsqrt(jnp.mean(centre * centre, axis=-1, keepdims=True) + NORM_EPS)
    return centre * inverse, inverse


def norm_rows_back(upstream, scaled, inverse, gain):
    weighted = upstream * gain
    inner = (
        weighted
        - jnp.mean(weighted, axis=-1, keepdims=True)
        - scaled * jnp.mean(weighted * scaled, axis=-1, keepdims=True)
    )
    return inverse * inner, column_sum(upstream * scaled), column_sum(upstream)


def column_sum(rows):
    return jnp.sum(rows, axis=0, keepdims=True)


def clear_first(refs):
    @pl.when(pl.program_id(0) == 0)
    def _():
        for ref in refs:
            ref[...] = jnp.zeros_like(ref)


def dec_middle_kernel(
    grad_scale,
    o_ref,
    y_ref,
    pixel_ref,
    masked_ref,
    out_w,
    up_w,
    down_w,
    head_w,
    vec_ref,
    bu_ref,
    bh_ref,
    do_ref,
    dmid_ref,
    grad_ref,
    vec_grad,
    slope_ref,
    act_ref,
):
    clear_first((grad_ref, vec_grad))
    bo, gain2, shift2, bd, gain3, shift3 = (vec_ref[i : i + 1, :] for i in range(6))
    attended = o_ref[0]
    middle = y_ref[0] + dot_f32(attended, out_w[...], NN) + bo
    scaled2, inverse2 = norm_rows(middle)
    second = low(scaled2 * gain2 + shift2)
    size = 512
    decoded = middle + bd
    for at in range(0, FF_D, size):
        span = slice(at, at + size)
        value, slope = gelu_parts(dot_f32(second, up_w[:, span], NN) + bu_ref[:, span])
        slope_ref[:, span] = slope
        act_ref[:, span] = low(value)
        decoded = decoded + dot_f32(act_ref[:, span], down_w[:, span], NT)
    scaled3, inverse3 = norm_rows(decoded)
    third = low(scaled3 * gain3 + shift3)
    predicted = dot_f32(third, head_w[...], NN) + bh_ref[...]
    pixel = pixel_ref[0].astype(jnp.float32)
    centre = pixel - jnp.mean(pixel, axis=-1, keepdims=True)
    target = centre * lax.rsqrt(
        jnp.sum(centre * centre, axis=-1, keepdims=True) / (PIX - 1) + PIXEL_EPS
    )
    masked = masked_ref[0][:, :1]
    error = (predicted - target) * masked
    pred_grad = error * grad_scale
    pred_low = low(pred_grad)
    vec_grad[6:7, :] += column_sum(pred_grad)
    vec_grad[7:8, :] += column_sum(error * error)
    o_span, u_span = D_D, D_D + FF_D
    h_span = D_D + 2 * FF_D
    grad_ref[:, h_span:] += dot_f32(third, pred_low, TN)
    up3, g_gain3, g_shift3 = norm_rows_back(
        dot_f32(pred_low, head_w[...], NT), scaled3, inverse3, gain3
    )
    up3_low = low(up3)
    back = jnp.zeros_like(up3)
    for at in range(0, FF_D, size):
        span = slice(at, at + size)
        hidden_grad = low(dot_f32(up3_low, down_w[:, span], NN) * slope_ref[:, span])
        grad_ref[:, u_span + at : u_span + at + size] += dot_f32(up3_low, act_ref[:, span], TN)
        grad_ref[:, o_span + at : o_span + at + size] += dot_f32(second, hidden_grad, TN)
        row = 8 + at // size
        vec_grad[row : row + 1, :size] += column_sum(hidden_grad.astype(jnp.float32))
        back = back + dot_f32(hidden_grad, up_w[:, span], NT)
    through, g_gain2, g_shift2 = norm_rows_back(back, scaled2, inverse2, gain2)
    middle_grad = up3 + through
    middle_low = low(middle_grad)
    dmid_ref[0] = middle_grad
    grad_ref[:, :o_span] += dot_f32(attended, middle_low, TN)
    do_ref[0] = low(dot_f32(middle_low, out_w[...], NT))
    sums = (column_sum(middle_grad), g_gain2, g_shift2, column_sum(up3), g_gain3, g_shift3)
    for at, part in enumerate(sums):
        vec_grad[at : at + 1, :D_D] += part


def whole(shape):
    return pl.BlockSpec(shape, lambda i: (0,) * len(shape), pipeline_mode=pl.Buffered(1))


def columns(rows, width, at):
    return pl.BlockSpec((rows, width), lambda i: (0, at), pipeline_mode=pl.Buffered(1))


def per_image(rows, width):
    return pl.BlockSpec((1, rows, width), lambda i: (i, 0, 0))


def dec_middle(attended, y_own, pixels, masked, dec_full, head_low, vectors, bu, bh, grad_scale):
    images, rows, _ = attended.shape
    f32 = jnp.float32
    return pl.pallas_call(
        partial(dec_middle_kernel, grad_scale),
        grid=(images,),
        in_specs=[
            per_image(rows, D_D),
            per_image(rows, D_D),
            per_image(rows, PIX),
            per_image(rows, 128),
            columns(D_D, D_D, 3),
            columns(D_D, FF_D, 1),
            columns(D_D, FF_D, 2),
            whole((D_D, PIX)),
            whole((8, D_D)),
            whole((1, FF_D)),
            whole((1, PIX)),
        ],
        out_specs=[
            per_image(rows, D_D),
            per_image(rows, D_D),
            whole((D_D, D_D + 2 * FF_D + PIX)),
            whole((16, PIX)),
        ],
        out_shape=[
            jax.ShapeDtypeStruct((images, rows, D_D), jnp.bfloat16),
            jax.ShapeDtypeStruct((images, rows, D_D), f32),
            jax.ShapeDtypeStruct((D_D, D_D + 2 * FF_D + PIX), f32),
            jax.ShapeDtypeStruct((16, PIX), f32),
        ],
        scratch_shapes=[pltpu.VMEM((rows, FF_D), f32), pltpu.VMEM((rows, FF_D), jnp.bfloat16)],
        compiler_params=pltpu.CompilerParams(vmem_limit_bytes=VMEM_LIMIT),
        cost_estimate=pl.CostEstimate(
            flops=12 * images * rows * D_D * (D_D + 2 * FF_D + PIX),
            bytes_accessed=30 * 1024 * 1024,
            transcendentals=2 * images * rows * FF_D,
        ),
    )(
        attended, y_own, pixels, masked, dec_full, dec_full, dec_full, head_low, vectors, bu, bh
    )


def dec_entry_kernel(e_ref, rank_ref, place_ref, q_w, k_w, v_w, vec_ref, y_ref, q_ref, k_ref, v_ref):
    mask_token, gain, shift, bq, bv = (vec_ref[i : i + 1, :] for i in range(5))
    ranks = jnp.broadcast_to(rank_ref[0], (E_ROWS, PATCHES))
    at = lax.broadcasted_iota(jnp.int32, (E_ROWS, PATCHES), 0)
    hidden = (at >= KEEP) & (at < KEEP + 3) & (ranks >= KEEP)
    pick = low(jnp.where(((at == ranks) & (at < KEEP)) | hidden, 1.0, 0.0))
    place = lax.broadcasted_iota(jnp.int32, (TAIL, D_D), 0)
    token = jnp.zeros((TAIL, D_D), jnp.float32)
    for row, part in enumerate(pieces_of(mask_token)):
        token = jnp.where(place == row, part, token)
    source = jnp.concatenate([e_ref[0, :KEEP], low(token)], axis=0)
    y_ref[0, :PATCHES] = dot_f32(pick, source, TN) + place_ref[...]
    cls = column_sum(jnp.where(place == 0, e_ref[0, KEEP:].astype(jnp.float32), 0.0))
    y_ref[0, PATCHES:] = tail_rows(cls)
    scaled, _ = norm_rows(y_ref[0])
    normed = low(scaled * gain + shift)
    q_ref[0] = low(dot_f32(normed[: q_ref.shape[1]], q_w[...], NN) + bq)
    k_ref[0] = low(dot_f32(normed, k_w[...], NN))
    v_ref[0] = low(dot_f32(normed, v_w[...], NN) + bv)


def dec_entry(shrunk, ranks, placed, dec_full, vectors, own):
    images = shrunk.shape[0]
    kinds = [(D_ROWS, jnp.float32), (own, jnp.bfloat16), (D_ROWS, jnp.bfloat16)]
    kinds.append(kinds[2])
    return pl.pallas_call(
        dec_entry_kernel,
        grid=(images,),
        in_specs=[
            per_image(E_ROWS, D_D),
            per_image(1, PATCHES),
            whole((PATCHES, D_D)),
            columns(D_D, D_D, 0),
            columns(D_D, D_D, 1),
            columns(D_D, D_D, 2),
            whole((8, D_D)),
        ],
        out_specs=[per_image(rows, D_D) for rows, _ in kinds],
        out_shape=[jax.ShapeDtypeStruct((images, rows, D_D), kind) for rows, kind in kinds],
        compiler_params=pltpu.CompilerParams(vmem_limit_bytes=VMEM_LIMIT),
        cost_estimate=pl.CostEstimate(
            flops=4 * images * D_ROWS * D_D * D_D * 2,
            bytes_accessed=20 * 1024 * 1024,
            transcendentals=0,
        ),
    )(shrunk, ranks, placed, dec_full, dec_full, dec_full, vectors)


def dec_entry_back_kernel(
    y_ref,
    dq_ref,
    dk_ref,
    dv_ref,
    dmid_ref,
    rank_ref,
    q_w,
    k_w,
    v_w,
    vec_ref,
    de_ref,
    grad_ref,
    vec_grad,
    cls_ref,
):
    image = pl.program_id(0)
    clear_first((grad_ref, vec_grad, cls_ref))
    gain, shift = vec_ref[0:1, :], vec_ref[1:2, :]
    scaled, inverse = norm_rows(y_ref[0])
    normed = low(scaled * gain + shift)
    dq, dk, dv = dq_ref[0], dk_ref[0], dv_ref[0]
    own = dq.shape[0]
    grad_ref[:, :D_D] += dot_f32(normed[:own], dq, TN)
    grad_ref[:, D_D : 2 * D_D] += dot_f32(normed, dk, TN)
    grad_ref[:, 2 * D_D :] += dot_f32(normed, dv, TN)
    up = dot_f32(dk, k_w[...], NT) + dot_f32(dv, v_w[...], NT)
    up = jnp.concatenate([up[:own] + dot_f32(dq, q_w[...], NT), up[own:]], axis=0)
    back, g_gain, g_shift = norm_rows_back(up, scaled, inverse, gain)
    back = jnp.concatenate([back[:own] + dmid_ref[0], back[own:]], axis=0)
    patches = back[:PATCHES]
    high = low(patches)
    rest = low(patches - high.astype(jnp.float32))
    ranks = rank_ref[0]
    at = lax.broadcasted_iota(jnp.int32, (KEEP, PATCHES), 0)
    pick = low(jnp.where(at == ranks, 1.0, 0.0))
    hidden = low(jnp.where(jnp.broadcast_to(ranks, (16, PATCHES)) >= KEEP, 1.0, 0.0))
    de_ref[pl.ds(pl.multiple_of(image * KEEP, KEEP), KEEP)] = low(dot_f32(pick, high, NN))
    g_mask = dot_f32(hidden, high, NN) + dot_f32(hidden, rest, NN)
    cls_ref[pl.ds(image, 1), :] = back[PATCHES : PATCHES + 1]
    sums = (
        g_mask[0:1],
        g_shift,
        column_sum(dq.astype(jnp.float32)),
        column_sum(dv.astype(jnp.float32)),
        g_gain,
    )
    for at, part in enumerate(sums):
        vec_grad[at : at + 1, :D_D] += part

    @pl.when(image == pl.num_programs(0) - 1)
    def _():
        de_ref[de_ref.shape[0] - TAIL :] = low(cls_ref[...])


def dec_entry_back(y0, dq, dk, dv, dmid, ranks, dec_full, vectors):
    images, rows, _ = y0.shape
    own = dq.shape[1]
    f32 = jnp.float32
    return pl.pallas_call(
        dec_entry_back_kernel,
        grid=(images,),
        in_specs=[
            per_image(rows, D_D),
            per_image(own, D_D),
            per_image(rows, D_D),
            per_image(rows, D_D),
            per_image(own, D_D),
            per_image(1, PATCHES),
            columns(D_D, D_D, 0),
            columns(D_D, D_D, 1),
            columns(D_D, D_D, 2),
            whole((8, D_D)),
        ],
        out_specs=[whole((images * KEEP + TAIL, D_D)), whole((D_D, 3 * D_D)), whole((8, D_E))],
        out_shape=[
            jax.ShapeDtypeStruct((images * KEEP + TAIL, D_D), jnp.bfloat16),
            jax.ShapeDtypeStruct((D_D, 3 * D_D), f32),
            jax.ShapeDtypeStruct((8, D_E), f32),
        ],
        scratch_shapes=[pltpu.VMEM((TAIL, D_D), f32)],
        compiler_params=pltpu.CompilerParams(vmem_limit_bytes=VMEM_LIMIT),
        cost_estimate=pl.CostEstimate(
            flops=12 * images * rows * D_D * D_D * 2,
            bytes_accessed=24 * 1024 * 1024,
            transcendentals=0,
        ),
    )(y0, dq, dk, dv, dmid, ranks, dec_full, dec_full, dec_full, vectors)


E_HEADS = 128 * H_E // D_E
E_DIM = D_E // H_E
E_OUT = 4 * D_E
E_UP = 5 * D_E
E_DOWN = E_UP + FF_E
E_EMBED = E_DOWN + FF_E
SIZE = 768


def tail_rows(first):
    at = lax.broadcasted_iota(jnp.int32, (TAIL, first.shape[1]), 0)
    return jnp.where(at == 0, first, 0.0)


def encoder_kernel(
    kept_ref,
    place_ref,
    w_ref,
    vec_ref,
    bu_ref,
    be_ref,
    x_ref,
    mid_ref,
    enc_ref,
    qkv_ref,
    lse_ref,
    o_ref,
    slope_ref,
    act_ref,
    e_ref,
):
    (gain1, gain2, gain3, cls, shift1, bq, bv, bo, shift2, bd, shift3) = (
        vec_ref[i : i + 1, :] for i in range(11)
    )
    rows = dot_f32(kept_ref[0], w_ref[:, :D_E], NN) + place_ref[0]
    x_ref[0] = jnp.concatenate([rows, tail_rows(cls)], axis=0)
    scaled, _ = norm_rows(x_ref[0])
    normed = low(scaled * gain1 + shift1)
    for at, bias in enumerate((bq, None, bv)):
        value = dot_f32(normed, w_ref[:, (at + 1) * D_E : (at + 2) * D_E], NN)
        qkv_ref[0, :, at * D_E : (at + 1) * D_E] = low(value if bias is None else value + bias)
    for group in range(D_E // 128):
        parts = [
            qkv_ref[0, :, at * D_E + group * 128 : at * D_E + (group + 1) * 128] for at in range(3)
        ]
        out, sums = attend_forward_group(E_HEADS, E_DIM, *parts)
        o_ref[0, :, group * 128 : (group + 1) * 128] = out
        for head in range(E_HEADS):
            at = group * E_HEADS + head
            lse_ref[0, at : at + 1, :] = sums[head]
    middle = x_ref[0] + dot_f32(o_ref[0], w_ref[:, E_OUT:E_UP], NN) + bo
    mid_ref[0] = middle
    scaled, _ = norm_rows(middle)
    second = low(scaled * gain2 + shift2)
    encoded = middle + bd
    for at in range(0, FF_E, SIZE):
        span = slice(at, at + SIZE)
        hidden = dot_f32(second, w_ref[:, E_UP + at : E_UP + at + SIZE], NN) + bu_ref[:, span]
        value, slope = gelu_parts(hidden)
        slope_ref[0, :, span] = slope
        act_ref[0, :, span] = low(value)
        encoded = encoded + dot_f32(
            act_ref[0, :, span], w_ref[:, E_DOWN + at : E_DOWN + at + SIZE], NT
        )
    enc_ref[0] = encoded
    scaled, _ = norm_rows(encoded)
    third = low(scaled * gain3 + shift3)
    e_ref[0] = low(dot_f32(third, w_ref[:, E_EMBED:], NN) + be_ref[...])


def encoder(kept, placed, enc_full, vectors, bu, be):
    images = kept.shape[0]
    f32, low_type = jnp.float32, jnp.bfloat16
    shapes = [
        ((E_ROWS, D_E), f32),
        ((E_ROWS, D_E), f32),
        ((E_ROWS, D_E), f32),
        ((E_ROWS, 3 * D_E), low_type),
        ((H_E, E_ROWS), f32),
        ((E_ROWS, D_E), low_type),
        ((E_ROWS, FF_E), f32),
        ((E_ROWS, FF_E), low_type),
        ((E_ROWS, D_D), low_type),
    ]
    return pl.pallas_call(
        encoder_kernel,
        grid=(images,),
        in_specs=[
            per_image(KEEP, D_E),
            per_image(KEEP, D_E),
            whole(enc_full.shape),
            whole((16, D_E)),
            whole((1, FF_E)),
            whole((1, D_D)),
        ],
        out_specs=[per_image(*shape) for shape, _ in shapes],
        out_shape=[jax.ShapeDtypeStruct((images,) + shape, kind) for shape, kind in shapes],
        compiler_params=pltpu.CompilerParams(vmem_limit_bytes=VMEM_LIMIT),
        cost_estimate=pl.CostEstimate(
            flops=2 * images * E_ROWS * enc_full.size,
            bytes_accessed=40 * 1024 * 1024,
            transcendentals=2 * images * E_ROWS * FF_E,
        ),
    )(kept, placed, enc_full, vectors, bu, be)


def turn_quarter(value, place):
    width = value.shape[1]
    quarter = width // 4
    turned = pltpu.roll(value, lax.rem(width - quarter * place, width), axis=1)
    return low(turned[:, :quarter])


def encoder_back_kernel(
    hosted,
    de_ref,
    cls_ref,
    mid_ref,
    enc_ref,
    o_ref,
    slope_ref,
    act_ref,
    w_ref,
    vec_ref,
    *refs,
):
    if hosted:
        dec_ref, do_ref, dmid_ref, grad_ref, vec_grad, dec_out, de_all, hidden_all, *refs = refs
        plane = PlaneSum(dec_ref, *refs[:5])
        line = LineSum(*refs[5:])
    else:
        do_ref, dmid_ref, grad_ref, vec_grad, de_all, hidden_all = refs
    image = pl.program_id(0)
    last = pl.num_programs(0) - 1
    place = lax.axis_index("seq")
    clear_first((grad_ref, vec_grad))
    if hosted:

        @pl.when(image == 0)
        def _():
            greet_all()
            plane.start()

    gain2, gain3, shift2, shift3 = (vec_ref[i : i + 1, :] for i in range(4))
    at = lax.broadcasted_iota(jnp.int32, (TAIL, D_D), 0)
    cls = column_sum(jnp.where(at == image, cls_ref[...].astype(jnp.float32), 0.0))
    de_all[:KEEP] = de_ref[...]
    de_all[KEEP:] = low(tail_rows(cls))
    de = de_all[...]
    vec_grad[6:7, :D_D] += column_sum(de.astype(jnp.float32))
    scaled3, inverse3 = norm_rows(enc_ref[0])
    third = low(scaled3 * gain3 + shift3)
    quarter = FF_E // 4
    first = D_E // 4
    small = D_D // 4
    grad_ref[:, first + 2 * quarter :] += dot_f32(
        third, de_all[:, pl.ds(pl.multiple_of(place * small, small), small)], TN
    )
    up3, g_gain3, g_shift3 = norm_rows_back(
        dot_f32(de, w_ref[:, E_EMBED:], NT), scaled3, inverse3, gain3
    )
    up3_low = low(up3)
    scaled2, inverse2 = norm_rows(mid_ref[0])
    second = low(scaled2 * gain2 + shift2)
    own_hidden = pl.ds(pl.multiple_of(place * quarter, quarter), quarter)
    back = jnp.zeros_like(up3)
    for at in range(0, FF_E, SIZE):
        span = slice(at, at + SIZE)
        hidden = dot_f32(up3_low, w_ref[:, E_DOWN + at : E_DOWN + at + SIZE], NN)
        hidden = low(hidden * slope_ref[0, :, span])
        hidden_all[:, span] = hidden
        row = 8 + at // SIZE
        vec_grad[row : row + 1, :] += column_sum(hidden.astype(jnp.float32))
        back = back + dot_f32(hidden, w_ref[:, E_UP + at : E_UP + at + SIZE], NT)
    grad_ref[:, first : first + quarter] += dot_f32(second, hidden_all[:, own_hidden], TN)
    grad_ref[:, first + quarter : first + 2 * quarter] += dot_f32(
        up3_low, act_ref[0, :, own_hidden], TN
    )
    through, g_gain2, g_shift2 = norm_rows_back(back, scaled2, inverse2, gain2)
    middle_grad = up3 + through
    dmid_ref[0] = middle_grad
    grad_ref[:, :first] += dot_f32(o_ref[0], turn_quarter(middle_grad, place), TN)
    do_ref[0] = low(dot_f32(low(middle_grad), w_ref[:, E_OUT:E_UP], NT))
    sums = (column_sum(middle_grad), g_shift2, column_sum(up3), g_shift3, g_gain2, g_gain3)
    for at, part in enumerate(sums):
        vec_grad[at : at + 1, :] += part
    if hosted:
        pl.when(image == 0)(plane.pass_on)
        pl.when(image == 1)(lambda: line.start(plane.total()))

        @pl.when(image == last)
        def _():
            line.spread()
            line.finish()
            plane.finish()
            dec_out[...] = line.result[...]


def encoder_back(de_sum, saved, enc_full, vectors, dec, collective_id):
    mid, enc, o, slope, act = saved
    images = mid.shape[0]
    f32 = jnp.float32
    width = D_E // 4 + FF_E // 2 + D_D // 4
    dec_rows, dec_cols = dec.shape[0] // lax.axis_size("fsdp"), dec.shape[1]
    hosted = plane_fits(dec.shape[0]) and images >= 3
    results = pl.pallas_call(
        partial(encoder_back_kernel, hosted),
        grid=(images,),
        in_specs=[
            pl.BlockSpec((KEEP, D_D), lambda i: (i, 0)),
            pl.BlockSpec((TAIL, D_D), lambda i: (images * KEEP // TAIL, 0)),
            per_image(E_ROWS, D_E),
            per_image(E_ROWS, D_E),
            per_image(E_ROWS, D_E),
            pl.BlockSpec((1, E_ROWS, FF_E), lambda i: (i, 0, 0), pipeline_mode=pl.Buffered(1)),
            per_image(E_ROWS, FF_E),
            whole(enc_full.shape),
            whole((8, D_E)),
        ]
        + [whole(dec.shape)] * hosted,
        out_specs=[
            per_image(E_ROWS, D_E),
            per_image(E_ROWS, D_E),
            whole((D_E, width)),
            whole((16, D_E)),
        ]
        + [whole((dec_rows, dec_cols))] * hosted,
        out_shape=[
            jax.ShapeDtypeStruct((images, E_ROWS, D_E), jnp.bfloat16),
            jax.ShapeDtypeStruct((images, E_ROWS, D_E), f32),
            jax.ShapeDtypeStruct((D_E, width), f32),
            jax.ShapeDtypeStruct((16, D_E), f32),
        ]
        + [jax.ShapeDtypeStruct((dec_rows, dec_cols), f32)] * hosted,
        scratch_shapes=[
            pltpu.VMEM((E_ROWS, D_D), jnp.bfloat16),
            pltpu.VMEM((E_ROWS, FF_E), jnp.bfloat16),
        ]
        + (
            PlaneSum.scratch(dec_rows, dec_cols, f32)
            + LineSum.scratch(dec_rows, dec_cols, lax.axis_size("seq"))
            if hosted
            else []
        ),
        compiler_params=pltpu.CompilerParams(
            vmem_limit_bytes=VMEM_LIMIT,
            **(dict(collective_id=collective_id, has_side_effects=True) if hosted else {}),
        ),
        cost_estimate=pl.CostEstimate(
            flops=3 * images * E_ROWS * enc_full.size,
            bytes_accessed=50 * 1024 * 1024,
            transcendentals=0,
        ),
    )(de_sum, de_sum, mid, enc, o, slope, act, enc_full, vectors, *([dec] * hosted))
    if hosted:
        return results
    dec_sum = lax.psum(lax.psum_scatter(dec, "fsdp", scatter_dimension=0, tiled=True), "seq")
    return *results, dec_sum


def encoder_entry_back_kernel(
    hosted,
    extra,
    kept_ref,
    x_ref,
    qkv_ref,
    lse_ref,
    o_ref,
    do_ref,
    dmid_ref,
    w_ref,
    vec_ref,
    *refs,
):
    if hosted:
        early_ref, grad_ref, vec_grad, early_out, dqkv_ref, *refs = refs
        plane = PlaneSum(early_ref, *refs[:5])
        line = LineGather(*refs[5:])
    else:
        grad_ref, vec_grad, dqkv_ref = refs
    place = lax.axis_index("seq")
    image = pl.program_id(0)
    last = pl.num_programs(0) - 1
    clear_first((grad_ref, vec_grad))
    if hosted:

        @pl.when(image == 0)
        def _():
            greet_all()
            plane.start()

    gain1, shift1 = (vec_ref[i : i + 1, :] for i in range(2))
    for group in range(D_E // 128):
        span = slice(group * 128, (group + 1) * 128)
        parts = [
            qkv_ref[0, :, at * D_E + group * 128 : at * D_E + (group + 1) * 128] for at in range(3)
        ]
        sums = [
            lse_ref[0, group * E_HEADS + head : group * E_HEADS + head + 1, :]
            for head in range(E_HEADS)
        ]
        dq, dk, dv = attend_backward_group(
            E_HEADS, E_DIM, *parts, sums, do_ref[0, :, span], o_ref[0, :, span]
        )
        dqkv_ref[:, group * 128 : (group + 1) * 128] = dq
        for at, pair in ((1, dk), (2, dv)):
            lanes = slice(at * D_E + group * 128, at * D_E + (group + 1) * 128)
            dqkv_ref[:KEEP, lanes], dqkv_ref[KEEP:, lanes] = pair
    scaled, inverse = norm_rows(x_ref[0])
    normed = low(scaled * gain1 + shift1)
    quarter = D_E // 4
    sums = []
    for at in range(3):
        part = dqkv_ref[:, at * D_E : (at + 1) * D_E].astype(jnp.float32)
        if at != 1:
            sums.append(column_sum(part))
        grad_ref[:, (at + 1) * quarter : (at + 2) * quarter] += dot_f32(
            normed, turn_quarter(part, place), TN
        )
    through, g_gain1, g_shift1 = norm_rows_back(
        dot_f32(dqkv_ref[...], w_ref[:, D_E : 4 * D_E], NT), scaled, inverse, gain1
    )
    back = dmid_ref[0] + through
    patches = back[:KEEP]
    grad_ref[:, :quarter] += dot_f32(kept_ref[0], turn_quarter(patches, place), TN)
    sums = [column_sum(patches), back[KEEP : KEEP + 1], g_shift1] + sums + [g_gain1]
    for at, part in enumerate(sums):
        vec_grad[at : at + 1, :] += part
    if hosted:
        pl.when(image == 0)(plane.pass_on)
        pl.when(image == 1)(lambda: line.start(with_rests(plane.total(), extra)))

        @pl.when(image == last)
        def _():
            line.wait_recv()
            line.finish()
            plane.finish()
            early_out[...] = line.slots[...]


def with_rests(total, extra):
    rounded = low(total)
    rest = total[:, -extra:] - rounded[:, -extra:].astype(jnp.float32)
    return jnp.concatenate([rounded, low(rest)], axis=1)


def encoder_entry_back(kept, saved, do, dmid, enc_full, vectors, early, extra, collective_id):
    x0, qkv, lse, o = saved
    images = kept.shape[0]
    f32 = jnp.float32
    line = lax.axis_size("seq")
    rows, width = early.shape[0] // lax.axis_size("fsdp"), early.shape[1]
    gathered = (line, rows, width + extra)
    hosted = plane_fits(early.shape[0]) and images >= 3
    results = pl.pallas_call(
        partial(encoder_entry_back_kernel, hosted, extra),
        grid=(images,),
        in_specs=[
            per_image(KEEP, D_E),
            per_image(E_ROWS, D_E),
            per_image(E_ROWS, 3 * D_E),
            per_image(H_E, E_ROWS),
            per_image(E_ROWS, D_E),
            per_image(E_ROWS, D_E),
            per_image(E_ROWS, D_E),
            columns(D_E, 5 * D_E, 0),
            whole((8, D_E)),
        ]
        + [whole(early.shape)] * hosted,
        out_specs=[whole((D_E, D_E)), whole((8, D_E))] + [whole(gathered)] * hosted,
        out_shape=[
            jax.ShapeDtypeStruct((D_E, D_E), f32),
            jax.ShapeDtypeStruct((8, D_E), f32),
        ]
        + [jax.ShapeDtypeStruct(gathered, jnp.bfloat16)] * hosted,
        scratch_shapes=[pltpu.VMEM((E_ROWS, 3 * D_E), jnp.bfloat16)]
        + (
            PlaneSum.scratch(rows, width, jnp.bfloat16)
            + [pltpu.VMEM(gathered, jnp.bfloat16), pltpu.SemaphoreType.DMA((2, line - 1))]
            if hosted
            else []
        ),
        compiler_params=pltpu.CompilerParams(
            vmem_limit_bytes=VMEM_LIMIT,
            **(dict(collective_id=collective_id, has_side_effects=True) if hosted else {}),
        ),
        cost_estimate=pl.CostEstimate(
            flops=8 * images * E_ROWS * D_E * 4 * D_E,
            bytes_accessed=20 * 1024 * 1024,
            transcendentals=images * H_E * E_ROWS * E_ROWS,
        ),
    )(kept, x0, qkv, lse, o, do, dmid, enc_full, vectors, *([early] * hosted))
    if hosted:
        return results
    own = lax.psum_scatter(early, "fsdp", scatter_dimension=0, tiled=True)
    return *results, lax.all_gather(with_rests(own, extra), "seq", axis=0, tiled=False)


def stack_rows(parts, count=8):
    rows = jnp.stack(parts)
    return jnp.pad(rows, ((0, count - len(parts)), (0, 0)))


def adamw(weight, moment_one, moment_two, gradient, step_rate, decay_rate):
    moment_one = BETA_ONE * moment_one + (1 - BETA_ONE) * gradient
    moment_two = BETA_TWO * moment_two + (1 - BETA_TWO) * gradient * gradient
    fixed_one = moment_one / (1 - BETA_ONE**STEP)
    fixed_two = moment_two / (1 - BETA_TWO**STEP)
    weight = weight - step_rate * (
        fixed_one / (jnp.sqrt(fixed_two) + ADAM_EPS) + decay_rate * weight
    )
    return (moment_one, moment_two, weight)


def enc_update_kernel(w_ref, m_ref, v_ref, early_ref, late_ref, m_out, v_out, w_out):
    lines = early_ref.shape[0]
    quarter_e, quarter_f, quarter_d = D_E // lines, FF_E // lines, D_D // lines
    pieces = [(late_ref, at * quarter_e, quarter_e) for at in range(4)]
    pieces += [
        (early_ref, 0, quarter_e),
        (early_ref, quarter_e, quarter_f),
        (early_ref, quarter_e + quarter_f, quarter_f),
        (early_ref, quarter_e + 2 * quarter_f, quarter_d),
    ]
    start = 0
    for number, (ref, offset, size) in enumerate(pieces):
        parts = [ref[at, :, offset : offset + size].astype(jnp.float32) for at in range(lines)]
        if number == len(pieces) - 1:
            rests = [ref[at, :, offset + size : offset + 2 * size] for at in range(lines)]
            parts = [a + b.astype(jnp.float32) for a, b in zip(parts, rests)]
        span = slice(start, start + lines * size)
        start += lines * size
        m_out[:, span], v_out[:, span], w_out[:, span] = adamw(
            w_ref[:, span],
            m_ref[:, span],
            v_ref[:, span],
            jnp.concatenate(parts, axis=1),
            MATRIX_RATE,
            MATRIX_DECAY,
        )


def enc_update(weight, moment_one, moment_two, early, late):
    rows, cols = weight.shape
    lines = early.shape[0]
    step = 16 if rows % 16 == 0 else rows
    plain = pl.BlockSpec((step, cols), lambda i: (i, 0))
    return pl.pallas_call(
        enc_update_kernel,
        grid=(rows // step,),
        in_specs=[plain] * 3
        + [
            pl.BlockSpec((lines, step, part.shape[2]), lambda i: (0, i, 0))
            for part in (early, late)
        ],
        out_specs=[plain] * 3,
        out_shape=[jax.ShapeDtypeStruct(weight.shape, jnp.float32)] * 3,
        compiler_params=pltpu.CompilerParams(vmem_limit_bytes=VMEM_LIMIT),
        cost_estimate=pl.CostEstimate(
            flops=20 * weight.size, bytes_accessed=26 * weight.size, transcendentals=0
        ),
    )(weight, moment_one, moment_two, early, late)


ENC_BACK, ENC_ENTRY, DEC_MIDDLE, DEC_ENTRY, SMALL_ROWS = 0, 16, 24, 40, 64
LOSS_ROW = DEC_MIDDLE + 7
GAIN_ROWS = (ENC_ENTRY + 5, ENC_BACK + 4, ENC_BACK + 5, DEC_ENTRY + 4, DEC_MIDDLE + 1, DEC_MIDDLE + 4)
BIAS_ROWS = (
    (ENC_ENTRY, ENC_ENTRY + 1, ENC_ENTRY + 2, ENC_ENTRY + 3, ENC_ENTRY + 4, ENC_BACK, ENC_BACK + 1)
    + (ENC_BACK + 8, ENC_BACK + 2, ENC_BACK + 3, ENC_BACK + 6)
    + (DEC_ENTRY, DEC_ENTRY + 1, DEC_ENTRY + 2, DEC_ENTRY + 3, DEC_MIDDLE, DEC_MIDDLE + 2)
    + (DEC_MIDDLE + 8, DEC_MIDDLE + 3, DEC_MIDDLE + 5, DEC_MIDDLE + 6)
)


def small_update_kernel(sums_ref, *refs):
    gains, biases, gain_out, bias_out = refs[:3], refs[3:6], refs[6:9], refs[9:12]
    gain_spans = list(zip(GAIN_ROWS, [D_E] * 3 + [D_D] * 3))
    bias_spans = []
    for row, width in zip(BIAS_ROWS, bias_widths()):
        pieces = 4 if width > D_E else 1
        bias_spans += [(row + at, width // pieces) for at in range(pieces)]
    for spans, ins, outs in ((gain_spans, gains, gain_out), (bias_spans, biases, bias_out)):
        start = 0
        for row, width in spans:
            span = slice(start, start + width)
            start += width
            weight, moment_one, moment_two = (ref[:, span] for ref in ins)
            news = adamw(
                weight, moment_one, moment_two, sums_ref[row : row + 1, :width], SMALL_RATE, 0.0
            )
            for out, new in zip(outs, news):
                out[:, span] = new


def small_update(sums, *vectors):
    rows = [vector[None] for vector in vectors]
    vmem = pl.BlockSpec(memory_space=pltpu.VMEM)
    news = pl.pallas_call(
        small_update_kernel,
        in_specs=[vmem] * 7,
        out_specs=[vmem] * 6,
        out_shape=[jax.ShapeDtypeStruct(row.shape, jnp.float32) for row in rows],
        compiler_params=pltpu.CompilerParams(vmem_limit_bytes=COPY_LIMIT),
    )(sums, *rows)
    return tuple(new[0] for new in news)


def shards(
    pixels,
    restore,
    enc_w,
    enc_m,
    enc_v,
    dec_w,
    dec_m,
    dec_v,
    head_w,
    head_m,
    head_v,
    gain_w,
    gain_m,
    gain_v,
    bias_w,
    bias_m,
    bias_v,
):
    seq_count = lax.axis_size("seq")
    place = lax.axis_index("seq")
    images, own_count, _ = pixels.shape
    masked_total = images * lax.axis_size("fsdp") * (PATCHES - KEEP)

    head_low = low(head_w)

    pieces = split_vector(bias_w, bias_widths())
    gains = split_vector(gain_w, [D_E, D_E, D_E, D_D, D_D, D_D])
    (b_patch, cls_token, e_shift1, e_bq, e_bv, e_bo, e_shift2, e_bu, e_bd, e_shift3) = pieces[:10]
    (b_embed, mask_token, d_shift1, d_bq, d_bv, d_bo, d_shift2, d_bu, d_bd, d_shift3) = pieces[
        10:20
    ]
    b_head = pieces[20]

    ranks = jnp.arange(KEEP, dtype=jnp.int32)
    turned = lax.dynamic_slice_in_dim(
        jnp.concatenate([restore, restore], axis=1), place * own_count, PATCHES, axis=1
    )
    own_restore = turned[:, :own_count]
    own_pick = low(own_restore[:, None, :] == ranks[None, :, None])
    own_kept = jnp.einsum("irp,ipd->ird", own_pick, pixels, preferred_element_type=jnp.float32)
    patch_ids = jnp.arange(PATCHES, dtype=jnp.int32)
    keep_ids = jnp.sum(
        jnp.where(restore[:, None, :] == ranks[None, :, None], patch_ids, 0), axis=2
    )
    enc_full, kept, kept_places, patch_places = start_gather(
        low(enc_w),
        low(own_kept).reshape(images * KEEP, PIX),
        keep_ids.reshape(-1),
        lax.rem(patch_ids + place * own_count, PATCHES),
        b_patch,
        0,
    )
    kept, dec_low = lax.optimization_barrier((kept, low(dec_w)))
    dec_full = lax.all_gather(dec_low, "fsdp", axis=0, tiled=True)
    kept = kept.reshape(images, KEEP, PIX)

    x0, e_mid, encoded, e_mixed, e_lse, e_o, e_slope, e_act, shrunk = encoder(
        kept,
        kept_places.reshape(images, KEEP, D_E),
        enc_full,
        stack_rows(
            gains[:3] + [cls_token, e_shift1, e_bq, e_bv, e_bo, e_shift2, e_bd, e_shift3], 16
        ),
        e_bu[None],
        b_embed[None],
    )

    ranks_row = turned[:, None, :]
    y0, d_q, d_k, d_v = dec_entry(
        shrunk,
        ranks_row,
        patch_places,
        dec_full,
        stack_rows([mask_token, gains[3], d_shift1, d_bq, d_bv]),
        own_count,
    )
    y0_own = y0[:, :own_count]
    d_o, d_lse = attend_forward(d_q, d_k, d_v, H_D)
    own_masked = (own_restore >= KEEP).astype(jnp.float32)
    own_masked = jnp.broadcast_to(own_masked[..., None], own_masked.shape + (128,))
    d_do, d_dmid, late_grads, middle_sums = dec_middle(
        d_o,
        y0_own,
        pixels,
        own_masked,
        dec_full,
        head_low,
        stack_rows([d_bo, gains[4], d_shift2, d_bd, gains[5], d_shift3]),
        d_bu[None],
        b_head[None],
        2.0 / (PIX * masked_total),
    )
    dec_late = lax.psum_scatter(late_grads, "fsdp", scatter_dimension=0, tiled=True)
    d_dq, d_dk, d_dv = attend_backward(d_q, d_k, d_v, d_lse, d_do, d_o, H_D)
    de_part, g_d_qkv, dec_entry_sums = dec_entry_back(
        y0, d_dq, d_dk, d_dv, d_dmid, ranks_row, dec_full, stack_rows([gains[3], d_shift1])
    )
    de_sum = line_sum(de_part, 7, 1)
    dec_late, de_sum = lax.optimization_barrier((dec_late, de_sum))
    dec_late = lax.psum(dec_late, "seq")

    embed_cols = D_D // seq_count
    e_do, e_dmid, early_grads, enc_back_sums, dec_early = encoder_back(
        de_sum,
        (e_mid, encoded, e_o, e_slope, e_act),
        enc_full,
        stack_rows([gains[1], gains[2], e_shift2, e_shift3]),
        g_d_qkv,
        2,
    )
    late_grads, enc_entry_sums, early_all = encoder_entry_back(
        kept,
        (x0, e_mixed, e_lse, e_o),
        e_do,
        e_dmid,
        enc_full,
        stack_rows([gains[0], e_shift1]),
        early_grads,
        embed_cols,
        3,
    )

    once = jnp.where(place == 0, 1.0, 0.0)
    small = jnp.concatenate(
        [
            enc_back_sums * once,
            enc_entry_sums * once,
            middle_sums,
            dec_entry_sums,
            jnp.zeros((SMALL_ROWS - DEC_ENTRY - 8, D_E), jnp.float32),
        ],
        axis=0,
    )
    dec_late, late_grads = lax.optimization_barrier((dec_late, late_grads))
    late_all, small, head_grad = exchange(
        late_grads, small, dec_late[:, D_D + 2 * FF_D :], seq_count, 4
    )
    loss_total = jnp.sum(small[LOSS_ROW]) / (PIX * masked_total)
    dec_grad = jnp.concatenate([dec_early, dec_late[:, : D_D + 2 * FF_D]], axis=1)
    small_new = small_update(small, gain_w, gain_m, gain_v, bias_w, bias_m, bias_v)
    enc_new = tuple(enc_update(enc_w, enc_m, enc_v, early_all, late_all))
    dec_new = adamw(dec_w, dec_m, dec_v, dec_grad, MATRIX_RATE, MATRIX_DECAY)
    head_new = adamw(head_w, head_m, head_v, head_grad, MATRIX_RATE, MATRIX_DECAY)
    return (loss_total,) + enc_new + dec_new + head_new + tuple(small_new)


def solution(mesh):
    rows = P("fsdp", None)
    in_specs = (P("fsdp", "seq", None), rows) + (rows,) * 6 + (P(),) * 9
    out_specs = (P(),) + (rows,) * 6 + (P(),) * 9
    return jax.shard_map(shards, mesh=mesh, in_specs=in_specs, out_specs=out_specs, check_vma=False)
```
